128 devices in a mesh: seq: 32 (over x, z, core), head: 4 (over y).
Axes of the slice: x: 4, y: 4, z: 4, core: 2. Of those that a mesh axis runs over, the one named last changes fastest.
Arguments:
- queries: bfloat16 [131072, 2048], P('seq', 'head'), may hold values from -100 to 100
- keys: bfloat16 [131072, 2048], P('seq', 'head'), may hold values from -5 to 5
- values: bfloat16 [131072, 2048], P('seq', 'head'), may hold values from -6 to 6
- key_count: int32 [256], replicated, may hold values from 64 to 512
- selected: int32 [256, 2], replicated, may hold values from 0 to 255, as said below
- w_out: bfloat16 [2048, 2048], replicated, may hold values from -0.125 to 0.125
Outputs:
- mixed: bfloat16 [131072, 2048], P(('seq', 'head'))
The draws below stay inside these ranges and needn't reach their ends.
Inputs may be any that keep to these rules, and one draw needn't show every extreme that they name: Each query block's two selected blocks differ from each other and from the block itself. Of the 16 selections of the query blocks on one index of seq, at most 1 name blocks held by any one index of seq (blocks j with j // 8 equal), and exactly 1 for some.
All inputs are finite; a program needn't handle non-finite values.
Results may differ from the reference program's by a relative error of at most 0.0061.
Values may be sent and summed in bfloat16 or wider, within the bound.
No kernel may reach another device: no remote copies, remote signals or barrier semaphores. Data moves between devices by JAX's collectives and lax.ppermute only.
A program may use at most 256 MiB of HBM per device.

```python
import math
import jax
import jax.numpy as jnp
from jax import lax

D = 2048
HEADS = 16
HS = 128
BSZ = 512
BLK_DEV = 8
NBLK = 256
TOKENS = 131072
N_SEQ = 32


def shared_keys(key):
    return jnp.clip(jax.random.normal(key, (TOKENS, D), jnp.float32), -5.0, 5.0)


def draw_keys(key, part):
    return shared_keys(key).astype(jnp.bfloat16)


def draw_queries(key, part):
    key = jax.random.fold_in(key, 5)
    fresh = jnp.clip(jax.random.normal(key, (TOKENS, D), jnp.float32), -5.0, 5.0)
    return fresh.astype(jnp.bfloat16)


def draw_selected(key, part):
    key = jax.random.fold_in(key, 3)
    pairs = 2 * BLK_DEV
    source = jnp.arange(N_SEQ, dtype=jnp.int32)[:, None]
    number = jnp.arange(pairs, dtype=jnp.int32)[None, :]
    if BLK_DEV == 1:
        offsets = jax.vmap(lambda sub: jax.random.permutation(sub, N_SEQ - 1))(jax.random.split(jax.random.fold_in(key, 1), N_SEQ)).astype(jnp.int32) + 1
        target = (source + offsets[:, :pairs]) % N_SEQ
        return target.astype(jnp.int32).reshape(NBLK, 2)
    offsets = jax.vmap(lambda sub: jax.random.permutation(sub, N_SEQ))(jax.random.split(jax.random.fold_in(key, 1), N_SEQ))
    target = (source + jnp.take_along_axis(offsets.astype(jnp.int32), jnp.broadcast_to(number % N_SEQ, (N_SEQ, pairs)), axis=1)) % N_SEQ
    anywhere = jax.random.randint(jax.random.fold_in(key, 2), (N_SEQ, pairs), 0, BLK_DEV)
    shifted = jax.random.randint(jax.random.fold_in(key, 4), (N_SEQ, pairs), 0, BLK_DEV - 1)
    own_local = number // 2
    other_local = (own_local + 1 + shifted) % BLK_DEV
    local = jnp.where(target == source, other_local, anywhere)
    return (target * BLK_DEV + local).astype(jnp.int32).reshape(NBLK, 2)


def place_ends(entries, stream_key, least, top_value):
    index_at = [jax.random.randint(jax.random.fold_in(stream_key, axis), (), 0, length) for axis, length in enumerate(entries.shape)]
    main_axis = entries.shape.index(max(entries.shape))
    neighbour = index_at[:main_axis] + [(index_at[main_axis] + 1) % entries.shape[main_axis]] + index_at[main_axis + 1:]
    return entries.at[tuple(index_at)].set(least).at[tuple(neighbour)].set(top_value)


def level_of(key, dims, cuts, low, top_value):
    loudness = 1.0
    for position, shards_of in cuts:
        steps = jax.random.uniform(jax.random.fold_in(jax.random.fold_in(key, 6), position), (shards_of,), jnp.float32, low / len(cuts), top_value / len(cuts))
        loudness = loudness * jnp.repeat(jnp.exp(steps), dims[position] // shards_of).reshape((-1,) + (1,) * (len(dims) - 1 - position))
    return loudness


def normal_values(own_key, extent, spread, most, cuts=(), kind=jnp.bfloat16):
    loudness = level_of(own_key, extent, cuts, -0.22, 0.18) if cuts else 1.0
    values = jax.random.normal(own_key, extent, jnp.float32) * spread * loudness
    return jnp.minimum(jnp.maximum(values, -most), most).astype(kind)


def setup_inputs(seed: int = 0) -> dict:
    seeds = jax.random.split(jax.random.key(seed), 7)
    queries = draw_queries(jax.random.fold_in(seeds[6], 71), 0)
    keys = draw_keys(jax.random.fold_in(seeds[6], 71), 0)
    values = normal_values(seeds[2], (TOKENS, D), 1.0, 6.0, ((0, 32), (1, 4)))
    key_count = place_ends(jax.random.randint(seeds[3], (NBLK,), BSZ // 8, BSZ + 1), jax.random.fold_in(seeds[3], 1), BSZ // 8, BSZ).astype(jnp.int32)
    selected = draw_selected(jax.random.fold_in(seeds[6], 71), 0)
    w_out = normal_values(seeds[5], (D, D), D ** -0.5, 0.125)
    return dict(queries=queries, keys=keys, values=values, key_count=key_count, selected=selected, w_out=w_out)


def part_block(qb, kb, vb, count):
    q4 = qb.astype(jnp.float32).reshape(BSZ, HEADS, HS)
    k4 = kb.astype(jnp.float32).reshape(BSZ, HEADS, HS)
    v4 = vb.astype(jnp.float32).reshape(BSZ, HEADS, HS)
    scores = jnp.einsum('qhd,khd->hqk', q4, k4) * (1.0 / math.sqrt(HS))
    live = jnp.arange(BSZ, dtype=jnp.int32) < count
    scores = jnp.where(live[None, None, :], scores, -1e+30)
    top = lax.optimization_barrier(jnp.max(scores, axis=-1))
    weights = jnp.exp(scores - top[..., None])
    total = lax.optimization_barrier(jnp.sum(weights, axis=-1))
    rounded = lax.optimization_barrier(weights.astype(jnp.bfloat16)).astype(jnp.float32)
    part = jnp.einsum('hqk,khd->qhd', rounded, v4) / jnp.transpose(total)[..., None]
    return (part, top, total)

def reference(queries, keys, values, key_count, selected, w_out):
    q_blocks = queries.reshape(NBLK, BSZ, D)
    k_blocks = keys.reshape(NBLK, BSZ, D)
    v_blocks = values.reshape(NBLK, BSZ, D)

    def one_block(index):
        parts = []
        tops = []
        totals = []
        for slot in range(3):
            if slot == 0:
                other = index
            else:
                other = selected[index, slot - 1]
            part, top, total = part_block(q_blocks[index], k_blocks[other], v_blocks[other], key_count[other])
            if slot > 0:
                part = lax.optimization_barrier(part.astype(jnp.bfloat16)).astype(jnp.float32)
            parts.append(part)
            tops.append(top)
            totals.append(total)
        biggest = jnp.maximum(jnp.maximum(tops[0], tops[1]), tops[2])
        numer = jnp.zeros((BSZ, HEADS, HS), jnp.float32)
        denom = jnp.zeros((HEADS, BSZ), jnp.float32)
        for slot in range(3):
            factor = totals[slot] * jnp.exp(tops[slot] - biggest)
            numer = numer + jnp.transpose(factor)[..., None] * parts[slot]
            denom = denom + factor
        return (numer / jnp.transpose(denom)[..., None]).reshape(BSZ, D).astype(jnp.bfloat16)
    attn = lax.map(one_block, jnp.arange(NBLK, dtype=jnp.int32)).reshape(TOKENS, D)
    return jnp.dot(attn, w_out, preferred_element_type=jnp.float32).astype(jnp.bfloat16)
```

```python
import functools
import math

import jax
import jax.numpy as jnp
from jax import lax
from jax.experimental import pallas as pl
from jax.experimental.pallas import tpu as pltpu
from jax.sharding import PartitionSpec as P

HS = 128
BSZ = 512
R = 64
CH = BSZ // R
HALF = CH // 2
NB = 8
NSEQ = 32
LEVELS = (28, 30, 32, 35, 64)
ROW = 128
F32 = jnp.float32
I32 = jnp.int32
BF = jnp.bfloat16
ANY = pl.BlockSpec(memory_space=pl.ANY)
SMEM = pl.BlockSpec(memory_space=pltpu.SMEM)
VMEM = pl.BlockSpec(memory_space=pltpu.VMEM)


def mm(a, b):
    return jnp.dot(a.astype(BF), b.astype(BF), preferred_element_type=F32)


def uv_of(index, plane):
    x = lax.shift_right_logical(index, 3) & 3
    z = lax.shift_right_logical(index, 1) & 3
    return (z, x) if plane == 0 else (x, z)


def iota(shape, dim):
    return lax.broadcasted_iota(I32, shape, dim)


def plan_kernel(sel_ref, cnt_ref, table_ref, need_ref):
    s = iota((NSEQ, ROW), 0)
    d = iota((NSEQ, ROW), 1)
    loc = jnp.full((NSEQ, ROW), -1, I32)
    grp = jnp.zeros((NSEQ, ROW), I32)
    for n in range(2 * NB):
        row = sel_ref[n : n + 1, :]
        hit = lax.shift_right_arithmetic(row, 3) == s
        loc = jnp.where(hit, row & 7, loc)
        grp = jnp.where(hit, (n >> 1) & 1, grp)
    count = jnp.zeros((NSEQ, ROW), I32)
    for j in range(NB):
        count = jnp.where(loc == j, cnt_ref[:, j : j + 1], count)
    total = lax.shift_right_logical(count + (R - 1), R.bit_length() - 1)

    i32, j32 = iota((NSEQ, NSEQ), 0), iota((NSEQ, NSEQ), 1)
    i128, j128 = iota((ROW, ROW), 0), iota((ROW, ROW), 1)
    chip_l = ((i32 >> 1) == (j32 >> 1)).astype(F32)
    chip_r = ((i128 >> 1) == (j128 >> 1)).astype(F32)
    odd_l = jnp.logical_and(j32 == i32 - 1, (i32 & 1) == 1).astype(F32)
    odd_r = jnp.logical_and(i128 == j128 - 1, (j128 & 1) == 1).astype(F32)
    lower = (j32 < i32).astype(F32)
    worst = jnp.zeros((1, 1), I32)
    for plane in range(2):
        first = (plane - loc) & 1
        n_of = jnp.where(loc >= 0, lax.shift_right_logical(total - first + 1, 1), 0)
        n_f = n_of.astype(F32)
        u_i, v_i = uv_of(i128, plane)
        u_j, v_j = uv_of(j128, plane)
        m1 = jnp.logical_and(
            u_i == u_j, (v_i * 2 + (i128 & 1)) < (v_j * 2 + (j128 & 1))
        ).astype(F32)
        a_n = mm(chip_l, n_f)
        pos1 = mm(a_n, m1) + mm(odd_l, n_f)
        u_s, v_s = uv_of(i32, plane)
        u_t, v_t = uv_of(j32, plane)
        m2 = jnp.logical_and(
            v_s == v_t, (u_t * 2 + (j32 & 1)) < (u_s * 2 + (i32 & 1))
        ).astype(F32)
        n_a = mm(n_f, chip_r)
        pos2 = mm(m2, n_a) + mm(n_f, odd_r)
        pos3 = jnp.where(
            grp == 0,
            mm(lower, jnp.where(grp == 0, n_f, 0.0)),
            mm(lower, jnp.where(grp == 1, n_f, 0.0)),
        )
        entry = n_of | (jnp.maximum(loc, 0) << 3)
        for index, place in enumerate((pos1, pos2, pos3)):
            entry = entry | (place.astype(I32) << (6 + 6 * index))
        table_ref[plane * NSEQ : (plane + 1) * NSEQ, :] = entry

        u_a, v_a = uv_of(s, plane)
        u_b, v_b = uv_of(d, plane)
        g1, g2, g3 = [
            jnp.sum(jnp.where(((u_b - u_a) & 3) == r, a_n, 0.0), axis=1, keepdims=True).astype(I32)
            for r in (1, 2, 3)
        ]
        hp, hm = lax.shift_right_logical(g2 + 1, 1), lax.shift_right_logical(g2, 1)
        same = jnp.logical_and(v_s == v_t, (i32 & 1) == (j32 & 1))
        before = jnp.logical_and(same, u_t == ((u_s - 1) & 3)).astype(F32)
        after = jnp.logical_and(same, u_t == ((u_s + 1) & 3)).astype(F32)
        wide = lambda col: jnp.broadcast_to(col.astype(F32), (NSEQ, ROW))
        plus = wide(g1) + wide(hp) + mm(before, wide(hp))
        minus = wide(g3) + wide(hm) + mm(after, wide(hm))
        load = jnp.maximum(jnp.maximum(plus, minus), 2.0 * wide(hp))
        k1, k2, k3 = [
            jnp.sum(jnp.where(((v_b - v_a) & 3) == r, n_a, 0.0), axis=0, keepdims=True).astype(I32)
            for r in (1, 2, 3)
        ]
        kp, km = lax.shift_right_logical(k2 + 1, 1), lax.shift_right_logical(k2, 1)
        same_r = jnp.logical_and(u_i == u_j, (i128 & 1) == (j128 & 1))
        nxt = jnp.logical_and(same_r, v_i == ((v_j + 1) & 3)).astype(F32)
        prv = jnp.logical_and(same_r, v_i == ((v_j - 1) & 3)).astype(F32)
        tall = lambda line: jnp.broadcast_to(line.astype(F32), (NSEQ, ROW))
        plus = tall(k1) + tall(kp) + mm(tall(kp), nxt)
        minus = tall(k3) + tall(km) + mm(tall(km), prv)
        load2 = jnp.maximum(jnp.maximum(plus, minus), 2.0 * tall(kp))
        load2 = jnp.where(d < NSEQ, load2, 0.0)
        both = jnp.maximum(load, load2)
        worst = jnp.maximum(
            worst, jnp.max(jnp.max(both, axis=1, keepdims=True), axis=0, keepdims=True).astype(I32)
        )
    need_ref[...] = jnp.broadcast_to(lax.shift_right_logical(worst + 1, 1), (8, ROW))


def plan(selected, key_count):
    by_dest = jnp.pad(
        selected.reshape(NSEQ, 2 * NB).T, ((0, 0), (0, ROW - NSEQ)), constant_values=-1
    )
    return pl.pallas_call(
        plan_kernel,
        out_shape=(
            jax.ShapeDtypeStruct((2 * NSEQ, ROW), I32),
            jax.ShapeDtypeStruct((8, ROW), I32),
        ),
        in_specs=[VMEM, VMEM],
        out_specs=(VMEM, VMEM),
        name="plan",
    )(by_dest, key_count.reshape(NSEQ, NB))


def both_start(src_k, src_v, dst, sem):
    pltpu.make_async_copy(src_k, dst.at[0], sem).start()
    pltpu.make_async_copy(src_v, dst.at[1], sem).start()


def drain(count, like, sem):
    def one(_, carry):
        pltpu.make_async_copy(like, like, sem).wait()
        return carry

    lax.fori_loop(0, count, one, 0)


def split_kernel(me_ref, k_ref, v_ref, out_ref, sem):
    other = 1 - (me_ref[0] & 1)

    def one(index, carry):
        block = index // HALF
        chunk = block * CH + 2 * (index % HALF) + ((other - block) & 1)
        both_start(k_ref.at[chunk], v_ref.at[chunk], out_ref.at[index], sem)
        return carry

    lax.fori_loop(0, NB * HALF, one, 0)
    drain(NB * HALF, out_ref.at[0], sem)


class Place:
    def __init__(self, me, table, cap):
        self.me, self.table, self.cap = me, table, cap
        self.p = me & 1
        x, z = (me >> 3) & 3, (me >> 1) & 3
        self.u0 = jnp.where(self.p == 0, z, x)
        self.v0 = jnp.where(self.p == 0, x, z)

    def index(self, u, v, c):
        x = jnp.where(self.p == 0, v, u)
        z = jnp.where(self.p == 0, u, v)
        return (x * 4 + z) * 2 + c

    def entry(self, s, d):
        return self.table[self.p * NSEQ + s, d]

    def length(self, stage, a, b):
        a, b = a & 3, b & 3
        if stage == 0:
            e = self.entry(self.index(a, self.v0, 1), self.index(b, 3, 1))
            return ((e >> 6) & 63) + (e & 7)
        e = self.entry(self.index(3, a, 1), self.index(self.u0, b, 1))
        return ((e >> 12) & 63) + (e & 7)

    def halves(self, stage, a):
        n = self.length(stage, a, a + 2)
        return (n + 1) >> 1, n >> 1

    def here(self, stage):
        return self.u0 if stage == 0 else self.v0


def chunk_of(loc, t, plane):
    return loc * CH + 2 * t + ((plane - loc) & 1)


class Source:
    def __init__(self, place, k_ref, v_ref, sib_ref, got):
        self.place, self.k, self.v, self.sib, self.got = place, k_ref, v_ref, sib_ref, got
        self.info = []
        for stage in range(len(got)):
            b = place.here(stage)
            far_p, far_m = place.halves(stage, b + 2)
            near_p, _ = place.halves(stage, b - 1)
            _, near_m = place.halves(stage, b + 1)
            self.info.append((far_p, far_m, near_p, near_m))

    def chunk(self, stage, a, q, t, loc, own, put):
        place = self.place
        if stage < 0:

            @pl.when(own)
            def _():
                c = chunk_of(loc, t, place.p)
                put(self.k.at[c], self.v.at[c])

            @pl.when(jnp.logical_not(own))
            def _():
                put(self.sib.at[loc * HALF + t])

            return
        g1p, g1m, g2p, g2m = self.got[stage]
        far_p, far_m, near_p, near_m = self.info[stage]
        cap = place.cap
        r = (place.here(stage) - a) & 3
        plus = jnp.logical_or(r == 1, jnp.logical_and(r == 2, q < far_p))
        near = jnp.where(r == 1, near_p, near_m)
        far = jnp.where(r == 1, far_p, far_m)
        first = jnp.logical_and(r != 2, q < cap - near)
        row = jnp.where(
            r == 2,
            jnp.where(plus, q, q - far_p),
            jnp.where(first, near + q, far + q - (cap - near)),
        )
        for is_plus, is_first, ref in (
            (True, True, g1p), (False, True, g1m), (True, False, g2p), (False, False, g2m),
        ):
            cond = jnp.logical_and(plus == is_plus, first == is_first)

            @pl.when(cond)
            def _(ref=ref):
                put(ref.at[row])

    def pair(self, s, e, put):
        place = self.place
        n, loc = e & 7, (e >> 3) & 7
        c = s & 1
        x, z = (s >> 3) & 3, (s >> 1) & 3
        u = jnp.where(place.p == 0, z, x)
        v = jnp.where(place.p == 0, x, z)
        own = c == place.p
        mine = u == place.u0
        last = len(self.got) - 1

        def loop(stage, a, base):
            def one(t, carry):
                self.chunk(stage, a, base + t, t, loc, own, functools.partial(put, t))
                return carry

            lax.fori_loop(0, n, one, 0)

        def early():
            if last < 0:
                loop(-1, 0, 0)
                return

            @pl.when(mine)
            def _():
                loop(-1, 0, 0)

            @pl.when(jnp.logical_not(mine))
            def _():
                loop(0, u, (e >> 6) & 63)

        if last < 1:
            early()
        else:
            same_v = v == place.v0

            @pl.when(same_v)
            def _():
                early()

            @pl.when(jnp.logical_not(same_v))
            def _():
                loop(1, v, (e >> 12) & 63)
        return n


def copier(dst, sem):
    def put(*src):
        if len(src) == 2:
            both_start(src[0], src[1], dst, sem)
        else:
            pltpu.make_async_copy(src[0], dst, sem).start()

    return put


def pack_kernel(stage, cap, me_ref, table, k_ref, v_ref, sib_ref, *refs):
    got = (refs[:4],) if stage else ()
    s1p, s1m, s2p, s2m, sem = refs[len(refs) - 5 :]
    place = Place(me_ref[0], table, cap)
    source = Source(place, k_ref, v_ref, sib_ref, got)
    b = place.here(stage)
    half_p, half_m = place.halves(stage, b)
    pass_p, _ = place.halves(stage, b - 1)
    _, pass_m = place.halves(stage, b + 1)
    shift = 6 if stage == 0 else 12
    started = 0
    for r in (2, 1, 3):
        to = (b + r) & 3

        def one(i, count, r=r, to=to):
            if stage == 0:
                s = place.index(place.u0, place.v0, i & 1)
                d = place.index(to, i >> 2, (i >> 1) & 1)
            else:
                s = place.index(i >> 2, place.v0, (i >> 1) & 1)
                d = place.index(place.u0, to, i & 1)
            e = place.entry(s, d)
            base = (e >> shift) & 63

            def put(t, *src):
                q = base + t
                if r == 2:
                    split, low, high = half_p, (s1p, q), (s1m, q - half_p)
                elif r == 1:
                    split = cap - half_p
                    low, high = (s1p, q + half_p), (s2p, q - split + pass_p)
                else:
                    split = cap - half_m
                    low, high = (s1m, q + half_m), (s2m, q - split + pass_m)

                @pl.when(q < split)
                def _():
                    copier(low[0].at[low[1]], sem)(*src)

                @pl.when(q >= split)
                def _():
                    copier(high[0].at[high[1]], sem)(*src)

            return count + source.pair(s, e, put)

        started = lax.fori_loop(0, 16, one, started)
    drain(started, s1p.at[0], sem)


def pass_kernel(stage, cap, me_ref, table, g1p, g1m, in_p, in_m, s2p, s2m, sem):
    place = Place(me_ref[0], table, cap)
    b = place.here(stage)
    pass_p, _ = place.halves(stage, b - 1)
    _, pass_m = place.halves(stage, b + 1)
    for n, src, dst in ((pass_p, g1p, s2p), (pass_m, g1m, s2m)):

        def one(t, carry, src=src, dst=dst):
            pltpu.make_async_copy(src.at[t], dst.at[t], sem).start()
            return carry

        lax.fori_loop(0, n, one, 0)
    drain(pass_p + pass_m, s2p.at[0], sem)


def cross_kernel(cap, me_ref, table, sel, k_ref, v_ref, sib_ref, *refs):
    got = (refs[:4], refs[4:8])
    x0, x1, sem = refs[8:]
    place = Place(me_ref[0], table, cap)
    source = Source(place, k_ref, v_ref, sib_ref, got)
    dest = place.me ^ 1

    def one(n, count):
        s = sel[dest * 2 * NB + n] >> 3
        e = place.entry(s, dest)
        base = (e >> 18) & 63
        group = (n >> 1) & 1

        def put(t, *src):
            @pl.when(group == 0)
            def _():
                copier(x0.at[base + t], sem)(*src)

            @pl.when(group == 1)
            def _():
                copier(x1.at[base + t], sem)(*src)

        return count + source.pair(s, e, put)

    count = lax.fori_loop(0, 2 * NB, one, 0)
    drain(count, x0.at[0], sem)


def land_kernel(cap, me_ref, table, sel, k_ref, v_ref, sib_ref, *refs):
    got = (refs[:4], refs[4:8])
    fk0, fv0, fk1, fv1, sem = refs[8:]
    place = Place(me_ref[0], table, cap)
    source = Source(place, k_ref, v_ref, sib_ref, got)

    def one(n, count):
        s = sel[place.me * 2 * NB + n] >> 3
        e = place.entry(s, place.me)
        loc = (e >> 3) & 7
        slot = ((n >> 2) * 2 + (n & 1)) * CH

        def put(t, *src):
            row = slot + 2 * t + ((place.p - loc) & 1)
            src_k, src_v = src if len(src) == 2 else (src[0].at[0], src[0].at[1])
            for group, fk, fv in ((0, fk0, fv0), (1, fk1, fv1)):

                @pl.when(((n >> 1) & 1) == group)
                def _(fk=fk, fv=fv):
                    pltpu.make_async_copy(src_k, fk.at[row], sem).start()
                    pltpu.make_async_copy(src_v, fv.at[row], sem).start()

        return count + source.pair(s, e, put)

    count = lax.fori_loop(0, 2 * NB, one, 0)
    drain(count, sib_ref.at[0], sem)


def fill_kernel(group, me_ref, table, sel, x_ref, in_k, in_v, fk, fv, sem):
    me = me_ref[0]
    plane = 1 - (me & 1)

    def one(i, count):
        n = ((i >> 1) * 2 + group) * 2 + (i & 1)
        s = sel[me * 2 * NB + n] >> 3
        e = table[plane * NSEQ + s, me]
        loc, base = (e >> 3) & 7, (e >> 18) & 63

        def chunk(t, carry):
            row = i * CH + 2 * t + ((plane - loc) & 1)
            pltpu.make_async_copy(x_ref.at[base + t, 0], fk.at[row], sem).start()
            pltpu.make_async_copy(x_ref.at[base + t, 1], fv.at[row], sem).start()
            return carry

        lax.fori_loop(0, e & 7, chunk, 0)
        return count + (e & 7)

    count = lax.fori_loop(0, NB, one, 0)
    drain(count, x_ref.at[0], sem)


def attend_kernel(pre, q_ref, k_ref, v_ref, fk_ref, fv_ref, *rest):
    outs, (kept, out_ref) = rest[:-2], rest[-2:]
    width = q_ref.shape[2]
    scale = 1.0 / math.sqrt(HS) * math.log2(math.e)
    counts = [pre[1], pre[2], pre[3]]
    live = [iota((1, BSZ), 1) < c for c in counts]
    live_rows = [iota((BSZ, 1), 0) < c for c in counts]
    keys = (k_ref.at[0], fk_ref.at[0, 0], fk_ref.at[0, 1])
    for index, ref in enumerate((v_ref.at[0], fv_ref.at[0, 0], fv_ref.at[0, 1])):
        kept[index] = jnp.where(live_rows[index], ref[...], jnp.zeros((), BF))
    tile = 256

    def rows(i, carry):
        where = pl.ds(pl.multiple_of(i * tile, tile), tile)
        for h in range(width // HS):
            cols = slice(h * HS, (h + 1) * HS)
            q = q_ref[0, where, cols]
            scores = []
            for index in range(3):
                s = lax.dot_general(
                    q, keys[index][:, cols], (((1,), (1,)), ((), ())), preferred_element_type=F32
                )
                scores.append(jnp.where(live[index], s, -1e30))
            top = jnp.max(
                jnp.maximum(jnp.maximum(scores[0], scores[1]), scores[2]), axis=1, keepdims=True
            )
            low = top * scale
            total = jnp.zeros((tile, 1), F32)
            acc = jnp.zeros((tile, HS), F32)
            for index in range(3):
                w = jnp.exp2(scores[index] * scale - low)
                total = total + jnp.sum(w, axis=1, keepdims=True)
                acc = acc + jnp.dot(w.astype(BF), kept[index, :, cols], preferred_element_type=F32)
            out_ref[where, cols] = (acc / total).astype(BF)
        return carry

    lax.fori_loop(0, BSZ // tile, rows, 0)
    if len(outs) == 1:
        outs[0][...] = out_ref[...]
    else:
        outs[0][...] = out_ref[: BSZ // 2]
        outs[1][...] = out_ref[BSZ // 2 :]


def attend(pre, q, k, v, fk, fv, halves):
    width = q.shape[-1]
    block = pl.BlockSpec((1, BSZ, width), lambda i, pre: (pre[0], 0, 0))
    pair = pl.BlockSpec((1, 2, BSZ, width), lambda i, pre: (lax.shift_right_logical(pre[0], 1), 0, 0, 0))
    rows = BSZ // 2 if halves else BSZ
    n_out = 2 if halves else 1
    flops = 3 * 4 * BSZ * BSZ * width
    return pl.pallas_call(
        attend_kernel,
        out_shape=[jax.ShapeDtypeStruct((rows, width), BF)] * n_out,
        grid_spec=pltpu.PrefetchScalarGridSpec(
            num_scalar_prefetch=1,
            grid=(1,),
            in_specs=[block, block, block, pair, pair],
            out_specs=[pl.BlockSpec((rows, width), lambda i, pre: (0, 0))] * n_out,
            scratch_shapes=[pltpu.VMEM((3, BSZ, width), BF), pltpu.VMEM((BSZ, width), BF)],
        ),
        compiler_params=pltpu.CompilerParams(vmem_limit_bytes=48 * 2**20),
        cost_estimate=pl.CostEstimate(flops=flops, bytes_accessed=8 * BSZ * width * 2, transcendentals=0),
        name="attend",
    )(pre, q, k, v, fk, fv)


def project_kernel(pre, a0, a1, a2, a3, a4, w0, w1, w2, w3, *rest):
    o_ref = rest[-1]
    acc = jnp.dot(a0[...], w0[0], preferred_element_type=F32)
    acc += jnp.dot(a1[...], w1[0], preferred_element_type=F32)
    acc += jnp.dot(a2[...], w3[0], preferred_element_type=F32)
    half = BSZ // 2
    o_ref[:half] = (acc[:half] + jnp.dot(a3[...], w2[0], preferred_element_type=F32)).astype(BF)
    o_ref[half:] = (acc[half:] + jnp.dot(a4[...], w2[0], preferred_element_type=F32)).astype(BF)


def project(head, group, parts, w_out, before):
    width = parts[0].shape[1]
    cols = w_out.shape[1]
    tile = 512
    whole = lambda a: pl.BlockSpec(a.shape, lambda n, pre: (0, 0))
    w4 = w_out.reshape(-1, width, cols)
    weight = lambda r: pl.BlockSpec((1, width, tile), lambda n, pre: ((pre[0] - r) & 3, 0, n))
    extra = [] if before is None else [before]
    return pl.pallas_call(
        project_kernel,
        out_shape=jax.ShapeDtypeStruct((2 * BSZ, cols), BF),
        grid_spec=pltpu.PrefetchScalarGridSpec(
            num_scalar_prefetch=1,
            grid=(cols // tile,),
            in_specs=[whole(a) for a in parts] + [weight(r) for r in range(4)] + [ANY] * len(extra),
            out_specs=pl.BlockSpec((BSZ, tile), lambda n, pre: (group, n)),
        ),
        input_output_aliases={10: 0} if extra else {},
        compiler_params=pltpu.CompilerParams(vmem_limit_bytes=48 * 2**20),
        cost_estimate=pl.CostEstimate(
            flops=2 * BSZ * cols * cols, bytes_accessed=2 * cols * cols + 4 * BSZ * cols, transcendentals=0
        ),
        name="project",
    )(head, *parts, w4, w4, w4, w4, *extra)


def ring(stage, step):
    pairs = []
    for x in range(4):
        for z in range(4):
            for c in range(2):
                along_z = (c == 0) == (stage == 0)
                to = (x, (z + step) % 4) if along_z else ((x + step) % 4, z)
                pairs.append(((x * 4 + z) * 2 + c, (to[0] * 4 + to[1]) * 2 + c))
    return pairs


def copies(kernel, outs, ins, specs, name, aliases=None, moved=8 * 2**20):
    return pl.pallas_call(
        kernel,
        out_shape=outs,
        in_specs=specs,
        out_specs=[ANY] * len(outs),
        scratch_shapes=[pltpu.SemaphoreType.DMA],
        input_output_aliases=aliases or {},
        cost_estimate=pl.CostEstimate(flops=0, bytes_accessed=moved, transcendentals=0),
        name=name,
    )(*ins)


def fetch(cap, me, table, sel, kc, vc, sib):
    width = kc.shape[-1]
    sends = [jax.ShapeDtypeStruct((cap, 2, R, width), BF)] * 4
    got = []
    for stage in range(2):
        flat = [ref for group in got for ref in group]
        s1p, s1m, s2p, s2m = copies(
            functools.partial(pack_kernel, stage, cap), sends, [me, table, kc, vc, sib] + flat,
            [SMEM, SMEM] + [ANY] * (3 + len(flat)), "pack%d" % stage,
        )
        g1p = lax.ppermute(s1p, "seq", ring(stage, 1))
        g1m = lax.ppermute(s1m, "seq", ring(stage, -1))
        s2p, s2m = copies(
            functools.partial(pass_kernel, stage, cap), sends[:2], [me, table, g1p, g1m, s2p, s2m],
            [SMEM, SMEM] + [ANY] * 4, "pass%d" % stage, {4: 0, 5: 1},
        )
        g2p = lax.ppermute(s2p, "seq", ring(stage, 1))
        g2m = lax.ppermute(s2m, "seq", ring(stage, -1))
        got.append((g1p, g1m, g2p, g2m))
    flat = [ref for group in got for ref in group]
    ins = [me, table, sel, kc, vc, sib] + flat
    specs = [SMEM] * 3 + [ANY] * 11
    x_shape = jax.ShapeDtypeStruct((NB * HALF, 2, R, width), BF)
    crossed = copies(functools.partial(cross_kernel, cap), [x_shape] * 2, ins, specs, "cross")
    swap = [(i, i ^ 1) for i in range(NSEQ)]
    crossed = [lax.ppermute(x, "seq", swap) for x in crossed]
    f_shape = jax.ShapeDtypeStruct((NB * CH, R, width), BF)
    fk0, fv0, fk1, fv1 = copies(functools.partial(land_kernel, cap), [f_shape] * 4, ins, specs, "land")
    far = []
    for group, (fk, fv) in enumerate(((fk0, fv0), (fk1, fv1))):
        fk, fv = copies(
            functools.partial(fill_kernel, group), [f_shape] * 2,
            [me, table, sel, crossed[group], fk, fv], [SMEM] * 3 + [ANY] * 3, "fill%d" % group, {4: 0, 5: 1},
        )
        far.append((fk.reshape(NB // 2, 2, BSZ, width), fv.reshape(NB // 2, 2, BSZ, width)))
    return far


def before_fetch(keys, values, key_count, selected):
    width = keys.shape[1]
    me = lax.axis_index("seq").astype(I32).reshape(1)
    kc = keys.reshape(NB * CH, R, width)
    vc = values.reshape(NB * CH, R, width)
    sent = copies(
        split_kernel, [jax.ShapeDtypeStruct((NB * HALF, 2, R, width), BF)], [me, kc, vc],
        [SMEM, ANY, ANY], "split",
    )[0]
    sib = lax.ppermute(sent, "seq", [(i, i ^ 1) for i in range(NSEQ)])
    table, need = plan(selected, key_count)
    return me, kc, vc, sib, table, need[0, 0]


def on_device(queries, keys, values, key_count, selected, w_out):
    width = queries.shape[1]
    me, kc, vc, sib, table, need = before_fetch(keys, values, key_count, selected)
    sel = selected.reshape(-1)
    head = lax.axis_index("head").astype(I32).reshape(1)
    q, k, v = [a.reshape(NB, BSZ, width) for a in (queries, keys, values)]
    own = me[0] * NB + jnp.arange(NB, dtype=I32)
    chosen = lax.dynamic_slice_in_dim(selected, me[0] * NB, NB)
    pre = jnp.concatenate(
        [jnp.arange(NB, dtype=I32)[:, None], key_count[own][:, None], key_count[chosen]], axis=1
    )
    order = [(g, r) for g in range(2) for r in (2, 1, 3, 0)]
    number = jnp.stack([((head[0] + r) & 3) * 2 + g for g, r in order])
    pre = jnp.take(pre, number, axis=0)
    up = [(i, (i + 1) % 4) for i in range(4)]
    down = [(i, (i - 1) % 4) for i in range(4)]

    def rest(cap, sib, table):
        far = fetch(cap, me, table, sel, kc, vc, sib)
        out = None
        for g in range(2):
            parts = {}
            for index, (group, r) in enumerate(order):
                if group == g:
                    parts[r] = attend(pre[index], q, k, v, *far[g], halves=r == 2)
            two_a = lax.ppermute(lax.ppermute(parts[2][0], "head", up), "head", up)
            two_b = lax.ppermute(lax.ppermute(parts[2][1], "head", down), "head", down)
            one = lax.ppermute(parts[1][0], "head", up)
            three = lax.ppermute(parts[3][0], "head", down)
            out = project(head, g, [parts[0][0], one, three, two_a, two_b], w_out, out)
        return out

    level = sum((need > cap).astype(I32) for cap in LEVELS[:-1])
    return lax.switch(level, [functools.partial(rest, cap) for cap in LEVELS], sib, table)


def solution(mesh):
    placed = (P("seq", "head"), P("seq", "head"), P("seq", "head"), P(), P(), P())
    return jax.shard_map(
        on_device, mesh=mesh, in_specs=placed, out_specs=P(("seq", "head"), None), check_vma=False
    )
```

```python
import functools
import math

import jax
import jax.numpy as jnp
from jax import lax
from jax.experimental import pallas as pl
from jax.experimental.pallas import tpu as pltpu
from jax.sharding import PartitionSpec as P

HS = 128
BSZ = 512
R = 64
CH = BSZ // R
HALF = CH // 2
NB = 8
NSEQ = 32
LEVELS = (28, 30, 32, 35, 64)
ROW = 128
F32 = jnp.float32
I32 = jnp.int32
BF = jnp.bfloat16
ANY = pl.BlockSpec(memory_space=pl.ANY)
SMEM = pl.BlockSpec(memory_space=pltpu.SMEM)
VMEM = pl.BlockSpec(memory_space=pltpu.VMEM)


def mm(a, b):
    return jnp.dot(a.astype(BF), b.astype(BF), preferred_element_type=F32)


def uv_of(index, plane):
    x = lax.shift_right_logical(index, 3) & 3
    z = lax.shift_right_logical(index, 1) & 3
    return (z, x) if plane == 0 else (x, z)


def iota(shape, dim):
    return lax.broadcasted_iota(I32, shape, dim)


def plan_kernel(sel_ref, cnt_ref, table_ref, need_ref):
    s = iota((NSEQ, ROW), 0)
    d = iota((NSEQ, ROW), 1)
    loc = jnp.full((NSEQ, ROW), -1, I32)
    grp = jnp.zeros((NSEQ, ROW), I32)
    for n in range(2 * NB):
        row = sel_ref[n : n + 1, :]
        hit = lax.shift_right_arithmetic(row, 3) == s
        loc = jnp.where(hit, row & 7, loc)
        grp = jnp.where(hit, (n >> 1) & 1, grp)
    count = jnp.zeros((NSEQ, ROW), I32)
    for j in range(NB):
        count = jnp.where(loc == j, cnt_ref[:, j : j + 1], count)
    total = lax.shift_right_logical(count + (R - 1), R.bit_length() - 1)

    i32, j32 = iota((NSEQ, NSEQ), 0), iota((NSEQ, NSEQ), 1)
    i128, j128 = iota((ROW, ROW), 0), iota((ROW, ROW), 1)
    chip_l = ((i32 >> 1) == (j32 >> 1)).astype(F32)
    chip_r = ((i128 >> 1) == (j128 >> 1)).astype(F32)
    odd_l = jnp.logical_and(j32 == i32 - 1, (i32 & 1) == 1).astype(F32)
    odd_r = jnp.logical_and(i128 == j128 - 1, (j128 & 1) == 1).astype(F32)
    lower = (j32 < i32).astype(F32)
    worst = jnp.zeros((1, 1), I32)
    for plane in range(2):
        first = (plane - loc) & 1
        n_of = jnp.where(loc >= 0, lax.shift_right_logical(total - first + 1, 1), 0)
        n_f = n_of.astype(F32)
        u_i, v_i = uv_of(i128, plane)
        u_j, v_j = uv_of(j128, plane)
        m1 = jnp.logical_and(
            u_i == u_j, (v_i * 2 + (i128 & 1)) < (v_j * 2 + (j128 & 1))
        ).astype(F32)
        a_n = mm(chip_l, n_f)
        pos1 = mm(a_n, m1) + mm(odd_l, n_f)
        u_s, v_s = uv_of(i32, plane)
        u_t, v_t = uv_of(j32, plane)
        m2 = jnp.logical_and(
            v_s == v_t, (u_t * 2 + (j32 & 1)) < (u_s * 2 + (i32 & 1))
        ).astype(F32)
        n_a = mm(n_f, chip_r)
        pos2 = mm(m2, n_a) + mm(n_f, odd_r)
        pos3 = jnp.where(
            grp == 0,
            mm(lower, jnp.where(grp == 0, n_f, 0.0)),
            mm(lower, jnp.where(grp == 1, n_f, 0.0)),
        )
        entry = n_of | (jnp.maximum(loc, 0) << 3)
        for index, place in enumerate((pos1, pos2, pos3)):
            entry = entry | (place.astype(I32) << (6 + 6 * index))
        table_ref[plane * NSEQ : (plane + 1) * NSEQ, :] = entry

        u_a, v_a = uv_of(s, plane)
        u_b, v_b = uv_of(d, plane)
        g1, g2, g3 = [
            jnp.sum(jnp.where(((u_b - u_a) & 3) == r, a_n, 0.0), axis=1, keepdims=True).astype(I32)
            for r in (1, 2, 3)
        ]
        hp, hm = lax.shift_right_logical(g2 + 1, 1), lax.shift_right_logical(g2, 1)
        same = jnp.logical_and(v_s == v_t, (i32 & 1) == (j32 & 1))
        before = jnp.logical_and(same, u_t == ((u_s - 1) & 3)).astype(F32)
        after = jnp.logical_and(same, u_t == ((u_s + 1) & 3)).astype(F32)
        wide = lambda col: jnp.broadcast_to(col.astype(F32), (NSEQ, ROW))
        plus = wide(g1) + wide(hp) + mm(before, wide(hp))
        minus = wide(g3) + wide(hm) + mm(after, wide(hm))
        load = jnp.maximum(jnp.maximum(plus, minus), 2.0 * wide(hp))
        k1, k2, k3 = [
            jnp.sum(jnp.where(((v_b - v_a) & 3) == r, n_a, 0.0), axis=0, keepdims=True).astype(I32)
            for r in (1, 2, 3)
        ]
        kp, km = lax.shift_right_logical(k2 + 1, 1), lax.shift_right_logical(k2, 1)
        same_r = jnp.logical_and(u_i == u_j, (i128 & 1) == (j128 & 1))
        nxt = jnp.logical_and(same_r, v_i == ((v_j + 1) & 3)).astype(F32)
        prv = jnp.logical_and(same_r, v_i == ((v_j - 1) & 3)).astype(F32)
        tall = lambda line: jnp.broadcast_to(line.astype(F32), (NSEQ, ROW))
        plus = tall(k1) + tall(kp) + mm(tall(kp), nxt)
        minus = tall(k3) + tall(km) + mm(tall(km), prv)
        load2 = jnp.maximum(jnp.maximum(plus, minus), 2.0 * tall(kp))
        load2 = jnp.where(d < NSEQ, load2, 0.0)
        both = jnp.maximum(load, load2)
        worst = jnp.maximum(
            worst, jnp.max(jnp.max(both, axis=1, keepdims=True), axis=0, keepdims=True).astype(I32)
        )
    need_ref[...] = jnp.broadcast_to(lax.shift_right_logical(worst + 1, 1), (8, ROW))


def plan(selected, key_count):
    by_dest = jnp.pad(
        selected.reshape(NSEQ, 2 * NB).T, ((0, 0), (0, ROW - NSEQ)), constant_values=-1
    )
    return pl.pallas_call(
        plan_kernel,
        out_shape=(
            jax.ShapeDtypeStruct((2 * NSEQ, ROW), I32),
            jax.ShapeDtypeStruct((8, ROW), I32),
        ),
        in_specs=[VMEM, VMEM],
        out_specs=(VMEM, VMEM),
        name="plan",
    )(by_dest, key_count.reshape(NSEQ, NB))


def both_start(src_k, src_v, dst, sem):
    pltpu.make_async_copy(src_k, dst.at[0], sem).start()
    pltpu.make_async_copy(src_v, dst.at[1], sem).start()


def drain(count, like, sem):
    def one(_, carry):
        pltpu.make_async_copy(like, like, sem).wait()
        return carry

    lax.fori_loop(0, count, one, 0)


def spill(low, high, src, dst, sem):
    def one(row, carry):
        pltpu.make_async_copy(src.at[row], dst.at[row], sem).start()
        return carry

    lax.fori_loop(low, high, one, 0)
    return jnp.maximum(high - low, 0)


def split_kernel(me_ref, k_ref, v_ref, out_ref, sem):
    other = 1 - (me_ref[0] & 1)

    def one(index, carry):
        block = index // HALF
        chunk = block * CH + 2 * (index % HALF) + ((other - block) & 1)
        both_start(k_ref.at[chunk], v_ref.at[chunk], out_ref.at[index], sem)
        return carry

    lax.fori_loop(0, NB * HALF, one, 0)
    pltpu.make_async_copy(out_ref, out_ref, sem).wait()


class Place:
    def __init__(self, me, table, cap):
        self.me, self.table, self.cap = me, table, cap
        self.p = me & 1
        x, z = (me >> 3) & 3, (me >> 1) & 3
        self.u0 = jnp.where(self.p == 0, z, x)
        self.v0 = jnp.where(self.p == 0, x, z)

    def index(self, u, v, c):
        x = jnp.where(self.p == 0, v, u)
        z = jnp.where(self.p == 0, u, v)
        return (x * 4 + z) * 2 + c

    def entry(self, s, d):
        return self.table[self.p * NSEQ + s, d]

    def length(self, stage, a, b):
        a, b = a & 3, b & 3
        if stage == 0:
            e = self.entry(self.index(a, self.v0, 1), self.index(b, 3, 1))
            return ((e >> 6) & 63) + (e & 7)
        e = self.entry(self.index(3, a, 1), self.index(self.u0, b, 1))
        return ((e >> 12) & 63) + (e & 7)

    def halves(self, stage, a):
        n = self.length(stage, a, a + 2)
        return (n + 1) >> 1, n >> 1

    def here(self, stage):
        return self.u0 if stage == 0 else self.v0


def chunk_of(loc, t, plane):
    return loc * CH + 2 * t + ((plane - loc) & 1)


class Source:
    def __init__(self, place, k_ref, v_ref, sib_ref, got):
        self.place, self.k, self.v, self.sib, self.got = place, k_ref, v_ref, sib_ref, got
        self.info = []
        for stage in range(len(got)):
            b = place.here(stage)
            far_p, far_m = place.halves(stage, b + 2)
            near_p, _ = place.halves(stage, b - 1)
            _, near_m = place.halves(stage, b + 1)
            self.info.append((far_p, far_m, near_p, near_m))

    def chunk(self, stage, a, q, t, loc, own, put):
        place = self.place
        if stage < 0:

            @pl.when(own)
            def _():
                c = chunk_of(loc, t, place.p)
                put(self.k.at[c], self.v.at[c])

            @pl.when(jnp.logical_not(own))
            def _():
                put(self.sib.at[loc * HALF + t])

            return
        g1p, g1m, g2p, g2m = self.got[stage]
        far_p, far_m, near_p, near_m = self.info[stage]
        cap = place.cap
        r = (place.here(stage) - a) & 3
        plus = jnp.logical_or(r == 1, jnp.logical_and(r == 2, q < far_p))
        near = jnp.where(r == 1, near_p, near_m)
        far = jnp.where(r == 1, far_p, far_m)
        first = jnp.logical_and(r != 2, q < cap - near)
        row = jnp.where(
            r == 2,
            jnp.where(plus, q, q - far_p),
            jnp.where(first, near + q, far + q - (cap - near)),
        )
        for is_plus, is_first, ref in (
            (True, True, g1p), (False, True, g1m), (True, False, g2p), (False, False, g2m),
        ):
            cond = jnp.logical_and(plus == is_plus, first == is_first)

            @pl.when(cond)
            def _(ref=ref):
                put(ref.at[row])

    def pair(self, s, e, put):
        place = self.place
        n, loc = e & 7, (e >> 3) & 7
        c = s & 1
        x, z = (s >> 3) & 3, (s >> 1) & 3
        u = jnp.where(place.p == 0, z, x)
        v = jnp.where(place.p == 0, x, z)
        own = c == place.p
        mine = u == place.u0
        last = len(self.got) - 1

        def loop(stage, a, base):
            def one(t, carry):
                self.chunk(stage, a, base + t, t, loc, own, functools.partial(put, t))
                return carry

            lax.fori_loop(0, n, one, 0)

        def early():
            if last < 0:
                loop(-1, 0, 0)
                return

            @pl.when(mine)
            def _():
                loop(-1, 0, 0)

            @pl.when(jnp.logical_not(mine))
            def _():
                loop(0, u, (e >> 6) & 63)

        if last < 1:
            early()
        else:
            same_v = v == place.v0

            @pl.when(same_v)
            def _():
                early()

            @pl.when(jnp.logical_not(same_v))
            def _():
                loop(1, v, (e >> 12) & 63)
        return n


def copier(dst, sem):
    def put(*src):
        if len(src) == 2:
            both_start(src[0], src[1], dst, sem)
        else:
            pltpu.make_async_copy(src[0], dst, sem).start()

    return put


def pack_kernel(stage, cap, me_ref, table, k_ref, v_ref, sib_ref, *refs):
    got = (refs[:4],) if stage else ()
    outs = refs[len(refs) - 10 : len(refs) - 6]
    s1p, s1m, s2p, s2m, sem, sem_out = refs[len(refs) - 6 :]
    place = Place(me_ref[0], table, cap)
    source = Source(place, k_ref, v_ref, sib_ref, got)
    b = place.here(stage)
    half_p, half_m = place.halves(stage, b)
    pass_p, _ = place.halves(stage, b - 1)
    _, pass_m = place.halves(stage, b + 1)
    shift = 6 if stage == 0 else 12
    started = 0
    for r in (2, 1, 3):
        to = (b + r) & 3

        def one(i, count, r=r, to=to):
            if stage == 0:
                s = place.index(place.u0, place.v0, i & 1)
                d = place.index(to, i >> 2, (i >> 1) & 1)
            else:
                s = place.index(i >> 2, place.v0, (i >> 1) & 1)
                d = place.index(place.u0, to, i & 1)
            e = place.entry(s, d)
            base = (e >> shift) & 63

            def put(t, *src):
                q = base + t
                if r == 2:
                    split, low, high = half_p, (s1p, q), (s1m, q - half_p)
                elif r == 1:
                    split = cap - half_p
                    low, high = (s1p, q + half_p), (s2p, q - split + pass_p)
                else:
                    split = cap - half_m
                    low, high = (s1m, q + half_m), (s2m, q - split + pass_m)

                @pl.when(q < split)
                def _():
                    copier(low[0].at[low[1]], sem)(*src)

                @pl.when(q >= split)
                def _():
                    copier(high[0].at[high[1]], sem)(*src)

            return count + source.pair(s, e, put)

        started = lax.fori_loop(0, 16, one, started)
    drain(started, s1p.at[0], sem)
    started = 0
    for half, passed, n, first, second, out1, out2 in (
        (half_p, pass_p, place.length(stage, b, b + 1), s1p, s2p, outs[0], outs[2]),
        (half_m, pass_m, place.length(stage, b, b - 1), s1m, s2m, outs[1], outs[3]),
    ):
        fits = jnp.minimum(n, cap - half)
        started += spill(0, half + fits, first, out1, sem_out)
        started += spill(passed, passed + n - fits, second, out2, sem_out)
    drain(started, s1p.at[0], sem_out)


def pass_kernel(stage, cap, me_ref, table, g1p, g1m, in_p, in_m, s2p, s2m, hold_p, hold_m, sem, sem_out):
    place = Place(me_ref[0], table, cap)
    b = place.here(stage)
    pass_p, _ = place.halves(stage, b - 1)
    _, pass_m = place.halves(stage, b + 1)
    started = spill(0, pass_p, g1p, hold_p, sem) + spill(0, pass_m, g1m, hold_m, sem)
    drain(started, hold_p.at[0], sem)
    started = spill(0, pass_p, hold_p, s2p, sem_out) + spill(0, pass_m, hold_m, s2m, sem_out)
    drain(started, hold_p.at[0], sem_out)


def cross_kernel(cap, me_ref, table, sel, k_ref, v_ref, sib_ref, *refs):
    got = (refs[:4], refs[4:8])
    out0, out1, x0, x1, sem, sem_out = refs[8:]
    place = Place(me_ref[0], table, cap)
    source = Source(place, k_ref, v_ref, sib_ref, got)
    dest = place.me ^ 1

    def one(n, counts):
        s = sel[dest * 2 * NB + n] >> 3
        e = place.entry(s, dest)
        base = (e >> 18) & 63
        group = (n >> 1) & 1

        def put(t, *src):
            @pl.when(group == 0)
            def _():
                copier(x0.at[base + t], sem)(*src)

            @pl.when(group == 1)
            def _():
                copier(x1.at[base + t], sem)(*src)

        here = source.pair(s, e, put)
        return counts[0] + jnp.where(group == 0, here, 0), counts[1] + jnp.where(group == 1, here, 0)

    count0, count1 = lax.fori_loop(0, 2 * NB, one, (0, 0))
    drain(count0 + count1, x0.at[0], sem)
    started = spill(0, count0, x0, out0, sem_out) + spill(0, count1, x1, out1, sem_out)
    drain(started, x0.at[0], sem_out)


SIZES = (4, 6, 8, 10, 12)
TILE = 256


def attend_kernel(cap, pre, table, sel, q_ref, k_ref, v_ref, sib_ref, *refs):
    got = (refs[:4], refs[4:8])
    x_ref, refs = refs[8], refs[9:]
    outs, (kb, vb, bias, out_ref, sem) = refs[:-5], refs[-5:]
    width = q_ref.shape[2]
    scale = 1.0 / math.sqrt(HS) * math.log2(math.e)
    block, me = pre[0], pre[4]
    place = Place(me, table, cap)
    source = Source(place, k_ref, v_ref, sib_ref, got)
    plane = 1 - place.p

    live = [lax.shift_right_logical(pre[1 + i] + (R - 1), R.bit_length() - 1) for i in range(3)]
    starts = [0, live[0], live[0] + live[1]]
    chunks = starts[2] + live[2]

    def one(t, carry):
        pltpu.make_async_copy(k_ref.at[block * CH + t], kb.at[t], sem).start()
        pltpu.make_async_copy(v_ref.at[block * CH + t], vb.at[t], sem).start()
        return carry

    lax.fori_loop(0, live[0], one, 0)
    for i in range(2):
        s = sel[(me * NB + block) * 2 + i] >> 3
        e = place.entry(s, me)
        loc = (e >> 3) & 7
        start = starts[1 + i]

        def put(t, *src):
            row = start + 2 * t + ((place.p - loc) & 1)
            src_k, src_v = src if len(src) == 2 else (src[0].at[0], src[0].at[1])
            pltpu.make_async_copy(src_k, kb.at[row], sem).start()
            pltpu.make_async_copy(src_v, vb.at[row], sem).start()

        source.pair(s, e, put)
        other = table[plane * NSEQ + s, me]
        base = (other >> 18) & 63

        def cross(t, carry):
            row = start + 2 * t + ((plane - loc) & 1)
            pltpu.make_async_copy(x_ref.at[base + t, 0], kb.at[row], sem).start()
            pltpu.make_async_copy(x_ref.at[base + t, 1], vb.at[row], sem).start()
            return carry

        lax.fori_loop(0, other & 7, cross, 0)

    key = iota((3 * BSZ, HS), 0)
    dead = jnp.ones((3 * BSZ, HS), jnp.bool_)
    for i in range(3):
        begin = starts[i] * R
        dead = jnp.logical_and(dead, jnp.logical_or(key < begin, key >= begin + pre[1 + i]))
    column = iota((3 * BSZ, HS), 1)
    bias[...] = jnp.where(jnp.logical_and(dead, column == 0), -1e30, 0.0).astype(BF)
    hot = (iota((TILE, HS), 1) == 0).astype(F32).astype(BF)

    for extra in range(4):

        @pl.when(chunks + extra < 3 * CH)
        def _():
            kb[chunks + extra] = jnp.zeros((R, width), BF)
            vb[chunks + extra] = jnp.zeros((R, width), BF)

    @pl.when(chunks < 4)
    def _():
        kb[7] = jnp.zeros((R, width), BF)
        vb[7] = jnp.zeros((R, width), BF)

    drain(2 * chunks, kb.at[0], sem)

    def work(tiles):
        keys = tiles * HS
        ones = jnp.ones((keys, HS), BF)

        def step(it, carry):
            rows = pl.ds(pl.multiple_of((it >> 1) * TILE, TILE), TILE)
            for side in range(2):
                cols = pl.ds(pl.multiple_of(((it & 1) * 2 + side) * HS, HS), HS)
                q = jnp.concatenate([q_ref[0, rows, cols], hot], axis=1)
                k = kb[: tiles * 2, :, cols].reshape(keys, HS)
                k = jnp.concatenate([k, bias[:keys]], axis=1)
                s = lax.dot_general(q, k, (((1,), (1,)), ((), ())), preferred_element_type=F32)
                low = jnp.max(s, axis=1, keepdims=True) * scale
                w = jnp.exp2(s * scale - low).astype(BF)
                v = jnp.concatenate([vb[: tiles * 2, :, cols].reshape(keys, HS), ones], axis=1)
                a = jnp.dot(w, v, preferred_element_type=F32)
                out_ref[rows, cols] = (a[:, :HS] / a[:, HS:]).astype(BF)
            return carry

        lax.fori_loop(0, BSZ // TILE * 2, step, 0)

    least = 0
    for tiles in SIZES:
        pl.when(jnp.logical_and(chunks > least, chunks <= 2 * tiles))(functools.partial(work, tiles))
        least = 2 * tiles
    if len(outs) == 1:
        outs[0][...] = out_ref[...]
    else:
        outs[0][...] = out_ref[: BSZ // 2]
        outs[1][...] = out_ref[BSZ // 2 :]


def attend(cap, pre, table, sel, q, kc, vc, sib, got, crossed, halves):
    width = q.shape[-1]
    rows = BSZ // 2 if halves else BSZ
    n_out = 2 if halves else 1
    return pl.pallas_call(
        functools.partial(attend_kernel, cap),
        out_shape=[jax.ShapeDtypeStruct((rows, width), BF)] * n_out,
        grid_spec=pltpu.PrefetchScalarGridSpec(
            num_scalar_prefetch=1,
            grid=(1,),
            in_specs=[SMEM, SMEM, pl.BlockSpec((1, BSZ, width), lambda i, pre: (pre[0], 0, 0))] + [ANY] * 12,
            out_specs=[pl.BlockSpec((rows, width), lambda i, pre: (0, 0))] * n_out,
            scratch_shapes=[
                pltpu.VMEM((3 * CH, R, width), BF),
                pltpu.VMEM((3 * CH, R, width), BF),
                pltpu.VMEM((3 * BSZ, HS), BF),
                pltpu.VMEM((BSZ, width), BF),
                pltpu.SemaphoreType.DMA,
            ],
        ),
        compiler_params=pltpu.CompilerParams(vmem_limit_bytes=48 * 2**20),
        cost_estimate=pl.CostEstimate(
            flops=12 * BSZ * BSZ * width, bytes_accessed=8 * BSZ * width * 2, transcendentals=0
        ),
        name="attend",
    )(pre, table, sel, q, kc, vc, sib, *got, crossed)


def project_kernel(pre, a0, a1, a2, a3, a4, w0, w1, w2, w3, *rest):
    o_ref = rest[-1]
    acc = jnp.dot(a0[...], w0[0], preferred_element_type=F32)
    acc += jnp.dot(a1[...], w1[0], preferred_element_type=F32)
    acc += jnp.dot(a2[...], w3[0], preferred_element_type=F32)
    half = BSZ // 2
    o_ref[:half] = (acc[:half] + jnp.dot(a3[...], w2[0], preferred_element_type=F32)).astype(BF)
    o_ref[half:] = (acc[half:] + jnp.dot(a4[...], w2[0], preferred_element_type=F32)).astype(BF)


def project(head, group, parts, w_out, before):
    width = parts[0].shape[1]
    cols = w_out.shape[1]
    tile = 512
    whole = lambda a: pl.BlockSpec(a.shape, lambda n, pre: (0, 0))
    w4 = w_out.reshape(-1, width, cols)
    weight = lambda r: pl.BlockSpec((1, width, tile), lambda n, pre: ((pre[0] - r) & 3, 0, n))
    extra = [] if before is None else [before]
    return pl.pallas_call(
        project_kernel,
        out_shape=jax.ShapeDtypeStruct((2 * BSZ, cols), BF),
        grid_spec=pltpu.PrefetchScalarGridSpec(
            num_scalar_prefetch=1,
            grid=(cols // tile,),
            in_specs=[whole(a) for a in parts] + [weight(r) for r in range(4)] + [ANY] * len(extra),
            out_specs=pl.BlockSpec((BSZ, tile), lambda n, pre: (group, n)),
        ),
        input_output_aliases={10: 0} if extra else {},
        compiler_params=pltpu.CompilerParams(vmem_limit_bytes=48 * 2**20),
        cost_estimate=pl.CostEstimate(
            flops=2 * BSZ * cols * cols, bytes_accessed=2 * cols * cols + 4 * BSZ * cols, transcendentals=0
        ),
        name="project",
    )(head, *parts, w4, w4, w4, w4, *extra)


def ring(stage, step):
    pairs = []
    for x in range(4):
        for z in range(4):
            for c in range(2):
                along_z = (c == 0) == (stage == 0)
                to = (x, (z + step) % 4) if along_z else ((x + step) % 4, z)
                pairs.append(((x * 4 + z) * 2 + c, (to[0] * 4 + to[1]) * 2 + c))
    return pairs


def copies(kernel, outs, ins, specs, hold, name, aliases=None, moved=8 * 2**20):
    return pl.pallas_call(
        kernel,
        out_shape=outs,
        in_specs=specs,
        out_specs=[ANY] * len(outs),
        scratch_shapes=[pltpu.VMEM(a.shape, a.dtype) for a in hold] + [pltpu.SemaphoreType.DMA] * 2,
        input_output_aliases=aliases or {},
        compiler_params=pltpu.CompilerParams(vmem_limit_bytes=56 * 2**20),
        cost_estimate=pl.CostEstimate(flops=0, bytes_accessed=moved, transcendentals=0),
        name=name,
    )(*ins)


def fetch(cap, me, table, sel, kc, vc, sib):
    width = kc.shape[-1]
    sends = [jax.ShapeDtypeStruct((cap, 2, R, width), BF)] * 4
    got = []
    for stage in range(2):
        s1p, s1m, s2p, s2m = copies(
            functools.partial(pack_kernel, stage, cap), sends, [me, table, kc, vc, sib] + got,
            [SMEM, SMEM] + [ANY] * (3 + len(got)), sends, "pack%d" % stage,
        )
        g1p = lax.ppermute(s1p, "seq", ring(stage, 1))
        g1m = lax.ppermute(s1m, "seq", ring(stage, -1))
        s2p, s2m = copies(
            functools.partial(pass_kernel, stage, cap), sends[:2], [me, table, g1p, g1m, s2p, s2m],
            [SMEM, SMEM] + [ANY] * 4, sends[:2], "pass%d" % stage, {4: 0, 5: 1},
        )
        g2p = lax.ppermute(s2p, "seq", ring(stage, 1))
        g2m = lax.ppermute(s2m, "seq", ring(stage, -1))
        got += [g1p, g1m, g2p, g2m]
    x_shapes = [jax.ShapeDtypeStruct((NB * HALF, 2, R, width), BF)] * 2
    crossed = copies(
        functools.partial(cross_kernel, cap), x_shapes, [me, table, sel, kc, vc, sib] + got,
        [SMEM] * 3 + [ANY] * 11, x_shapes, "cross",
    )
    swap = [(i, i ^ 1) for i in range(NSEQ)]
    return got, [lax.ppermute(x, "seq", swap) for x in crossed]


def before_fetch(keys, values, key_count, selected):
    width = keys.shape[1]
    me = lax.axis_index("seq").astype(I32).reshape(1)
    kc = keys.reshape(NB * CH, R, width)
    vc = values.reshape(NB * CH, R, width)
    sent = pl.pallas_call(
        split_kernel,
        out_shape=jax.ShapeDtypeStruct((NB * HALF, 2, R, width), BF),
        in_specs=[SMEM, ANY, ANY],
        out_specs=VMEM,
        scratch_shapes=[pltpu.SemaphoreType.DMA],
        compiler_params=pltpu.CompilerParams(vmem_limit_bytes=32 * 2**20),
        cost_estimate=pl.CostEstimate(flops=0, bytes_accessed=8 * 2**20, transcendentals=0),
        name="split",
    )(me, kc, vc)
    sib = lax.ppermute(sent, "seq", [(i, i ^ 1) for i in range(NSEQ)])
    table, need = plan(selected, key_count)
    return me, kc, vc, sib, table, need[0, 0]


def on_device(queries, keys, values, key_count, selected, w_out):
    width = queries.shape[1]
    me, kc, vc, sib, table, need = before_fetch(keys, values, key_count, selected)
    sel = selected.reshape(-1)
    head = lax.axis_index("head").astype(I32).reshape(1)
    q = queries.reshape(NB, BSZ, width)
    own = me[0] * NB + jnp.arange(NB, dtype=I32)
    chosen = lax.dynamic_slice_in_dim(selected, me[0] * NB, NB)
    pre = jnp.concatenate(
        [
            jnp.arange(NB, dtype=I32)[:, None], key_count[own][:, None], key_count[chosen],
            jnp.broadcast_to(me, (NB, 1)),
        ],
        axis=1,
    )
    order = [(g, r) for g in range(2) for r in (2, 1, 3, 0)]
    number = jnp.stack([((head[0] + r) & 3) * 2 + g for g, r in order])
    pre = jnp.take(pre, number, axis=0)
    up = [(i, (i + 1) % 4) for i in range(4)]
    down = [(i, (i - 1) % 4) for i in range(4)]

    def rest(cap, sib, table):
        got, crossed = fetch(cap, me, table, sel, kc, vc, sib)
        out = None
        for g in range(2):
            parts = {}
            for index, (group, r) in enumerate(order):
                if group == g:
                    parts[r] = attend(
                        cap, pre[index], table, sel, q, kc, vc, sib, got, crossed[g], halves=r == 2
                    )
            two_a = lax.ppermute(lax.ppermute(parts[2][0], "head", up), "head", up)
            two_b = lax.ppermute(lax.ppermute(parts[2][1], "head", down), "head", down)
            one = lax.ppermute(parts[1][0], "head", up)
            three = lax.ppermute(parts[3][0], "head", down)
            out = project(head, g, [parts[0][0], one, three, two_a, two_b], w_out, out)
        return out

    level = sum((need > cap).astype(I32) for cap in LEVELS[:-1])
    return lax.switch(level, [functools.partial(rest, cap) for cap in LEVELS], sib, table)


def solution(mesh):
    placed = (P("seq", "head"), P("seq", "head"), P("seq", "head"), P(), P(), P())
    return jax.shard_map(
        on_device, mesh=mesh, in_specs=placed, out_specs=P(("seq", "head"), None), check_vma=False
    )
```

```python
import functools
import math

import jax
import jax.numpy as jnp
from jax import lax
from jax.experimental import pallas as pl
from jax.experimental.pallas import tpu as pltpu
from jax.sharding import PartitionSpec as P

HS = 128
BSZ = 512
R = 64
CH = BSZ // R
HALF = CH // 2
NB = 8
NSEQ = 32
LEVELS = ((21, 24), (22, 25), (23, 27), (26, 30), (64, 64))
VLIM = 60 * 2**20
ROW = 128
F32 = jnp.float32
I32 = jnp.int32
BF = jnp.bfloat16
ANY = pl.BlockSpec(memory_space=pl.ANY)
SMEM = pl.BlockSpec(memory_space=pltpu.SMEM)
VMEM = pl.BlockSpec(memory_space=pltpu.VMEM)


def mm(a, b):
    return jnp.dot(a.astype(BF), b.astype(BF), preferred_element_type=F32)


def uv_of(index, plane):
    x = lax.shift_right_logical(index, 3) & 3
    z = lax.shift_right_logical(index, 1) & 3
    return (z, x) if plane == 0 else (x, z)


def iota(shape, dim):
    return lax.broadcasted_iota(I32, shape, dim)


def plan_kernel(sel_ref, cnt_ref, table_ref):
    s = iota((NSEQ, ROW), 0)
    d = iota((NSEQ, ROW), 1)
    loc = jnp.full((NSEQ, ROW), -1, I32)
    grp = jnp.zeros((NSEQ, ROW), I32)
    for n in range(2 * NB):
        row = sel_ref[n : n + 1, :]
        hit = lax.shift_right_arithmetic(row, 3) == s
        loc = jnp.where(hit, row & 7, loc)
        grp = jnp.where(hit, (n >> 1) & 1, grp)
    count = jnp.zeros((NSEQ, ROW), I32)
    for j in range(NB):
        count = jnp.where(loc == j, cnt_ref[:, j : j + 1], count)
    total = lax.shift_right_logical(count + (R - 1), R.bit_length() - 1)

    i32, j32 = iota((NSEQ, NSEQ), 0), iota((NSEQ, NSEQ), 1)
    i128, j128 = iota((ROW, ROW), 0), iota((ROW, ROW), 1)
    chip_l = ((i32 >> 1) == (j32 >> 1)).astype(F32)
    chip_r = ((i128 >> 1) == (j128 >> 1)).astype(F32)
    odd_l = jnp.logical_and(j32 == i32 - 1, (i32 & 1) == 1).astype(F32)
    odd_r = jnp.logical_and(i128 == j128 - 1, (j128 & 1) == 1).astype(F32)
    lower = (j32 < i32).astype(F32)
    for plane in range(2):
        first = (plane - loc) & 1
        n_of = jnp.where(loc >= 0, lax.shift_right_logical(total - first + 1, 1), 0)
        n_f = n_of.astype(F32)
        u_i, v_i = uv_of(i128, plane)
        u_j, v_j = uv_of(j128, plane)
        same_u = u_i == u_j
        m1 = jnp.logical_and(same_u, (v_i * 2 + (i128 & 1)) < (v_j * 2 + (j128 & 1))).astype(F32)
        same_u = same_u.astype(F32)
        dup = jnp.zeros((NSEQ, ROW), jnp.bool_)
        for j in range(NB):
            is_j = loc == j
            dup = jnp.logical_or(dup, jnp.logical_and(is_j, mm(is_j.astype(F32), m1) > 0.5))
        n1 = jnp.where(dup, 0.0, n_f)
        a_n = mm(chip_l, n1)
        pos1 = mm(a_n, m1) + mm(odd_l, n1)
        of_first = jnp.zeros((NSEQ, ROW), F32)
        for j in range(NB):
            is_j = loc == j
            there = mm(jnp.where(jnp.logical_and(is_j, jnp.logical_not(dup)), pos1, 0.0), same_u)
            of_first = jnp.where(is_j, there, of_first)
        pos1 = jnp.where(dup, of_first, pos1)
        u_s, v_s = uv_of(i32, plane)
        u_t, v_t = uv_of(j32, plane)
        same_v = v_s == v_t
        m2 = jnp.logical_and(same_v, (u_t * 2 + (j32 & 1)) < (u_s * 2 + (i32 & 1))).astype(F32)
        pos2 = mm(m2, mm(n_f, chip_r)) + mm(n_f, odd_r)
        pos3 = jnp.where(
            grp == 0,
            mm(lower, jnp.where(grp == 0, n_f, 0.0)),
            mm(lower, jnp.where(grp == 1, n_f, 0.0)),
        )
        entry = n_of | (jnp.maximum(loc, 0) << 3)
        for index, place in enumerate((pos1, pos2, pos3)):
            entry = entry | (place.astype(I32) << (6 + 6 * index))
        entry = entry | (dup.astype(I32) << 24)

        to_u = jnp.logical_and(i128 < NSEQ, j128 - NSEQ == u_i).astype(F32)
        to_v = jnp.logical_and(i128 < NSEQ, j128 - NSEQ - 4 == v_i).astype(F32)
        u_a, _ = uv_of(s, plane)
        u_b, _ = uv_of(d, plane)
        line = jnp.where(u_a == u_b, mm(same_v.astype(F32), n_f), 0.0)
        lengths = mm(a_n, to_u) + mm(line, to_v)
        table_ref[plane * NSEQ : (plane + 1) * NSEQ, :] = jnp.where(d < NSEQ, entry, lengths.astype(I32))


def balance_kernel(table, share_ref, level_ref):
    def one(ring_number, need):
        plane, stage, g = ring_number >> 3, (ring_number >> 2) & 1, ring_number & 3
        by_x = plane == stage
        rows = [
            plane * NSEQ + jnp.where(by_x, g * 4 + a, a * 4 + g) * 2 for a in range(4)
        ]
        far = NSEQ + stage * 4
        l1, l2, l3 = [[table[rows[a], far + ((a + r) & 3)] for a in range(4)] for r in (1, 2, 3)]
        h = [(n + 1) >> 1 for n in l2]

        def loads():
            plus = [l1[a] + h[a] + h[(a - 1) & 3] for a in range(4)]
            minus = [l3[a] + l2[a] - h[a] + l2[(a + 1) & 3] - h[(a + 1) & 3] for a in range(4)]
            return plus, minus

        for a in range(4):
            plus, minus = loads()
            high = jnp.maximum(plus[a], plus[(a + 1) & 3]) - h[a]
            low = jnp.maximum(minus[a], minus[(a - 1) & 3]) - (l2[a] - h[a])
            h[a] = jnp.clip((low + l2[a] - high + 1) >> 1, 0, l2[a])
        plus, minus = loads()
        most = functools.reduce(jnp.maximum, plus + minus)
        least = functools.reduce(jnp.maximum, h + [l2[a] - h[a] for a in range(4)])
        for a in range(4):
            share_ref[ring_number * 4 + a] = h[a]
        here = jnp.maximum((most + 1) >> 1, least)
        return (
            jnp.where(stage == 0, jnp.maximum(need[0], here), need[0]),
            jnp.where(stage == 1, jnp.maximum(need[1], here), need[1]),
        )

    need = lax.fori_loop(0, 16, one, (jnp.int32(0), jnp.int32(0)))
    level = jnp.int32(0)
    for cap in LEVELS[:-1]:
        level += jnp.logical_or(need[0] > cap[0], need[1] > cap[1]).astype(I32)
    level_ref[0] = level


def plan(selected, key_count):
    by_dest = jnp.pad(
        selected.reshape(NSEQ, 2 * NB).T, ((0, 0), (0, ROW - NSEQ)), constant_values=-1
    )
    table = pl.pallas_call(
        plan_kernel,
        out_shape=jax.ShapeDtypeStruct((2 * NSEQ, ROW), I32),
        in_specs=[VMEM, VMEM],
        out_specs=VMEM,
        compiler_params=pltpu.CompilerParams(vmem_limit_bytes=VLIM),
        name="plan",
    )(by_dest, key_count.reshape(NSEQ, NB))
    share, level = pl.pallas_call(
        balance_kernel,
        out_shape=(jax.ShapeDtypeStruct((64,), I32), jax.ShapeDtypeStruct((1,), I32)),
        in_specs=[SMEM],
        out_specs=(SMEM, SMEM),
        compiler_params=pltpu.CompilerParams(vmem_limit_bytes=VLIM),
        name="balance",
    )(table)
    return table, share, level[0]


def both_start(src_k, src_v, dst, sem):
    pltpu.make_async_copy(src_k, dst.at[0], sem).start()
    pltpu.make_async_copy(src_v, dst.at[1], sem).start()


def drain(count, like, sem):
    def one(_, carry):
        pltpu.make_async_copy(like, like, sem).wait()
        return carry

    lax.fori_loop(0, count, one, 0)


def spill(low, high, src, dst, sem):
    def one(row, carry):
        pltpu.make_async_copy(src.at[row], dst.at[row], sem).start()
        return carry

    lax.fori_loop(low, high, one, 0)
    return jnp.maximum(high - low, 0)


def split_kernel(me_ref, k_ref, v_ref, out_ref, sem):
    other = 1 - (me_ref[0] & 1)

    def one(index, carry):
        block = index // HALF
        chunk = block * CH + 2 * (index % HALF) + ((other - block) & 1)
        both_start(k_ref.at[chunk], v_ref.at[chunk], out_ref.at[index], sem)
        return carry

    lax.fori_loop(0, NB * HALF, one, 0)
    pltpu.make_async_copy(out_ref, out_ref, sem).wait()


class Place:
    def __init__(self, me, table, share, caps):
        self.me, self.table, self.share, self.caps = me, table, share, caps
        self.p = me & 1
        x, z = (me >> 3) & 3, (me >> 1) & 3
        self.u0 = jnp.where(self.p == 0, z, x)
        self.v0 = jnp.where(self.p == 0, x, z)

    def index(self, u, v, c):
        x = jnp.where(self.p == 0, v, u)
        z = jnp.where(self.p == 0, u, v)
        return (x * 4 + z) * 2 + c

    def entry(self, s, d):
        return self.table[self.p * NSEQ + s, d]

    def length(self, stage, a, b):
        a, b = a & 3, b & 3
        node = self.index(a, self.v0, 0) if stage == 0 else self.index(self.u0, a, 0)
        return self.table[self.p * NSEQ + node, NSEQ + 4 * stage + b]

    def halves(self, stage, a):
        a = a & 3
        ring_of = self.v0 if stage == 0 else self.u0
        h = self.share[((self.p * 2 + stage) * 4 + ring_of) * 4 + a]
        return h, self.length(stage, a, a + 2) - h

    def here(self, stage):
        return self.u0 if stage == 0 else self.v0


def chunk_of(loc, t, plane):
    return loc * CH + 2 * t + ((plane - loc) & 1)


class Source:
    def __init__(self, place, k_ref, v_ref, sib_ref, got):
        self.place, self.k, self.v, self.sib, self.got = place, k_ref, v_ref, sib_ref, got
        self.info = []
        for stage in range(len(got)):
            b = place.here(stage)
            far_p, far_m = place.halves(stage, b + 2)
            near_p, _ = place.halves(stage, b - 1)
            _, near_m = place.halves(stage, b + 1)
            self.info.append((far_p, far_m, near_p, near_m))

    def chunk(self, stage, a, q, t, loc, own, put):
        place = self.place
        if stage < 0:

            @pl.when(own)
            def _():
                c = chunk_of(loc, t, place.p)
                put(self.k.at[c], self.v.at[c])

            @pl.when(jnp.logical_not(own))
            def _():
                put(self.sib.at[loc * HALF + t])

            return
        g1p, g1m, g2p, g2m = self.got[stage]
        far_p, far_m, near_p, near_m = self.info[stage]
        cap = place.caps[stage]
        r = (place.here(stage) - a) & 3
        plus = jnp.logical_or(r == 1, jnp.logical_and(r == 2, q < far_p))
        near = jnp.where(r == 1, near_p, near_m)
        far = jnp.where(r == 1, far_p, far_m)
        first = jnp.logical_and(r != 2, q < cap - near)
        row = jnp.where(
            r == 2,
            jnp.where(plus, q, q - far_p),
            jnp.where(first, near + q, far + q - (cap - near)),
        )
        for is_plus, is_first, ref in (
            (True, True, g1p), (False, True, g1m), (True, False, g2p), (False, False, g2m),
        ):
            cond = jnp.logical_and(plus == is_plus, first == is_first)

            @pl.when(cond)
            def _(ref=ref):
                put(ref.at[row])

    def pair(self, s, e, put):
        place = self.place
        n, loc = e & 7, (e >> 3) & 7
        c = s & 1
        x, z = (s >> 3) & 3, (s >> 1) & 3
        u = jnp.where(place.p == 0, z, x)
        v = jnp.where(place.p == 0, x, z)
        own = c == place.p
        mine = u == place.u0
        last = len(self.got) - 1

        def loop(stage, a, base):
            def one(t, carry):
                self.chunk(stage, a, base + t, t, loc, own, functools.partial(put, t))
                return carry

            lax.fori_loop(0, n, one, 0)

        def early():
            if last < 0:
                loop(-1, 0, 0)
                return

            @pl.when(mine)
            def _():
                loop(-1, 0, 0)

            @pl.when(jnp.logical_not(mine))
            def _():
                loop(0, u, (e >> 6) & 63)

        if last < 1:
            early()
        else:
            same_v = v == place.v0

            @pl.when(same_v)
            def _():
                early()

            @pl.when(jnp.logical_not(same_v))
            def _():
                loop(1, v, (e >> 12) & 63)
        return n


def copier(dst, sem):
    def put(*src):
        if len(src) == 2:
            both_start(src[0], src[1], dst, sem)
        else:
            pltpu.make_async_copy(src[0], dst, sem).start()

    return put


def pack_kernel(stage, caps, me_ref, table, share, k_ref, v_ref, sib_ref, *refs):
    got = (refs[:4],) if stage else ()
    outs = refs[len(refs) - 10 : len(refs) - 6]
    s1p, s1m, s2p, s2m, sem, sem_out = refs[len(refs) - 6 :]
    place = Place(me_ref[0], table, share, caps)
    source = Source(place, k_ref, v_ref, sib_ref, got)
    b = place.here(stage)
    cap = caps[stage]
    half_p, half_m = place.halves(stage, b)
    pass_p, _ = place.halves(stage, b - 1)
    _, pass_m = place.halves(stage, b + 1)
    shift = 6 if stage == 0 else 12
    started = 0
    for r in (2, 1, 3):
        to = (b + r) & 3

        def one(i, count, r=r, to=to):
            if stage == 0:
                s = place.index(place.u0, place.v0, i & 1)
                d = place.index(to, i >> 2, (i >> 1) & 1)
            else:
                s = place.index(i >> 2, place.v0, (i >> 1) & 1)
                d = place.index(place.u0, to, i & 1)
            e = place.entry(s, d)
            base = (e >> shift) & 63
            if stage == 0:
                e = jnp.where((e >> 24) & 1 == 1, 0, e)

            def put(t, *src):
                q = base + t
                if r == 2:
                    split, low, high = half_p, (s1p, q), (s1m, q - half_p)
                elif r == 1:
                    split = cap - half_p
                    low, high = (s1p, q + half_p), (s2p, q - split + pass_p)
                else:
                    split = cap - half_m
                    low, high = (s1m, q + half_m), (s2m, q - split + pass_m)

                @pl.when(q < split)
                def _():
                    copier(low[0].at[low[1]], sem)(*src)

                @pl.when(q >= split)
                def _():
                    copier(high[0].at[high[1]], sem)(*src)

            return count + source.pair(s, e, put)

        started = lax.fori_loop(0, 16, one, started)
    drain(started, s1p.at[0], sem)
    started = 0
    for half, passed, n, first, second, out1, out2 in (
        (half_p, pass_p, place.length(stage, b, b + 1), s1p, s2p, outs[0], outs[2]),
        (half_m, pass_m, place.length(stage, b, b - 1), s1m, s2m, outs[1], outs[3]),
    ):
        fits = jnp.minimum(n, cap - half)
        started += spill(0, half + fits, first, out1, sem_out)
        started += spill(passed, passed + n - fits, second, out2, sem_out)
    drain(started, s1p.at[0], sem_out)


def pass_kernel(stage, caps, me_ref, table, share, g1p, g1m, in_p, in_m, after, s2p, s2m, hold_p, hold_m, sem, sem_out):
    place = Place(me_ref[0], table, share, caps)
    b = place.here(stage)
    pass_p, _ = place.halves(stage, b - 1)
    _, pass_m = place.halves(stage, b + 1)
    started = spill(0, pass_p, g1p, hold_p, sem) + spill(0, pass_m, g1m, hold_m, sem)
    drain(started, hold_p.at[0], sem)
    started = spill(0, pass_p, hold_p, s2p, sem_out) + spill(0, pass_m, hold_m, s2m, sem_out)
    drain(started, hold_p.at[0], sem_out)


def cross_kernel(caps, me_ref, table, share, sel, k_ref, v_ref, sib_ref, *refs):
    got = (refs[:4], refs[4:8])
    out0, out1, x0, x1, sem, sem_out = refs[-6:]
    place = Place(me_ref[0], table, share, caps)
    source = Source(place, k_ref, v_ref, sib_ref, got)
    dest = place.me ^ 1

    def one(n, counts):
        s = sel[dest * 2 * NB + n] >> 3
        e = place.entry(s, dest)
        base = (e >> 18) & 63
        group = (n >> 1) & 1

        def put(t, *src):
            @pl.when(group == 0)
            def _():
                copier(x0.at[base + t], sem)(*src)

            @pl.when(group == 1)
            def _():
                copier(x1.at[base + t], sem)(*src)

        here = source.pair(s, e, put)
        return counts[0] + jnp.where(group == 0, here, 0), counts[1] + jnp.where(group == 1, here, 0)

    count0, count1 = lax.fori_loop(0, 2 * NB, one, (0, 0))
    drain(count0 + count1, x0.at[0], sem)
    started = spill(0, count0, x0, out0, sem_out) + spill(0, count1, x1, out1, sem_out)
    drain(started, x0.at[0], sem_out)


SIZES = (2, 4, 6, 8)
SCALE = 1.0 / math.sqrt(HS) * math.log2(math.e)


def softmax_rows(q, k, bias, v, top):
    hot = (iota(q.shape, 1) == 0).astype(F32).astype(BF)
    s = lax.dot_general(
        jnp.concatenate([q, hot], axis=1), jnp.concatenate([k, bias], axis=1),
        (((1,), (1,)), ((), ())), preferred_element_type=F32,
    )
    m = jnp.max(s, axis=1, keepdims=True)
    if top is not None:
        m = jnp.maximum(m, top)
    w = jnp.exp2(s * SCALE - m * SCALE).astype(BF)
    return m, jnp.dot(w, jnp.concatenate([v, jnp.ones(v.shape, BF)], axis=1), preferred_element_type=F32)


def bias_of(dead):
    return jnp.where(jnp.logical_and(dead, iota(dead.shape, 1) == 0), -1e30, 0.0).astype(BF)


def own_kernel(pre, q_ref, k_ref, v_ref, after, acc_ref, stat_ref, bias, stat):
    count = pre[pl.program_id(0) + pre[NB]]
    bias[...] = bias_of(iota((BSZ, HS), 0) >= count)
    lane = iota((BSZ, HS), 1)
    stat[...] = jnp.zeros((BSZ, HS), F32)

    def work(keys):
        def step(it, carry):
            for side in range(2):
                h = it * 2 + side
                cols = pl.ds(pl.multiple_of(h * HS, HS), HS)
                m, a = softmax_rows(q_ref[0, :, cols], k_ref[0, :keys, cols], bias[:keys], v_ref[0, :keys, cols], None)
                acc_ref[0, :, cols] = a[:, :HS]
                stat[...] = jnp.where(lane == h, m, jnp.where(lane == h + 4, a[:, HS:], stat[...]))
            return carry

        lax.fori_loop(0, 2, step, 0)

    pl.when(count <= BSZ // 2)(functools.partial(work, BSZ // 2))
    pl.when(count > BSZ // 2)(functools.partial(work, BSZ))
    stat_ref[0] = stat[...]


def own_blocks(first, number, counts, q, k, v, after):
    width = q.shape[-1]
    block = pl.BlockSpec((1, BSZ, width), lambda i, pre: (pre[NB] + i, 0, 0))
    return pl.pallas_call(
        own_kernel,
        out_shape=(
            jax.ShapeDtypeStruct((number, BSZ, width), F32),
            jax.ShapeDtypeStruct((number, BSZ, HS), F32),
        ),
        grid_spec=pltpu.PrefetchScalarGridSpec(
            num_scalar_prefetch=1,
            grid=(number,),
            in_specs=[block] * 3 + [ANY],
            out_specs=(
                pl.BlockSpec((1, BSZ, width), lambda i, pre: (i, 0, 0)),
                pl.BlockSpec((1, BSZ, HS), lambda i, pre: (i, 0, 0)),
            ),
            scratch_shapes=[pltpu.VMEM((BSZ, HS), BF), pltpu.VMEM((BSZ, HS), F32)],
        ),
        compiler_params=pltpu.CompilerParams(vmem_limit_bytes=VLIM),
        cost_estimate=pl.CostEstimate(
            flops=number * 8 * BSZ * BSZ * width, bytes_accessed=number * BSZ * width * 10, transcendentals=0
        ),
        name="own",
    )(jnp.concatenate([counts, first]), q, k, v, after)


def attend_kernel(caps, pre, table, share, sel, q_ref, acc_ref, stat_ref, k_ref, v_ref, sib_ref, *refs):
    got = (refs[:4], refs[4:8])
    x_ref, refs = refs[8], refs[9:]
    out_ref, kb, vb, bias, sem = refs
    width = q_ref.shape[2]
    block, me = pre[0], pre[3]
    place = Place(me, table, share, caps)
    source = Source(place, k_ref, v_ref, sib_ref, got)
    plane = 1 - place.p

    live = [lax.shift_right_logical(pre[1 + i] + (R - 1), R.bit_length() - 1) for i in range(2)]
    starts = [0, live[0]]
    chunks = live[0] + live[1]
    for i in range(2):
        s = sel[(me * NB + block) * 2 + i] >> 3
        e = place.entry(s, me)
        loc = (e >> 3) & 7
        start = starts[i]

        def put(t, *src):
            row = start + 2 * t + ((place.p - loc) & 1)
            src_k, src_v = src if len(src) == 2 else (src[0].at[0], src[0].at[1])
            pltpu.make_async_copy(src_k, kb.at[row], sem).start()
            pltpu.make_async_copy(src_v, vb.at[row], sem).start()

        source.pair(s, e, put)
        other = table[plane * NSEQ + s, me]
        base = (other >> 18) & 63

        def cross(t, carry):
            row = start + 2 * t + ((plane - loc) & 1)
            pltpu.make_async_copy(x_ref.at[base + t, 0], kb.at[row], sem).start()
            pltpu.make_async_copy(x_ref.at[base + t, 1], vb.at[row], sem).start()
            return carry

        lax.fori_loop(0, other & 7, cross, 0)

    key = iota((2 * BSZ, HS), 0)
    dead = jnp.ones((2 * BSZ, HS), jnp.bool_)
    for i in range(2):
        begin = starts[i] * R
        dead = jnp.logical_and(dead, jnp.logical_or(key < begin, key >= begin + pre[1 + i]))
    bias[...] = bias_of(dead)

    for extra in range(3):

        @pl.when(chunks + extra < 2 * CH)
        def _():
            kb[chunks + extra] = jnp.zeros((R, width), BF)
            vb[chunks + extra] = jnp.zeros((R, width), BF)

    drain(2 * chunks, kb.at[0], sem)

    def work(tiles):
        keys = tiles * HS

        def step(it, carry):
            for side in range(2):
                h = it * 2 + side
                cols = pl.ds(pl.multiple_of(h * HS, HS), HS)
                lane = iota((BSZ, HS), 1)
                stat = stat_ref[0]
                own_m = jnp.sum(jnp.where(lane == h, stat, 0.0), axis=1, keepdims=True)
                own_l = jnp.sum(jnp.where(lane == h + 4, stat, 0.0), axis=1, keepdims=True)
                m, a = softmax_rows(
                    q_ref[0, :, cols],
                    kb[: tiles * 2, :, cols].reshape(keys, HS),
                    bias[:keys],
                    vb[: tiles * 2, :, cols].reshape(keys, HS),
                    own_m,
                )
                factor = jnp.exp2((own_m - m) * SCALE)
                numer = a[:, :HS] + factor * acc_ref[0, :, cols]
                out_ref[:, cols] = (numer / (a[:, HS:] + factor * own_l)).astype(BF)
            return carry

        lax.fori_loop(0, 2, step, 0)

    least = 0
    for tiles in SIZES:
        pl.when(jnp.logical_and(chunks > least, chunks <= 2 * tiles))(functools.partial(work, tiles))
        least = 2 * tiles


def attend(caps, group, pre, table, share, sel, q, own, kc, vc, sib, got, crossed):
    width = q.shape[-1]
    of_own = lambda cols: pl.BlockSpec((1, BSZ, cols), lambda i, pre: (group, 0, 0))
    return pl.pallas_call(
        functools.partial(attend_kernel, caps),
        out_shape=jax.ShapeDtypeStruct((BSZ, width), BF),
        grid_spec=pltpu.PrefetchScalarGridSpec(
            num_scalar_prefetch=1,
            grid=(1,),
            in_specs=[SMEM, SMEM, SMEM, pl.BlockSpec((1, BSZ, width), lambda i, pre: (pre[0], 0, 0))]
            + [of_own(width), of_own(HS)] + [ANY] * 12,
            out_specs=pl.BlockSpec((BSZ, width), lambda i, pre: (0, 0)),
            scratch_shapes=[
                pltpu.VMEM((2 * CH, R, width), BF),
                pltpu.VMEM((2 * CH, R, width), BF),
                pltpu.VMEM((2 * BSZ, HS), BF),
                pltpu.SemaphoreType.DMA,
            ],
        ),
        compiler_params=pltpu.CompilerParams(vmem_limit_bytes=VLIM),
        cost_estimate=pl.CostEstimate(
            flops=8 * BSZ * BSZ * width, bytes_accessed=8 * BSZ * width * 2, transcendentals=0
        ),
        name="attend",
    )(pre, table, share, sel, q, own[0], own[1], kc, vc, sib, *got, crossed)


def project_kernel(pre, a0, a1, a2, a3, w0, w1, w2, w3, *rest):
    acc = jnp.dot(a0[...], w0[0], preferred_element_type=F32)
    acc += jnp.dot(a1[...], w1[0], preferred_element_type=F32)
    acc += jnp.dot(a2[...], w2[0], preferred_element_type=F32)
    acc += jnp.dot(a3[...], w3[0], preferred_element_type=F32)
    rest[-1][...] = acc.astype(BF)


def project(head, group, parts, w_out, before):
    width = parts[0].shape[1]
    cols = w_out.shape[1]
    tile = 512
    whole = lambda a: pl.BlockSpec(a.shape, lambda n, pre: (0, 0))
    w4 = w_out.reshape(-1, width, cols)
    weight = lambda r: pl.BlockSpec((1, width, tile), lambda n, pre: ((pre[0] - r) & 3, 0, n))
    extra = [] if before is None else [before]
    return pl.pallas_call(
        project_kernel,
        out_shape=jax.ShapeDtypeStruct((2 * BSZ, cols), BF),
        grid_spec=pltpu.PrefetchScalarGridSpec(
            num_scalar_prefetch=1,
            grid=(cols // tile,),
            in_specs=[whole(a) for a in parts] + [weight(r) for r in range(4)] + [ANY] * len(extra),
            out_specs=pl.BlockSpec((BSZ, tile), lambda n, pre: (group, n)),
        ),
        input_output_aliases={9: 0} if extra else {},
        compiler_params=pltpu.CompilerParams(vmem_limit_bytes=VLIM),
        cost_estimate=pl.CostEstimate(
            flops=2 * BSZ * cols * cols, bytes_accessed=2 * cols * cols + 4 * BSZ * cols, transcendentals=0
        ),
        name="project",
    )(head, *parts, w4, w4, w4, w4, *extra)


def ring(stage, step):
    pairs = []
    for x in range(4):
        for z in range(4):
            for c in range(2):
                along_z = (c == 0) == (stage == 0)
                to = (x, (z + step) % 4) if along_z else ((x + step) % 4, z)
                pairs.append(((x * 4 + z) * 2 + c, (to[0] * 4 + to[1]) * 2 + c))
    return pairs


def copies(kernel, outs, ins, specs, hold, name, aliases=None, moved=8 * 2**20):
    return pl.pallas_call(
        kernel,
        out_shape=outs,
        in_specs=specs,
        out_specs=[ANY] * len(outs),
        scratch_shapes=[pltpu.VMEM(a.shape, a.dtype) for a in hold] + [pltpu.SemaphoreType.DMA] * 2,
        input_output_aliases=aliases or {},
        compiler_params=pltpu.CompilerParams(vmem_limit_bytes=VLIM),
        cost_estimate=pl.CostEstimate(flops=0, bytes_accessed=moved, transcendentals=0),
        name=name,
    )(*ins)


def fetch(caps, me, table, share, sel, kc, vc, sib, beside):
    width = kc.shape[-1]
    got, done, after = [], [], []
    for stage in range(2):
        sends = [jax.ShapeDtypeStruct((caps[stage], 2, R, width), BF)] * 4
        ins = [me, table, share, kc, vc, sib] + got + after
        s1p, s1m, s2p, s2m = copies(
            functools.partial(pack_kernel, stage, caps), sends, ins,
            [SMEM] * 3 + [ANY] * (len(ins) - 3), sends, "pack%d" % stage,
        )
        g1p = lax.ppermute(s1p, "seq", ring(stage, 1))
        g1m = lax.ppermute(s1m, "seq", ring(stage, -1))
        done.append(beside(2 * stage, s1p))
        s2p, s2m = copies(
            functools.partial(pass_kernel, stage, caps), sends[:2],
            [me, table, share, g1p, g1m, s2p, s2m, done[-1][0]],
            [SMEM] * 3 + [ANY] * 5, sends[:2], "pass%d" % stage, {5: 0, 6: 1},
        )
        g2p = lax.ppermute(s2p, "seq", ring(stage, 1))
        g2m = lax.ppermute(s2m, "seq", ring(stage, -1))
        done.append(beside(2 * stage + 1, s2p))
        got += [g1p, g1m, g2p, g2m]
        after = [done[-1][0]]
    x_shapes = [jax.ShapeDtypeStruct((NB * HALF, 2, R, width), BF)] * 2
    ins = [me, table, share, sel, kc, vc, sib] + got + after
    crossed = copies(
        functools.partial(cross_kernel, caps), x_shapes, ins, [SMEM] * 4 + [ANY] * (len(ins) - 4), x_shapes, "cross",
    )
    swap = [(i, i ^ 1) for i in range(NSEQ)]
    return got, [lax.ppermute(x, "seq", swap) for x in crossed], done


def before_fetch(keys, values, key_count, selected):
    width = keys.shape[1]
    me = lax.axis_index("seq").astype(I32).reshape(1)
    kc = keys.reshape(NB * CH, R, width)
    vc = values.reshape(NB * CH, R, width)
    sent = pl.pallas_call(
        split_kernel,
        out_shape=jax.ShapeDtypeStruct((NB * HALF, 2, R, width), BF),
        in_specs=[SMEM, ANY, ANY],
        out_specs=VMEM,
        scratch_shapes=[pltpu.SemaphoreType.DMA],
        compiler_params=pltpu.CompilerParams(vmem_limit_bytes=VLIM),
        cost_estimate=pl.CostEstimate(flops=0, bytes_accessed=8 * 2**20, transcendentals=0),
        name="split",
    )(me, kc, vc)
    sib = lax.ppermute(sent, "seq", [(i, i ^ 1) for i in range(NSEQ)])
    return (me, kc, vc, sib) + plan(selected, key_count)


def on_device(queries, keys, values, key_count, selected, w_out):
    width = queries.shape[1]
    me, kc, vc, sib, table, share, level = before_fetch(keys, values, key_count, selected)
    sel = selected.reshape(-1)
    head = lax.axis_index("head").astype(I32).reshape(1)
    q, k, v = [a.reshape(NB, BSZ, width) for a in (queries, keys, values)]
    own_counts = lax.dynamic_slice_in_dim(key_count, me[0] * NB, NB)
    far_counts = key_count[lax.dynamic_slice_in_dim(selected, me[0] * NB, NB)]
    pre = jnp.concatenate(
        [jnp.arange(NB, dtype=I32)[:, None], far_counts, jnp.broadcast_to(me, (NB, 1))], axis=1
    )
    order = [(g, r) for g in range(2) for r in (2, 1, 3, 0)]
    number = jnp.stack([((head[0] + r) & 3) * 2 + g for g, r in order])
    pre = jnp.take(pre, number, axis=0)
    up = [(i, (i + 1) % 4) for i in range(4)]
    down = [(i, (i - 1) % 4) for i in range(4)]

    def rest(caps, sib, table, share, pre, own_counts):
        def beside(r, after):
            return own_blocks(((head + r) & 3) * 2, 2, own_counts, q, k, v, after)

        got, crossed, own = fetch(caps, me, table, share, sel, kc, vc, sib, beside)
        out = None
        for g in range(2):
            parts = {}
            for index, (group, r) in enumerate(order):
                if group == g:
                    parts[r] = attend(
                        caps, g, pre[index], table, share, sel, q, own[r], kc, vc, sib, got, crossed[g]
                    )
            way = up if g == 0 else down
            two = lax.ppermute(lax.ppermute(parts[2], "head", way), "head", way)
            one = lax.ppermute(parts[1], "head", up)
            three = lax.ppermute(parts[3], "head", down)
            out = project(head, g, [parts[0], one, two, three], w_out, out)
        return out

    return lax.switch(
        level, [functools.partial(rest, caps) for caps in LEVELS], sib, table, share, pre, own_counts
    )


def solution(mesh):
    placed = (P("seq", "head"), P("seq", "head"), P("seq", "head"), P(), P(), P())
    return jax.shard_map(
        on_device, mesh=mesh, in_specs=placed, out_specs=P(("seq", "head"), None), check_vma=False
    )
```

```python
import functools
import math

import jax
import jax.numpy as jnp
from jax import lax
from jax.experimental import pallas as pl
from jax.experimental.pallas import tpu as pltpu
from jax.sharding import PartitionSpec as P

HS = 128
BSZ = 512
R = 64
CH = BSZ // R
HALF = CH // 2
NB = 8
NSEQ = 32
LEVELS = ((21, 24), (22, 25), (23, 27), (26, 30), (64, 64))
VLIM = 60 * 2**20
ROW = 128
F32 = jnp.float32
I32 = jnp.int32
BF = jnp.bfloat16
ANY = pl.BlockSpec(memory_space=pl.ANY)
SMEM = pl.BlockSpec(memory_space=pltpu.SMEM)
VMEM = pl.BlockSpec(memory_space=pltpu.VMEM)


def mm(a, b):
    return jnp.dot(a.astype(BF), b.astype(BF), preferred_element_type=F32)


def uv_of(index, plane):
    x = lax.shift_right_logical(index, 3) & 3
    z = lax.shift_right_logical(index, 1) & 3
    return (z, x) if plane == 0 else (x, z)


def iota(shape, dim):
    return lax.broadcasted_iota(I32, shape, dim)


def plan_kernel(sel_ref, cnt_ref, table_ref):
    s = iota((NSEQ, ROW), 0)
    d = iota((NSEQ, ROW), 1)
    loc = jnp.full((NSEQ, ROW), -1, I32)
    grp = jnp.zeros((NSEQ, ROW), I32)
    for n in range(2 * NB):
        row = sel_ref[n : n + 1, :]
        hit = lax.shift_right_arithmetic(row, 3) == s
        loc = jnp.where(hit, row & 7, loc)
        grp = jnp.where(hit, (n >> 1) & 1, grp)
    count = jnp.zeros((NSEQ, ROW), I32)
    for j in range(NB):
        count = jnp.where(loc == j, cnt_ref[:, j : j + 1], count)
    total = lax.shift_right_logical(count + (R - 1), R.bit_length() - 1)

    i32, j32 = iota((NSEQ, NSEQ), 0), iota((NSEQ, NSEQ), 1)
    i128, j128 = iota((ROW, ROW), 0), iota((ROW, ROW), 1)
    chip_l = ((i32 >> 1) == (j32 >> 1)).astype(F32)
    chip_r = ((i128 >> 1) == (j128 >> 1)).astype(F32)
    odd_l = jnp.logical_and(j32 == i32 - 1, (i32 & 1) == 1).astype(F32)
    odd_r = jnp.logical_and(i128 == j128 - 1, (j128 & 1) == 1).astype(F32)
    lower = (j32 < i32).astype(F32)
    for plane in range(2):
        first = (plane - loc) & 1
        n_of = jnp.where(loc >= 0, lax.shift_right_logical(total - first + 1, 1), 0)
        n_f = n_of.astype(F32)
        u_i, v_i = uv_of(i128, plane)
        u_j, v_j = uv_of(j128, plane)
        same_u = u_i == u_j
        m1 = jnp.logical_and(same_u, (v_i * 2 + (i128 & 1)) < (v_j * 2 + (j128 & 1))).astype(F32)
        same_u = same_u.astype(F32)
        dup = jnp.zeros((NSEQ, ROW), jnp.bool_)
        for j in range(NB):
            is_j = loc == j
            dup = jnp.logical_or(dup, jnp.logical_and(is_j, mm(is_j.astype(F32), m1) > 0.5))
        n1 = jnp.where(dup, 0.0, n_f)
        a_n = mm(chip_l, n1)
        pos1 = mm(a_n, m1) + mm(odd_l, n1)
        of_first = jnp.zeros((NSEQ, ROW), F32)
        for j in range(NB):
            is_j = loc == j
            there = mm(jnp.where(jnp.logical_and(is_j, jnp.logical_not(dup)), pos1, 0.0), same_u)
            of_first = jnp.where(is_j, there, of_first)
        pos1 = jnp.where(dup, of_first, pos1)
        u_s, v_s = uv_of(i32, plane)
        u_t, v_t = uv_of(j32, plane)
        same_v = v_s == v_t
        m2 = jnp.logical_and(same_v, (u_t * 2 + (j32 & 1)) < (u_s * 2 + (i32 & 1))).astype(F32)
        pos2 = mm(m2, mm(n_f, chip_r)) + mm(n_f, odd_r)
        pos3 = jnp.where(
            grp == 0,
            mm(lower, jnp.where(grp == 0, n_f, 0.0)),
            mm(lower, jnp.where(grp == 1, n_f, 0.0)),
        )
        entry = n_of | (jnp.maximum(loc, 0) << 3)
        for index, place in enumerate((pos1, pos2, pos3)):
            entry = entry | (place.astype(I32) << (6 + 6 * index))
        entry = entry | (dup.astype(I32) << 24)

        to_u = jnp.logical_and(i128 < NSEQ, j128 - NSEQ == u_i).astype(F32)
        to_v = jnp.logical_and(i128 < NSEQ, j128 - NSEQ - 4 == v_i).astype(F32)
        u_a, _ = uv_of(s, plane)
        u_b, _ = uv_of(d, plane)
        line = jnp.where(u_a == u_b, mm(same_v.astype(F32), n_f), 0.0)
        lengths = mm(a_n, to_u) + mm(line, to_v)
        table_ref[plane * NSEQ : (plane + 1) * NSEQ, :] = jnp.where(d < NSEQ, entry, lengths.astype(I32))


def balance_kernel(table, share_ref, level_ref):
    def one(ring_number, need):
        plane, stage, g = ring_number >> 3, (ring_number >> 2) & 1, ring_number & 3
        by_x = plane == stage
        rows = [
            plane * NSEQ + jnp.where(by_x, g * 4 + a, a * 4 + g) * 2 for a in range(4)
        ]
        far = NSEQ + stage * 4
        l1, l2, l3 = [[table[rows[a], far + ((a + r) & 3)] for a in range(4)] for r in (1, 2, 3)]
        h = [(n + 1) >> 1 for n in l2]

        def loads():
            plus = [l1[a] + h[a] + h[(a - 1) & 3] for a in range(4)]
            minus = [l3[a] + l2[a] - h[a] + l2[(a + 1) & 3] - h[(a + 1) & 3] for a in range(4)]
            return plus, minus

        for a in range(4):
            plus, minus = loads()
            high = jnp.maximum(plus[a], plus[(a + 1) & 3]) - h[a]
            low = jnp.maximum(minus[a], minus[(a - 1) & 3]) - (l2[a] - h[a])
            h[a] = jnp.clip((low + l2[a] - high + 1) >> 1, 0, l2[a])
        plus, minus = loads()
        most = functools.reduce(jnp.maximum, plus + minus)
        least = functools.reduce(jnp.maximum, h + [l2[a] - h[a] for a in range(4)])
        for a in range(4):
            share_ref[ring_number * 4 + a] = h[a]
        here = jnp.maximum((most + 1) >> 1, least)
        return (
            jnp.where(stage == 0, jnp.maximum(need[0], here), need[0]),
            jnp.where(stage == 1, jnp.maximum(need[1], here), need[1]),
        )

    need = lax.fori_loop(0, 16, one, (jnp.int32(0), jnp.int32(0)))
    level = jnp.int32(0)
    for cap in LEVELS[:-1]:
        level += jnp.logical_or(need[0] > cap[0], need[1] > cap[1]).astype(I32)
    level_ref[0] = level


def plan(selected, key_count):
    by_dest = jnp.pad(
        selected.reshape(NSEQ, 2 * NB).T, ((0, 0), (0, ROW - NSEQ)), constant_values=-1
    )
    table = pl.pallas_call(
        plan_kernel,
        out_shape=jax.ShapeDtypeStruct((2 * NSEQ, ROW), I32),
        in_specs=[VMEM, VMEM],
        out_specs=VMEM,
        compiler_params=pltpu.CompilerParams(vmem_limit_bytes=VLIM),
        name="plan",
    )(by_dest, key_count.reshape(NSEQ, NB))
    share, level = pl.pallas_call(
        balance_kernel,
        out_shape=(jax.ShapeDtypeStruct((64,), I32), jax.ShapeDtypeStruct((1,), I32)),
        in_specs=[SMEM],
        out_specs=(SMEM, SMEM),
        compiler_params=pltpu.CompilerParams(vmem_limit_bytes=VLIM),
        name="balance",
    )(table)
    return table, share, level[0]


def both_start(src_k, src_v, dst, sem):
    pltpu.make_async_copy(src_k, dst.at[0], sem).start()
    pltpu.make_async_copy(src_v, dst.at[1], sem).start()


def drain(count, like, sem):
    def one(_, carry):
        pltpu.make_async_copy(like, like, sem).wait()
        return carry

    lax.fori_loop(0, count, one, 0)


def spill(low, high, src, dst, sem):
    def one(row, carry):
        pltpu.make_async_copy(src.at[row], dst.at[row], sem).start()
        return carry

    lax.fori_loop(low, high, one, 0)
    return jnp.maximum(high - low, 0)


def split_kernel(me_ref, k_ref, v_ref, out_ref, sem):
    other = 1 - (me_ref[0] & 1)

    def one(index, carry):
        block = index // HALF
        chunk = block * CH + 2 * (index % HALF) + ((other - block) & 1)
        both_start(k_ref.at[chunk], v_ref.at[chunk], out_ref.at[index], sem)
        return carry

    lax.fori_loop(0, NB * HALF, one, 0)
    pltpu.make_async_copy(out_ref, out_ref, sem).wait()


class Place:
    def __init__(self, me, table, share, caps):
        self.me, self.table, self.share, self.caps = me, table, share, caps
        self.p = me & 1
        x, z = (me >> 3) & 3, (me >> 1) & 3
        self.u0 = jnp.where(self.p == 0, z, x)
        self.v0 = jnp.where(self.p == 0, x, z)

    def index(self, u, v, c):
        x = jnp.where(self.p == 0, v, u)
        z = jnp.where(self.p == 0, u, v)
        return (x * 4 + z) * 2 + c

    def entry(self, s, d):
        return self.table[self.p * NSEQ + s, d]

    def length(self, stage, a, b):
        a, b = a & 3, b & 3
        node = self.index(a, self.v0, 0) if stage == 0 else self.index(self.u0, a, 0)
        return self.table[self.p * NSEQ + node, NSEQ + 4 * stage + b]

    def halves(self, stage, a):
        a = a & 3
        ring_of = self.v0 if stage == 0 else self.u0
        h = self.share[((self.p * 2 + stage) * 4 + ring_of) * 4 + a]
        return h, self.length(stage, a, a + 2) - h

    def here(self, stage):
        return self.u0 if stage == 0 else self.v0


def chunk_of(loc, t, plane):
    return loc * CH + 2 * t + ((plane - loc) & 1)


class Source:
    def __init__(self, place, k_ref, v_ref, sib_ref, got):
        self.place, self.k, self.v, self.sib, self.got = place, k_ref, v_ref, sib_ref, got
        self.info = []
        for stage in range(len(got)):
            b = place.here(stage)
            far_p, far_m = place.halves(stage, b + 2)
            near_p, _ = place.halves(stage, b - 1)
            _, near_m = place.halves(stage, b + 1)
            self.info.append((far_p, far_m, near_p, near_m))

    def chunk(self, stage, a, q, t, loc, own, put):
        place = self.place
        if stage < 0:

            @pl.when(own)
            def _():
                c = chunk_of(loc, t, place.p)
                put(self.k.at[c], self.v.at[c])

            @pl.when(jnp.logical_not(own))
            def _():
                put(self.sib.at[loc * HALF + t])

            return
        g1p, g1m, g2p, g2m = self.got[stage]
        far_p, far_m, near_p, near_m = self.info[stage]
        cap = place.caps[stage]
        r = (place.here(stage) - a) & 3
        plus = jnp.logical_or(r == 1, jnp.logical_and(r == 2, q < far_p))
        near = jnp.where(r == 1, near_p, near_m)
        far = jnp.where(r == 1, far_p, far_m)
        first = jnp.logical_and(r != 2, q < cap - near)
        row = jnp.where(
            r == 2,
            jnp.where(plus, q, q - far_p),
            jnp.where(first, near + q, far + q - (cap - near)),
        )
        for is_plus, is_first, ref in (
            (True, True, g1p), (False, True, g1m), (True, False, g2p), (False, False, g2m),
        ):
            cond = jnp.logical_and(plus == is_plus, first == is_first)

            @pl.when(cond)
            def _(ref=ref):
                put(ref.at[row])

    def pair(self, s, e, put):
        place = self.place
        n, loc = e & 7, (e >> 3) & 7
        c = s & 1
        x, z = (s >> 3) & 3, (s >> 1) & 3
        u = jnp.where(place.p == 0, z, x)
        v = jnp.where(place.p == 0, x, z)
        own = c == place.p
        mine = u == place.u0
        last = len(self.got) - 1

        def loop(stage, a, base):
            def one(t, carry):
                self.chunk(stage, a, base + t, t, loc, own, functools.partial(put, t))
                return carry

            lax.fori_loop(0, n, one, 0)

        def early():
            if last < 0:
                loop(-1, 0, 0)
                return

            @pl.when(mine)
            def _():
                loop(-1, 0, 0)

            @pl.when(jnp.logical_not(mine))
            def _():
                loop(0, u, (e >> 6) & 63)

        if last < 1:
            early()
        else:
            same_v = v == place.v0

            @pl.when(same_v)
            def _():
                early()

            @pl.when(jnp.logical_not(same_v))
            def _():
                loop(1, v, (e >> 12) & 63)
        return n


def copier(dst, sem):
    def put(*src):
        if len(src) == 2:
            both_start(src[0], src[1], dst, sem)
        else:
            pltpu.make_async_copy(src[0], dst, sem).start()

    return put


def pack_kernel(stage, part, caps, me_ref, table, share, k_ref, v_ref, sib_ref, *refs):
    got = (refs[:4],) if stage else ()
    out_p, out_m, hold_p, hold_m, sem, sem_out = refs[len(refs) - 6 :]
    place = Place(me_ref[0], table, share, caps)
    source = Source(place, k_ref, v_ref, sib_ref, got)
    b = place.here(stage)
    cap = caps[stage]
    half_p, half_m = place.halves(stage, b)
    pass_p, _ = place.halves(stage, b - 1)
    _, pass_m = place.halves(stage, b + 1)
    shift = 6 if stage == 0 else 12
    started = 0
    for r in (2, 1, 3) if part == 0 else (1, 3):
        to = (b + r) & 3

        def one(i, count, r=r, to=to):
            if stage == 0:
                s = place.index(place.u0, place.v0, i & 1)
                d = place.index(to, i >> 2, (i >> 1) & 1)
            else:
                s = place.index(i >> 2, place.v0, (i >> 1) & 1)
                d = place.index(place.u0, to, i & 1)
            e = place.entry(s, d)
            base = (e >> shift) & 63
            if stage == 0:
                e = jnp.where((e >> 24) & 1 == 1, 0, e)

            if r == 2:
                rows = ((hold_p, 0, half_p, 0), (hold_m, half_p, 1 << 20, -half_p))
            else:
                hold, half, passed = (hold_p, half_p, pass_p) if r == 1 else (hold_m, half_m, pass_m)
                fits = cap - half
                rows = ((hold, 0, fits, half),) if part == 0 else ((hold, fits, 1 << 20, passed - fits),)

            def put(t, *src):
                q = base + t
                for hold, low, high, move in rows:

                    @pl.when(jnp.logical_and(q >= low, q < high))
                    def _(hold=hold, move=move):
                        copier(hold.at[q + move], sem)(*src)

            source.pair(s, e, put)
            n = e & 7
            return count + sum(
                jnp.maximum(jnp.minimum(base + n, high) - jnp.maximum(base, low), 0) for _, low, high, _ in rows
            )

        started = lax.fori_loop(0, 16, one, started)
    drain(started, hold_p.at[0], sem)
    started = 0
    for half, passed, n, hold, out in (
        (half_p, pass_p, place.length(stage, b, b + 1), hold_p, out_p),
        (half_m, pass_m, place.length(stage, b, b - 1), hold_m, out_m),
    ):
        fits = jnp.minimum(n, cap - half)
        if part == 0:
            started += spill(0, half + fits, hold, out, sem_out)
        else:
            started += spill(passed, passed + n - fits, hold, out, sem_out)
    drain(started, hold_p.at[0], sem_out)


def pass_kernel(stage, caps, me_ref, table, share, g1p, g1m, in_p, in_m, after, s2p, s2m, hold_p, hold_m, sem, sem_out):
    place = Place(me_ref[0], table, share, caps)
    b = place.here(stage)
    pass_p, _ = place.halves(stage, b - 1)
    _, pass_m = place.halves(stage, b + 1)
    started = spill(0, pass_p, g1p, hold_p, sem) + spill(0, pass_m, g1m, hold_m, sem)
    drain(started, hold_p.at[0], sem)
    started = spill(0, pass_p, hold_p, s2p, sem_out) + spill(0, pass_m, hold_m, s2m, sem_out)
    drain(started, hold_p.at[0], sem_out)


def cross_kernel(caps, me_ref, table, share, sel, k_ref, v_ref, sib_ref, *refs):
    got = (refs[:4], refs[4:8])
    out0, out1, x0, x1, sem, sem_out = refs[-6:]
    place = Place(me_ref[0], table, share, caps)
    source = Source(place, k_ref, v_ref, sib_ref, got)
    dest = place.me ^ 1

    def one(n, counts):
        s = sel[dest * 2 * NB + n] >> 3
        e = place.entry(s, dest)
        base = (e >> 18) & 63
        group = (n >> 1) & 1

        def put(t, *src):
            @pl.when(group == 0)
            def _():
                copier(x0.at[base + t], sem)(*src)

            @pl.when(group == 1)
            def _():
                copier(x1.at[base + t], sem)(*src)

        here = source.pair(s, e, put)
        return counts[0] + jnp.where(group == 0, here, 0), counts[1] + jnp.where(group == 1, here, 0)

    count0, count1 = lax.fori_loop(0, 2 * NB, one, (0, 0))
    drain(count0 + count1, x0.at[0], sem)
    started = spill(0, count0, x0, out0, sem_out) + spill(0, count1, x1, out1, sem_out)
    drain(started, x0.at[0], sem_out)


SIZES = (2, 4, 6, 8)
SCALE = 1.0 / math.sqrt(HS)


def heads_pipeline(keys, heads, q_of, k_of, v_of, bias, top_of, finish, scores, weights):
    tops = {}
    for i in range(heads + 2):
        if i < heads:
            q = q_of(i)
            hot = (iota(q.shape, 1) == 0).astype(F32).astype(BF)
            s = lax.dot_general(
                jnp.concatenate([q, hot], axis=1), jnp.concatenate([k_of(i), bias[:keys]], axis=1),
                (((1,), (1,)), ((), ())), preferred_element_type=F32,
            )
            scores[i % 2][:, :keys] = s
            tops[i] = jnp.max(s, axis=1, keepdims=True)
            top = top_of(i)
            if top is not None:
                tops[i] = jnp.maximum(tops[i], top)
        if 0 <= i - 1 < heads:
            h = i - 1
            w = jnp.exp(scores[h % 2][:, :keys] * SCALE - tops[h] * SCALE)
            weights[h % 2][:, :keys] = w.astype(BF)
        if i - 2 >= 0:
            h = i - 2
            v = v_of(h)
            a = jnp.dot(
                weights[h % 2][:, :keys], jnp.concatenate([v, jnp.ones(v.shape, BF)], axis=1),
                preferred_element_type=F32,
            )
            finish(h, tops.pop(h), a)


def bias_of(dead):
    return jnp.where(jnp.logical_and(dead, iota(dead.shape, 1) == 0), -1e30, 0.0).astype(BF)


def own_kernel(pre, q_ref, k_ref, v_ref, after, acc_ref, stat_ref, bias, s0, s1, w0, w1):
    count = pre[pl.program_id(0) + pre[NB]]
    bias[...] = bias_of(iota((BSZ, HS), 0) >= count)
    lane = iota((BSZ, HS), 1)

    def work(keys):
        def finish(h, m, a):
            acc_ref[0, :, h * HS : (h + 1) * HS] = a[:, :HS]
            before = stat_ref[0] if h else jnp.zeros((BSZ, HS), F32)
            stat_ref[0] = jnp.where(lane == h, m, jnp.where(lane == h + 4, a[:, HS:], before))

        cols = lambda ref, rows: lambda h: ref[0, :rows, h * HS : (h + 1) * HS]
        heads_pipeline(
            keys, q_ref.shape[2] // HS, cols(q_ref, BSZ), cols(k_ref, keys), cols(v_ref, keys), bias,
            lambda h: None, finish, (s0, s1), (w0, w1),
        )

    pl.when(count <= BSZ // 2)(functools.partial(work, BSZ // 2))
    pl.when(count > BSZ // 2)(functools.partial(work, BSZ))


def own_blocks(first, number, counts, q, k, v, after):
    width = q.shape[-1]
    block = pl.BlockSpec((1, BSZ, width), lambda i, pre: (pre[NB] + i, 0, 0))
    return pl.pallas_call(
        own_kernel,
        out_shape=(
            jax.ShapeDtypeStruct((number, BSZ, width), F32),
            jax.ShapeDtypeStruct((number, BSZ, HS), F32),
        ),
        grid_spec=pltpu.PrefetchScalarGridSpec(
            num_scalar_prefetch=1,
            grid=(number,),
            in_specs=[block] * 3 + [ANY],
            out_specs=(
                pl.BlockSpec((1, BSZ, width), lambda i, pre: (i, 0, 0)),
                pl.BlockSpec((1, BSZ, HS), lambda i, pre: (i, 0, 0)),
            ),
            scratch_shapes=[pltpu.VMEM((BSZ, HS), BF)]
            + [pltpu.VMEM((BSZ, BSZ), F32)] * 2 + [pltpu.VMEM((BSZ, BSZ), BF)] * 2,
        ),
        compiler_params=pltpu.CompilerParams(vmem_limit_bytes=VLIM),
        cost_estimate=pl.CostEstimate(
            flops=number * 8 * BSZ * BSZ * width, bytes_accessed=number * BSZ * width * 10, transcendentals=0
        ),
        name="own",
    )(jnp.concatenate([counts, first]), q, k, v, after)


def attend_kernel(caps, pre, table, share, sel, q_ref, acc_ref, stat_ref, k_ref, v_ref, sib_ref, *refs):
    got = (refs[:4], refs[4:8])
    x_ref, refs = refs[8], refs[9:]
    out_ref, kb, vb, bias, s0, s1, w0, w1, sem = refs
    width = q_ref.shape[2]
    block, me = pre[0], pre[3]
    place = Place(me, table, share, caps)
    source = Source(place, k_ref, v_ref, sib_ref, got)
    plane = 1 - place.p

    live = [lax.shift_right_logical(pre[1 + i] + (R - 1), R.bit_length() - 1) for i in range(2)]
    starts = [0, live[0]]
    chunks = live[0] + live[1]
    for i in range(2):
        s = sel[(me * NB + block) * 2 + i] >> 3
        e = place.entry(s, me)
        loc = (e >> 3) & 7
        start = starts[i]

        def put(t, *src):
            row = start + 2 * t + ((place.p - loc) & 1)
            src_k, src_v = src if len(src) == 2 else (src[0].at[0], src[0].at[1])
            pltpu.make_async_copy(src_k, kb.at[row], sem).start()
            pltpu.make_async_copy(src_v, vb.at[row], sem).start()

        source.pair(s, e, put)
        other = table[plane * NSEQ + s, me]
        base = (other >> 18) & 63

        def cross(t, carry):
            row = start + 2 * t + ((plane - loc) & 1)
            pltpu.make_async_copy(x_ref.at[base + t, 0], kb.at[row], sem).start()
            pltpu.make_async_copy(x_ref.at[base + t, 1], vb.at[row], sem).start()
            return carry

        lax.fori_loop(0, other & 7, cross, 0)

    key = iota((2 * BSZ, HS), 0)
    dead = jnp.ones((2 * BSZ, HS), jnp.bool_)
    for i in range(2):
        begin = starts[i] * R
        dead = jnp.logical_and(dead, jnp.logical_or(key < begin, key >= begin + pre[1 + i]))
    bias[...] = bias_of(dead)

    for extra in range(3):

        @pl.when(chunks + extra < 2 * CH)
        def _():
            kb[chunks + extra] = jnp.zeros((R, width), BF)
            vb[chunks + extra] = jnp.zeros((R, width), BF)

    drain(2 * chunks, kb.at[0], sem)

    def work(tiles):
        keys = tiles * HS
        column = lambda i: jnp.sum(jnp.where(iota((BSZ, HS), 1) == i, stat_ref[0], 0.0), axis=1, keepdims=True)
        part = lambda h: slice(h * HS, (h + 1) * HS)
        own_m = {}

        def top_of(h):
            own_m[h] = column(h)
            return own_m[h]

        def finish(h, m, a):
            factor = jnp.exp((own_m[h] - m) * SCALE)
            numer = a[:, :HS] + factor * acc_ref[0, :, part(h)]
            out_ref[:, part(h)] = (numer / (a[:, HS:] + factor * column(h + 4))).astype(BF)

        heads_pipeline(
            keys, width // HS,
            lambda h: q_ref[0, :, part(h)],
            lambda h: kb[: tiles * 2, :, part(h)].reshape(keys, HS),
            lambda h: vb[: tiles * 2, :, part(h)].reshape(keys, HS),
            bias, top_of, finish, (s0, s1), (w0, w1),
        )

    least = 0
    for tiles in SIZES:
        pl.when(jnp.logical_and(chunks > least, chunks <= 2 * tiles))(functools.partial(work, tiles))
        least = 2 * tiles


def attend(caps, group, pre, table, share, sel, q, own, kc, vc, sib, got, crossed):
    width = q.shape[-1]
    of_own = lambda cols: pl.BlockSpec((1, BSZ, cols), lambda i, pre: (group, 0, 0))
    return pl.pallas_call(
        functools.partial(attend_kernel, caps),
        out_shape=jax.ShapeDtypeStruct((BSZ, width), BF),
        grid_spec=pltpu.PrefetchScalarGridSpec(
            num_scalar_prefetch=1,
            grid=(1,),
            in_specs=[SMEM, SMEM, SMEM, pl.BlockSpec((1, BSZ, width), lambda i, pre: (pre[0], 0, 0))]
            + [of_own(width), of_own(HS)] + [ANY] * 12,
            out_specs=pl.BlockSpec((BSZ, width), lambda i, pre: (0, 0)),
            scratch_shapes=[
                pltpu.VMEM((2 * CH, R, width), BF),
                pltpu.VMEM((2 * CH, R, width), BF),
                pltpu.VMEM((2 * BSZ, HS), BF),
                pltpu.VMEM((BSZ, 2 * BSZ), F32),
                pltpu.VMEM((BSZ, 2 * BSZ), F32),
                pltpu.VMEM((BSZ, 2 * BSZ), BF),
                pltpu.VMEM((BSZ, 2 * BSZ), BF),
                pltpu.SemaphoreType.DMA,
            ],
        ),
        compiler_params=pltpu.CompilerParams(vmem_limit_bytes=VLIM),
        cost_estimate=pl.CostEstimate(
            flops=8 * BSZ * BSZ * width, bytes_accessed=8 * BSZ * width * 2, transcendentals=0
        ),
        name="attend",
    )(pre, table, share, sel, q, own[0], own[1], kc, vc, sib, *got, crossed)


def project_kernel(pre, a0, a1, a2, a3, w_ref, *rest):
    o_ref, rows = rest[-2:]
    width = a0.shape[1]

    @pl.when(pl.program_id(0) == 0)
    def _():
        for r, part in enumerate((a0, a1, a2, a3)):
            head = (pre[0] - r) & 3
            rows[:, pl.ds(pl.multiple_of(head * width, width), width)] = part[...]

    o_ref[...] = jnp.dot(rows[...], w_ref[...], preferred_element_type=F32).astype(BF)


def project(head, group, parts, w_out, before):
    cols = w_out.shape[1]
    tile = 512
    whole = lambda a: pl.BlockSpec(a.shape, lambda n, pre: (0, 0))
    extra = [] if before is None else [before]
    return pl.pallas_call(
        project_kernel,
        out_shape=jax.ShapeDtypeStruct((2 * BSZ, cols), BF),
        grid_spec=pltpu.PrefetchScalarGridSpec(
            num_scalar_prefetch=1,
            grid=(cols // tile,),
            in_specs=[whole(a) for a in parts]
            + [pl.BlockSpec((w_out.shape[0], tile), lambda n, pre: (0, n))] + [ANY] * len(extra),
            out_specs=pl.BlockSpec((BSZ, tile), lambda n, pre: (group, n)),
            scratch_shapes=[pltpu.VMEM((BSZ, w_out.shape[0]), BF)],
        ),
        input_output_aliases={6: 0} if extra else {},
        compiler_params=pltpu.CompilerParams(vmem_limit_bytes=VLIM),
        cost_estimate=pl.CostEstimate(
            flops=2 * BSZ * cols * cols, bytes_accessed=2 * cols * cols + 4 * BSZ * cols, transcendentals=0
        ),
        name="project",
    )(head, *parts, w_out, *extra)


def ring(stage, step):
    pairs = []
    for x in range(4):
        for z in range(4):
            for c in range(2):
                along_z = (c == 0) == (stage == 0)
                to = (x, (z + step) % 4) if along_z else ((x + step) % 4, z)
                pairs.append(((x * 4 + z) * 2 + c, (to[0] * 4 + to[1]) * 2 + c))
    return pairs


def copies(kernel, outs, ins, specs, hold, name, aliases=None, moved=8 * 2**20):
    return pl.pallas_call(
        kernel,
        out_shape=outs,
        in_specs=specs,
        out_specs=[ANY] * len(outs),
        scratch_shapes=[pltpu.VMEM(a.shape, a.dtype) for a in hold] + [pltpu.SemaphoreType.DMA] * 2,
        input_output_aliases=aliases or {},
        compiler_params=pltpu.CompilerParams(vmem_limit_bytes=VLIM),
        cost_estimate=pl.CostEstimate(flops=0, bytes_accessed=moved, transcendentals=0),
        name=name,
    )(*ins)


def fetch(caps, me, table, share, sel, kc, vc, sib, beside):
    width = kc.shape[-1]
    got, done, after = [], [], []
    for stage in range(2):
        sends = [jax.ShapeDtypeStruct((caps[stage], 2, R, width), BF)] * 2
        ins = [me, table, share, kc, vc, sib] + got + after
        s1p, s1m = copies(
            functools.partial(pack_kernel, stage, 0, caps), sends, ins,
            [SMEM] * 3 + [ANY] * (len(ins) - 3), sends, "pack%d" % stage,
        )
        g1p = lax.ppermute(s1p, "seq", ring(stage, 1))
        g1m = lax.ppermute(s1m, "seq", ring(stage, -1))
        done.append(beside(2 * stage, s1p))
        ins = [me, table, share, kc, vc, sib] + got + [done[-1][0]]
        s2p, s2m = copies(
            functools.partial(pack_kernel, stage, 1, caps), sends, ins,
            [SMEM] * 3 + [ANY] * (len(ins) - 3), sends, "rest%d" % stage,
        )
        s2p, s2m = copies(
            functools.partial(pass_kernel, stage, caps), sends,
            [me, table, share, g1p, g1m, s2p, s2m, done[-1][0]],
            [SMEM] * 3 + [ANY] * 5, sends, "pass%d" % stage, {5: 0, 6: 1},
        )
        g2p = lax.ppermute(s2p, "seq", ring(stage, 1))
        g2m = lax.ppermute(s2m, "seq", ring(stage, -1))
        done.append(beside(2 * stage + 1, s2p))
        got += [g1p, g1m, g2p, g2m]
        after = [done[-1][0]]
    x_shapes = [jax.ShapeDtypeStruct((NB * HALF, 2, R, width), BF)] * 2
    ins = [me, table, share, sel, kc, vc, sib] + got + after
    crossed = copies(
        functools.partial(cross_kernel, caps), x_shapes, ins, [SMEM] * 4 + [ANY] * (len(ins) - 4), x_shapes, "cross",
    )
    swap = [(i, i ^ 1) for i in range(NSEQ)]
    return got, [lax.ppermute(x, "seq", swap) for x in crossed], done


def before_fetch(keys, values, key_count, selected):
    width = keys.shape[1]
    me = lax.axis_index("seq").astype(I32).reshape(1)
    kc = keys.reshape(NB * CH, R, width)
    vc = values.reshape(NB * CH, R, width)
    sent = pl.pallas_call(
        split_kernel,
        out_shape=jax.ShapeDtypeStruct((NB * HALF, 2, R, width), BF),
        in_specs=[SMEM, ANY, ANY],
        out_specs=VMEM,
        scratch_shapes=[pltpu.SemaphoreType.DMA],
        compiler_params=pltpu.CompilerParams(vmem_limit_bytes=VLIM),
        cost_estimate=pl.CostEstimate(flops=0, bytes_accessed=8 * 2**20, transcendentals=0),
        name="split",
    )(me, kc, vc)
    sib = lax.ppermute(sent, "seq", [(i, i ^ 1) for i in range(NSEQ)])
    return (me, kc, vc, sib) + plan(selected, key_count)


def on_device(queries, keys, values, key_count, selected, w_out):
    width = queries.shape[1]
    me, kc, vc, sib, table, share, level = before_fetch(keys, values, key_count, selected)
    sel = selected.reshape(-1)
    head = lax.axis_index("head").astype(I32).reshape(1)
    q, k, v = [a.reshape(NB, BSZ, width) for a in (queries, keys, values)]
    own_counts = lax.dynamic_slice_in_dim(key_count, me[0] * NB, NB)
    far_counts = key_count[lax.dynamic_slice_in_dim(selected, me[0] * NB, NB)]
    pre = jnp.concatenate(
        [jnp.arange(NB, dtype=I32)[:, None], far_counts, jnp.broadcast_to(me, (NB, 1))], axis=1
    )
    order = [(g, r) for g in range(2) for r in (2, 1, 3, 0)]
    number = jnp.stack([((head[0] + r) & 3) * 2 + g for g, r in order])
    pre = jnp.take(pre, number, axis=0)
    up = [(i, (i + 1) % 4) for i in range(4)]
    down = [(i, (i - 1) % 4) for i in range(4)]

    def rest(caps, sib, table, share, pre, own_counts):
        def beside(r, after):
            return own_blocks(((head + r) & 3) * 2, 2, own_counts, q, k, v, after)

        got, crossed, own = fetch(caps, me, table, share, sel, kc, vc, sib, beside)
        out = None
        for g in range(2):
            parts = {}
            for index, (group, r) in enumerate(order):
                if group == g:
                    parts[r] = attend(
                        caps, g, pre[index], table, share, sel, q, own[r], kc, vc, sib, got, crossed[g]
                    )
            way = up if g == 0 else down
            two = lax.ppermute(lax.ppermute(parts[2], "head", way), "head", way)
            one = lax.ppermute(parts[1], "head", up)
            three = lax.ppermute(parts[3], "head", down)
            out = project(head, g, [parts[0], one, two, three], w_out, out)
        return out

    return lax.switch(
        level, [functools.partial(rest, caps) for caps in LEVELS], sib, table, share, pre, own_counts
    )


def solution(mesh):
    placed = (P("seq", "head"), P("seq", "head"), P("seq", "head"), P(), P(), P())
    return jax.shard_map(
        on_device, mesh=mesh, in_specs=placed, out_specs=P(("seq", "head"), None), check_vma=False
    )
```

```python
import functools
import math

import jax
import jax.numpy as jnp
from jax import lax
from jax.experimental import pallas as pl
from jax.experimental.pallas import tpu as pltpu
from jax.sharding import PartitionSpec as P

HS = 128
BSZ = 512
R = 64
CH = BSZ // R
HALF = CH // 2
NB = 8
NSEQ = 32
LEVELS = ((21, 24), (22, 25), (23, 27), (26, 30), (64, 64))
VLIM = 60 * 2**20
ROW = 128
F32 = jnp.float32
I32 = jnp.int32
BF = jnp.bfloat16
ANY = pl.BlockSpec(memory_space=pl.ANY)
SMEM = pl.BlockSpec(memory_space=pltpu.SMEM)
VMEM = pl.BlockSpec(memory_space=pltpu.VMEM)


def mm(a, b):
    return jnp.dot(a.astype(BF), b.astype(BF), preferred_element_type=F32)


def uv_of(index, plane):
    x = lax.shift_right_logical(index, 3) & 3
    z = lax.shift_right_logical(index, 1) & 3
    return (z, x) if plane == 0 else (x, z)


def iota(shape, dim):
    return lax.broadcasted_iota(I32, shape, dim)


def plan_kernel(sel_ref, cnt_ref, table_ref):
    s = iota((NSEQ, ROW), 0)
    d = iota((NSEQ, ROW), 1)
    loc = jnp.full((NSEQ, ROW), -1, I32)
    grp = jnp.zeros((NSEQ, ROW), I32)
    for n in range(2 * NB):
        row = sel_ref[n : n + 1, :]
        hit = lax.shift_right_arithmetic(row, 3) == s
        loc = jnp.where(hit, row & 7, loc)
        grp = jnp.where(hit, (n >> 1) & 1, grp)
    count = jnp.zeros((NSEQ, ROW), I32)
    for j in range(NB):
        count = jnp.where(loc == j, cnt_ref[:, j : j + 1], count)
    total = lax.shift_right_logical(count + (R - 1), R.bit_length() - 1)

    i32, j32 = iota((NSEQ, NSEQ), 0), iota((NSEQ, NSEQ), 1)
    i128, j128 = iota((ROW, ROW), 0), iota((ROW, ROW), 1)
    chip_l = ((i32 >> 1) == (j32 >> 1)).astype(F32)
    chip_r = ((i128 >> 1) == (j128 >> 1)).astype(F32)
    odd_l = jnp.logical_and(j32 == i32 - 1, (i32 & 1) == 1).astype(F32)
    odd_r = jnp.logical_and(i128 == j128 - 1, (j128 & 1) == 1).astype(F32)
    lower = (j32 < i32).astype(F32)
    for plane in range(2):
        first = (plane - loc) & 1
        n_of = jnp.where(loc >= 0, lax.shift_right_logical(total - first + 1, 1), 0)
        n_f = n_of.astype(F32)
        u_i, v_i = uv_of(i128, plane)
        u_j, v_j = uv_of(j128, plane)
        same_u = u_i == u_j
        m1 = jnp.logical_and(same_u, (v_i * 2 + (i128 & 1)) < (v_j * 2 + (j128 & 1))).astype(F32)
        same_u = same_u.astype(F32)
        dup = jnp.zeros((NSEQ, ROW), jnp.bool_)
        for j in range(NB):
            is_j = loc == j
            dup = jnp.logical_or(dup, jnp.logical_and(is_j, mm(is_j.astype(F32), m1) > 0.5))
        n1 = jnp.where(dup, 0.0, n_f)
        a_n = mm(chip_l, n1)
        pos1 = mm(a_n, m1) + mm(odd_l, n1)
        of_first = jnp.zeros((NSEQ, ROW), F32)
        for j in range(NB):
            is_j = loc == j
            there = mm(jnp.where(jnp.logical_and(is_j, jnp.logical_not(dup)), pos1, 0.0), same_u)
            of_first = jnp.where(is_j, there, of_first)
        pos1 = jnp.where(dup, of_first, pos1)
        u_s, v_s = uv_of(i32, plane)
        u_t, v_t = uv_of(j32, plane)
        same_v = v_s == v_t
        m2 = jnp.logical_and(same_v, (u_t * 2 + (j32 & 1)) < (u_s * 2 + (i32 & 1))).astype(F32)
        pos2 = mm(m2, mm(n_f, chip_r)) + mm(n_f, odd_r)
        pos3 = jnp.where(
            grp == 0,
            mm(lower, jnp.where(grp == 0, n_f, 0.0)),
            mm(lower, jnp.where(grp == 1, n_f, 0.0)),
        )
        entry = n_of | (jnp.maximum(loc, 0) << 3)
        for index, place in enumerate((pos1, pos2, pos3)):
            entry = entry | (place.astype(I32) << (6 + 6 * index))
        entry = entry | (dup.astype(I32) << 24)

        to_u = jnp.logical_and(i128 < NSEQ, j128 - NSEQ == u_i).astype(F32)
        to_v = jnp.logical_and(i128 < NSEQ, j128 - NSEQ - 4 == v_i).astype(F32)
        u_a, _ = uv_of(s, plane)
        u_b, _ = uv_of(d, plane)
        line = jnp.where(u_a == u_b, mm(same_v.astype(F32), n_f), 0.0)
        lengths = mm(a_n, to_u) + mm(line, to_v)
        table_ref[plane * NSEQ : (plane + 1) * NSEQ, :] = jnp.where(d < NSEQ, entry, lengths.astype(I32))


def balance_kernel(table, share_ref, level_ref):
    def one(ring_number, need):
        plane, stage, g = ring_number >> 3, (ring_number >> 2) & 1, ring_number & 3
        by_x = plane == stage
        rows = [
            plane * NSEQ + jnp.where(by_x, g * 4 + a, a * 4 + g) * 2 for a in range(4)
        ]
        far = NSEQ + stage * 4
        l1, l2, l3 = [[table[rows[a], far + ((a + r) & 3)] for a in range(4)] for r in (1, 2, 3)]
        h = [(n + 1) >> 1 for n in l2]

        def loads():
            plus = [l1[a] + h[a] + h[(a - 1) & 3] for a in range(4)]
            minus = [l3[a] + l2[a] - h[a] + l2[(a + 1) & 3] - h[(a + 1) & 3] for a in range(4)]
            return plus, minus

        for a in range(4):
            plus, minus = loads()
            high = jnp.maximum(plus[a], plus[(a + 1) & 3]) - h[a]
            low = jnp.maximum(minus[a], minus[(a - 1) & 3]) - (l2[a] - h[a])
            h[a] = jnp.clip((low + l2[a] - high + 1) >> 1, 0, l2[a])
        plus, minus = loads()
        most = functools.reduce(jnp.maximum, plus + minus)
        least = functools.reduce(jnp.maximum, h + [l2[a] - h[a] for a in range(4)])
        for a in range(4):
            share_ref[ring_number * 4 + a] = h[a]
        here = jnp.maximum((most + 1) >> 1, least)
        return (
            jnp.where(stage == 0, jnp.maximum(need[0], here), need[0]),
            jnp.where(stage == 1, jnp.maximum(need[1], here), need[1]),
        )

    need = lax.fori_loop(0, 16, one, (jnp.int32(0), jnp.int32(0)))
    level = jnp.int32(0)
    for cap in LEVELS[:-1]:
        level += jnp.logical_or(need[0] > cap[0], need[1] > cap[1]).astype(I32)
    level_ref[0] = level


def plan(selected, key_count):
    by_dest = jnp.pad(
        selected.reshape(NSEQ, 2 * NB).T, ((0, 0), (0, ROW - NSEQ)), constant_values=-1
    )
    table = pl.pallas_call(
        plan_kernel,
        out_shape=jax.ShapeDtypeStruct((2 * NSEQ, ROW), I32),
        in_specs=[VMEM, VMEM],
        out_specs=VMEM,
        compiler_params=pltpu.CompilerParams(vmem_limit_bytes=VLIM),
        name="plan",
    )(by_dest, key_count.reshape(NSEQ, NB))
    share, level = pl.pallas_call(
        balance_kernel,
        out_shape=(jax.ShapeDtypeStruct((64,), I32), jax.ShapeDtypeStruct((1,), I32)),
        in_specs=[SMEM],
        out_specs=(SMEM, SMEM),
        compiler_params=pltpu.CompilerParams(vmem_limit_bytes=VLIM),
        name="balance",
    )(table)
    return table, share, level[0]


def both_start(src_k, src_v, dst, sem):
    pltpu.make_async_copy(src_k, dst.at[0], sem).start()
    pltpu.make_async_copy(src_v, dst.at[1], sem).start()


def drain(count, like, sem):
    def one(_, carry):
        pltpu.make_async_copy(like, like, sem).wait()
        return carry

    lax.fori_loop(0, count, one, 0)


def spill(low, high, src, dst, sem):
    def one(row, carry):
        pltpu.make_async_copy(src.at[row], dst.at[row], sem).start()
        return carry

    lax.fori_loop(low, high, one, 0)
    return jnp.maximum(high - low, 0)


def split_kernel(me_ref, k_ref, v_ref, out_ref, sem):
    other = 1 - (me_ref[0] & 1)

    def one(index, carry):
        block = index // HALF
        chunk = block * CH + 2 * (index % HALF) + ((other - block) & 1)
        both_start(k_ref.at[chunk], v_ref.at[chunk], out_ref.at[index], sem)
        return carry

    lax.fori_loop(0, NB * HALF, one, 0)
    pltpu.make_async_copy(out_ref, out_ref, sem).wait()


class Place:
    def __init__(self, me, table, share, caps):
        self.me, self.table, self.share, self.caps = me, table, share, caps
        self.p = me & 1
        x, z = (me >> 3) & 3, (me >> 1) & 3
        self.u0 = jnp.where(self.p == 0, z, x)
        self.v0 = jnp.where(self.p == 0, x, z)

    def index(self, u, v, c):
        x = jnp.where(self.p == 0, v, u)
        z = jnp.where(self.p == 0, u, v)
        return (x * 4 + z) * 2 + c

    def entry(self, s, d):
        return self.table[self.p * NSEQ + s, d]

    def length(self, stage, a, b):
        a, b = a & 3, b & 3
        node = self.index(a, self.v0, 0) if stage == 0 else self.index(self.u0, a, 0)
        return self.table[self.p * NSEQ + node, NSEQ + 4 * stage + b]

    def halves(self, stage, a):
        a = a & 3
        ring_of = self.v0 if stage == 0 else self.u0
        h = self.share[((self.p * 2 + stage) * 4 + ring_of) * 4 + a]
        return h, self.length(stage, a, a + 2) - h

    def here(self, stage):
        return self.u0 if stage == 0 else self.v0


def chunk_of(loc, t, plane):
    return loc * CH + 2 * t + ((plane - loc) & 1)


class Source:
    def __init__(self, place, k_ref, v_ref, sib_ref, got):
        self.place, self.k, self.v, self.sib, self.got = place, k_ref, v_ref, sib_ref, got
        self.info = []
        for stage in range(len(got)):
            b = place.here(stage)
            far_p, far_m = place.halves(stage, b + 2)
            near_p, _ = place.halves(stage, b - 1)
            _, near_m = place.halves(stage, b + 1)
            self.info.append((far_p, far_m, near_p, near_m))

    def chunk(self, stage, a, q, t, loc, own, put):
        place = self.place
        if stage < 0:

            @pl.when(own)
            def _():
                c = chunk_of(loc, t, place.p)
                put(self.k.at[c], self.v.at[c])

            @pl.when(jnp.logical_not(own))
            def _():
                put(self.sib.at[loc * HALF + t])

            return
        g1p, g1m, g2p, g2m = self.got[stage]
        far_p, far_m, near_p, near_m = self.info[stage]
        cap = place.caps[stage]
        r = (place.here(stage) - a) & 3
        plus = jnp.logical_or(r == 1, jnp.logical_and(r == 2, q < far_p))
        near = jnp.where(r == 1, near_p, near_m)
        far = jnp.where(r == 1, far_p, far_m)
        first = jnp.logical_and(r != 2, q < cap - near)
        row = jnp.where(
            r == 2,
            jnp.where(plus, q, q - far_p),
            jnp.where(first, near + q, far + q - (cap - near)),
        )
        for is_plus, is_first, ref in (
            (True, True, g1p), (False, True, g1m), (True, False, g2p), (False, False, g2m),
        ):
            cond = jnp.logical_and(plus == is_plus, first == is_first)

            @pl.when(cond)
            def _(ref=ref):
                put(ref.at[row])

    def pair(self, s, e, put):
        place = self.place
        n, loc = e & 7, (e >> 3) & 7
        c = s & 1
        x, z = (s >> 3) & 3, (s >> 1) & 3
        u = jnp.where(place.p == 0, z, x)
        v = jnp.where(place.p == 0, x, z)
        own = c == place.p
        mine = u == place.u0
        last = len(self.got) - 1

        def loop(stage, a, base):
            def one(t, carry):
                self.chunk(stage, a, base + t, t, loc, own, functools.partial(put, t))
                return carry

            lax.fori_loop(0, n, one, 0)

        def early():
            if last < 0:
                loop(-1, 0, 0)
                return

            @pl.when(mine)
            def _():
                loop(-1, 0, 0)

            @pl.when(jnp.logical_not(mine))
            def _():
                loop(0, u, (e >> 6) & 63)

        if last < 1:
            early()
        else:
            same_v = v == place.v0

            @pl.when(same_v)
            def _():
                early()

            @pl.when(jnp.logical_not(same_v))
            def _():
                loop(1, v, (e >> 12) & 63)
        return n


def copier(dst, sem):
    def put(*src):
        if len(src) == 2:
            both_start(src[0], src[1], dst, sem)
        else:
            pltpu.make_async_copy(src[0], dst, sem).start()

    return put


def pack_kernel(stage, part, caps, me_ref, table, share, k_ref, v_ref, sib_ref, *refs):
    got = (refs[:4],) if stage else ()
    out_p, out_m, hold_p, hold_m, sem, sem_out = refs[len(refs) - 6 :]
    place = Place(me_ref[0], table, share, caps)
    source = Source(place, k_ref, v_ref, sib_ref, got)
    b = place.here(stage)
    cap = caps[stage]
    half_p, half_m = place.halves(stage, b)
    pass_p, _ = place.halves(stage, b - 1)
    _, pass_m = place.halves(stage, b + 1)
    shift = 6 if stage == 0 else 12
    started = 0
    for r in (2, 1, 3) if part == 0 else (1, 3):
        to = (b + r) & 3

        def one(i, count, r=r, to=to):
            if stage == 0:
                s = place.index(place.u0, place.v0, i & 1)
                d = place.index(to, i >> 2, (i >> 1) & 1)
            else:
                s = place.index(i >> 2, place.v0, (i >> 1) & 1)
                d = place.index(place.u0, to, i & 1)
            e = place.entry(s, d)
            base = (e >> shift) & 63
            if stage == 0:
                e = jnp.where((e >> 24) & 1 == 1, 0, e)

            if r == 2:
                rows = ((hold_p, 0, half_p, 0), (hold_m, half_p, 1 << 20, -half_p))
            else:
                hold, half, passed = (hold_p, half_p, pass_p) if r == 1 else (hold_m, half_m, pass_m)
                fits = cap - half
                rows = ((hold, 0, fits, half),) if part == 0 else ((hold, fits, 1 << 20, passed - fits),)

            def put(t, *src):
                q = base + t
                for hold, low, high, move in rows:

                    @pl.when(jnp.logical_and(q >= low, q < high))
                    def _(hold=hold, move=move):
                        copier(hold.at[q + move], sem)(*src)

            source.pair(s, e, put)
            n = e & 7
            return count + sum(
                jnp.maximum(jnp.minimum(base + n, high) - jnp.maximum(base, low), 0) for _, low, high, _ in rows
            )

        started = lax.fori_loop(0, 16, one, started)
    drain(started, hold_p.at[0], sem)
    started = 0
    for half, passed, n, hold, out in (
        (half_p, pass_p, place.length(stage, b, b + 1), hold_p, out_p),
        (half_m, pass_m, place.length(stage, b, b - 1), hold_m, out_m),
    ):
        fits = jnp.minimum(n, cap - half)
        if part == 0:
            started += spill(0, half + fits, hold, out, sem_out)
        else:
            started += spill(passed, passed + n - fits, hold, out, sem_out)
    drain(started, hold_p.at[0], sem_out)


def pass_kernel(stage, caps, me_ref, table, share, g1p, g1m, in_p, in_m, after, s2p, s2m, hold_p, hold_m, sem, sem_out):
    place = Place(me_ref[0], table, share, caps)
    b = place.here(stage)
    pass_p, _ = place.halves(stage, b - 1)
    _, pass_m = place.halves(stage, b + 1)
    started = spill(0, pass_p, g1p, hold_p, sem) + spill(0, pass_m, g1m, hold_m, sem)
    drain(started, hold_p.at[0], sem)
    started = spill(0, pass_p, hold_p, s2p, sem_out) + spill(0, pass_m, hold_m, s2m, sem_out)
    drain(started, hold_p.at[0], sem_out)


def cross_kernel(group, caps, me_ref, table, share, sel, k_ref, v_ref, sib_ref, *refs):
    got = (refs[:4], refs[4:8])
    out, hold, sem, sem_out = refs[-4:]
    place = Place(me_ref[0], table, share, caps)
    source = Source(place, k_ref, v_ref, sib_ref, got)
    dest = place.me ^ 1

    def one(i, count):
        n = ((i >> 1) * 2 + group) * 2 + (i & 1)
        s = sel[dest * 2 * NB + n] >> 3
        e = place.entry(s, dest)
        base = (e >> 18) & 63

        def put(t, *src):
            copier(hold.at[base + t], sem)(*src)

        return count + source.pair(s, e, put)

    count = lax.fori_loop(0, NB, one, 0)
    drain(count, hold.at[0], sem)
    drain(spill(0, count, hold, out, sem_out), hold.at[0], sem_out)


SIZES = (2, 4, 6, 8)
SCALE = 1.0 / math.sqrt(HS)


def heads_pipeline(keys, heads, q_of, k_of, v_of, bias, top_of, finish, scores, weights):
    tops = {}
    for i in range(heads + 2):
        if i < heads:
            q = q_of(i)
            hot = (iota(q.shape, 1) == 0).astype(F32).astype(BF)
            s = lax.dot_general(
                jnp.concatenate([q, hot], axis=1), jnp.concatenate([k_of(i), bias[:keys]], axis=1),
                (((1,), (1,)), ((), ())), preferred_element_type=F32,
            )
            scores[i % 2][:, :keys] = s
            tops[i] = jnp.max(s, axis=1, keepdims=True)
            top = top_of(i)
            if top is not None:
                tops[i] = jnp.maximum(tops[i], top)
        if 0 <= i - 1 < heads:
            h = i - 1
            w = jnp.exp(scores[h % 2][:, :keys] * SCALE - tops[h] * SCALE)
            weights[h % 2][:, :keys] = w.astype(BF)
        if i - 2 >= 0:
            h = i - 2
            v = v_of(h)
            a = jnp.dot(
                weights[h % 2][:, :keys], jnp.concatenate([v, jnp.ones(v.shape, BF)], axis=1),
                preferred_element_type=F32,
            )
            finish(h, tops.pop(h), a)


def bias_of(dead):
    return jnp.where(jnp.logical_and(dead, iota(dead.shape, 1) == 0), -1e30, 0.0).astype(BF)


def own_kernel(pre, q_ref, k_ref, v_ref, after, acc_ref, stat_ref, bias, s0, s1, w0, w1):
    count = pre[pl.program_id(0) + pre[NB]]
    bias[...] = bias_of(iota((BSZ, HS), 0) >= count)
    lane = iota((BSZ, HS), 1)

    def work(keys):
        def finish(h, m, a):
            acc_ref[0, :, h * HS : (h + 1) * HS] = a[:, :HS]
            before = stat_ref[0] if h else jnp.zeros((BSZ, HS), F32)
            stat_ref[0] = jnp.where(lane == h, m, jnp.where(lane == h + 4, a[:, HS:], before))

        cols = lambda ref, rows: lambda h: ref[0, :rows, h * HS : (h + 1) * HS]
        heads_pipeline(
            keys, q_ref.shape[2] // HS, cols(q_ref, BSZ), cols(k_ref, keys), cols(v_ref, keys), bias,
            lambda h: None, finish, (s0, s1), (w0, w1),
        )

    pl.when(count <= BSZ // 2)(functools.partial(work, BSZ // 2))
    pl.when(count > BSZ // 2)(functools.partial(work, BSZ))


def own_blocks(first, number, counts, q, k, v, after):
    width = q.shape[-1]
    block = pl.BlockSpec((1, BSZ, width), lambda i, pre: (pre[NB] + i, 0, 0))
    return pl.pallas_call(
        own_kernel,
        out_shape=(
            jax.ShapeDtypeStruct((number, BSZ, width), F32),
            jax.ShapeDtypeStruct((number, BSZ, HS), F32),
        ),
        grid_spec=pltpu.PrefetchScalarGridSpec(
            num_scalar_prefetch=1,
            grid=(number,),
            in_specs=[block] * 3 + [ANY],
            out_specs=(
                pl.BlockSpec((1, BSZ, width), lambda i, pre: (i, 0, 0)),
                pl.BlockSpec((1, BSZ, HS), lambda i, pre: (i, 0, 0)),
            ),
            scratch_shapes=[pltpu.VMEM((BSZ, HS), BF)]
            + [pltpu.VMEM((BSZ, BSZ), F32)] * 2 + [pltpu.VMEM((BSZ, BSZ), BF)] * 2,
        ),
        compiler_params=pltpu.CompilerParams(vmem_limit_bytes=VLIM),
        cost_estimate=pl.CostEstimate(
            flops=number * 8 * BSZ * BSZ * width, bytes_accessed=number * BSZ * width * 10, transcendentals=0
        ),
        name="own",
    )(jnp.concatenate([counts, first]), q, k, v, after)


def attend_kernel(steps, caps, pre, table, share, sel, q_ref, k_ref, v_ref, sib_ref, *refs):
    got, refs = (refs[:4], refs[4:8]), refs[8:]
    groups = sorted({g for g, _ in steps})
    crossed, refs = dict(zip(groups, refs)), refs[len(groups) :]
    owns, refs = [refs[2 * i : 2 * i + 2] for i in range(len(steps))], refs[2 * len(steps) :]
    outs, refs = refs[: len(steps)], refs[len(steps) :]
    kb, vb, bias, qb, accb, statb, ob, s0, s1, w0, w1, sem, fixed = refs
    width = q_ref.shape[2]
    me = pre[0]
    place = Place(me, table, share, caps)
    source = Source(place, k_ref, v_ref, sib_ref, got)
    plane = 1 - place.p

    def live(t):
        return [lax.shift_right_logical(pre[4 * t + 3 + i] + (R - 1), R.bit_length() - 1) for i in range(2)]

    def operands(t):
        acc, stat = owns[t]
        return [
            pltpu.make_async_copy(q_ref.at[pre[4 * t + 1]], qb.at[t], fixed.at[t]),
            pltpu.make_async_copy(acc.at[steps[t][0]], accb.at[t], fixed.at[t]),
            pltpu.make_async_copy(stat.at[steps[t][0]], statb.at[t], fixed.at[t]),
        ]

    for t in range(len(steps)):
        for copy in operands(t):
            copy.start()

    def gather(t, carry):
        block, group = pre[4 * t + 1], pre[4 * t + 2]
        n0, n1 = live(t)
        chunks = n0 + n1

        def pair(i, start):
            s = sel[(me * NB + block) * 2 + i] >> 3
            e = place.entry(s, me)
            loc = (e >> 3) & 7

            def put(c, *src):
                row = start + 2 * c + ((place.p - loc) & 1)
                src_k, src_v = src if len(src) == 2 else (src[0].at[0], src[0].at[1])
                pltpu.make_async_copy(src_k, kb.at[t, row], sem.at[t]).start()
                pltpu.make_async_copy(src_v, vb.at[t, row], sem.at[t]).start()

            source.pair(s, e, put)
            other = table[plane * NSEQ + s, me]
            base = (other >> 18) & 63
            for g, x_ref in crossed.items():

                def cross(c, carry):
                    row = start + 2 * c + ((plane - loc) & 1)
                    pltpu.make_async_copy(x_ref.at[base + c, 0], kb.at[t, row], sem.at[t]).start()
                    pltpu.make_async_copy(x_ref.at[base + c, 1], vb.at[t, row], sem.at[t]).start()
                    return carry

                lax.fori_loop(0, jnp.where(group == g, other & 7, 0), cross, 0)
            return n0

        lax.fori_loop(0, 2, pair, 0)

        key = iota((2 * BSZ, HS), 0)
        begin = n0 * R
        dead = jnp.logical_and(
            key >= pre[4 * t + 3], jnp.logical_or(key < begin, key >= begin + pre[4 * t + 4])
        )
        bias[t] = bias_of(dead)

        for extra in range(3):

            @pl.when(chunks + extra < 2 * CH)
            def _():
                kb[t, chunks + extra] = jnp.zeros((R, width), BF)
                vb[t, chunks + extra] = jnp.zeros((R, width), BF)

        return carry

    lax.fori_loop(0, len(steps), gather, 0)

    def work(tiles, t):
        keys = tiles * HS
        column = lambda i: jnp.sum(jnp.where(iota((BSZ, HS), 1) == i, statb[t], 0.0), axis=1, keepdims=True)
        part = lambda h: slice(h * HS, (h + 1) * HS)
        own_m = {}

        def top_of(h):
            own_m[h] = column(h)
            return own_m[h]

        def finish(h, m, a):
            factor = jnp.exp((own_m[h] - m) * SCALE)
            numer = a[:, :HS] + factor * accb[t, :, part(h)]
            ob[t, :, part(h)] = (numer / (a[:, HS:] + factor * column(h + 4))).astype(BF)

        heads_pipeline(
            keys, width // HS,
            lambda h: qb[t, :, part(h)],
            lambda h: kb[t, : tiles * 2, :, part(h)].reshape(keys, HS),
            lambda h: vb[t, : tiles * 2, :, part(h)].reshape(keys, HS),
            bias.at[t], top_of, finish, (s0, s1), (w0, w1),
        )

    def compute(t, carry):
        n0, n1 = live(t)
        chunks = n0 + n1
        drain(2 * chunks, kb.at[0, 0], sem.at[t])
        for like in (qb, accb, statb):
            pltpu.make_async_copy(like.at[0], like.at[0], fixed.at[t]).wait()
        least = 0
        for tiles in SIZES:
            pl.when(jnp.logical_and(chunks > least, chunks <= 2 * tiles))(functools.partial(work, tiles, t))
            least = 2 * tiles
        return carry

    lax.fori_loop(0, len(steps), compute, 0)
    for t in range(len(steps)):
        outs[t][...] = ob[t]


def attend(caps, steps, pre, table, share, sel, q, own, kc, vc, sib, got, crossed):
    width = q.shape[-1]
    n = len(steps)
    ins = [q, kc, vc, sib] + got + [crossed[g] for g in sorted({g for g, _ in steps})]
    for _, r in steps:
        ins += own[r]
    out = pl.BlockSpec((BSZ, width), lambda i, pre: (0, 0))
    return pl.pallas_call(
        functools.partial(attend_kernel, steps, caps),
        out_shape=[jax.ShapeDtypeStruct((BSZ, width), BF)] * n,
        grid_spec=pltpu.PrefetchScalarGridSpec(
            num_scalar_prefetch=1,
            grid=(1,),
            in_specs=[SMEM] * 3 + [ANY] * len(ins),
            out_specs=[out] * n,
            scratch_shapes=[
                pltpu.VMEM((n, 2 * CH, R, width), BF),
                pltpu.VMEM((n, 2 * CH, R, width), BF),
                pltpu.VMEM((n, 2 * BSZ, HS), BF),
                pltpu.VMEM((n, BSZ, width), BF),
                pltpu.VMEM((n, BSZ, width), F32),
                pltpu.VMEM((n, BSZ, HS), F32),
                pltpu.VMEM((n, BSZ, width), BF),
                pltpu.VMEM((BSZ, 2 * BSZ), F32),
                pltpu.VMEM((BSZ, 2 * BSZ), F32),
                pltpu.VMEM((BSZ, 2 * BSZ), BF),
                pltpu.VMEM((BSZ, 2 * BSZ), BF),
                pltpu.SemaphoreType.DMA((n,)),
                pltpu.SemaphoreType.DMA((n,)),
            ],
        ),
        compiler_params=pltpu.CompilerParams(vmem_limit_bytes=VLIM),
        cost_estimate=pl.CostEstimate(
            flops=n * 8 * BSZ * BSZ * width, bytes_accessed=n * 8 * BSZ * width * 2, transcendentals=0
        ),
        name="attend",
    )(pre, table, share, sel, *ins)


def project_kernel(pre, *refs):
    parts, (w_ref, o_ref, rows) = refs[:-3], refs[-3:]
    width = parts[0].shape[1]

    @pl.when(pl.program_id(0) == 0)
    def _():
        for index, part in enumerate(parts):
            g, r = index >> 2, index & 3
            head = (pre[0] - r) & 3
            rows[g * BSZ : (g + 1) * BSZ, pl.ds(pl.multiple_of(head * width, width), width)] = part[...]

    o_ref[...] = jnp.dot(rows[...], w_ref[...], preferred_element_type=F32).astype(BF)


def project(head, parts, w_out):
    cols = w_out.shape[1]
    tile = 512
    whole = lambda a: pl.BlockSpec(a.shape, lambda n, pre: (0, 0))
    return pl.pallas_call(
        project_kernel,
        out_shape=jax.ShapeDtypeStruct((2 * BSZ, cols), BF),
        grid_spec=pltpu.PrefetchScalarGridSpec(
            num_scalar_prefetch=1,
            grid=(cols // tile,),
            in_specs=[whole(a) for a in parts] + [pl.BlockSpec((w_out.shape[0], tile), lambda n, pre: (0, n))],
            out_specs=pl.BlockSpec((2 * BSZ, tile), lambda n, pre: (0, n)),
            scratch_shapes=[pltpu.VMEM((2 * BSZ, w_out.shape[0]), BF)],
        ),
        compiler_params=pltpu.CompilerParams(vmem_limit_bytes=VLIM),
        cost_estimate=pl.CostEstimate(
            flops=4 * BSZ * cols * cols, bytes_accessed=2 * cols * cols + 8 * BSZ * cols, transcendentals=0
        ),
        name="project",
    )(head, *parts, w_out)


def ring(stage, step):
    pairs = []
    for x in range(4):
        for z in range(4):
            for c in range(2):
                along_z = (c == 0) == (stage == 0)
                to = (x, (z + step) % 4) if along_z else ((x + step) % 4, z)
                pairs.append(((x * 4 + z) * 2 + c, (to[0] * 4 + to[1]) * 2 + c))
    return pairs


def copies(kernel, outs, ins, specs, hold, name, aliases=None, moved=8 * 2**20):
    return pl.pallas_call(
        kernel,
        out_shape=outs,
        in_specs=specs,
        out_specs=[ANY] * len(outs),
        scratch_shapes=[pltpu.VMEM(a.shape, a.dtype) for a in hold] + [pltpu.SemaphoreType.DMA] * 2,
        input_output_aliases=aliases or {},
        compiler_params=pltpu.CompilerParams(vmem_limit_bytes=VLIM),
        cost_estimate=pl.CostEstimate(flops=0, bytes_accessed=moved, transcendentals=0),
        name=name,
    )(*ins)


def fetch(caps, me, table, share, sel, kc, vc, sib, beside):
    width = kc.shape[-1]
    got, done, after = [], [], []
    for stage in range(2):
        sends = [jax.ShapeDtypeStruct((caps[stage], 2, R, width), BF)] * 2
        ins = [me, table, share, kc, vc, sib] + got + after
        s1p, s1m = copies(
            functools.partial(pack_kernel, stage, 0, caps), sends, ins,
            [SMEM] * 3 + [ANY] * (len(ins) - 3), sends, "pack%d" % stage,
        )
        g1p = lax.ppermute(s1p, "seq", ring(stage, 1))
        g1m = lax.ppermute(s1m, "seq", ring(stage, -1))
        done.append(beside(2 * stage, s1p))
        ins = [me, table, share, kc, vc, sib] + got + [done[-1][0]]
        s2p, s2m = copies(
            functools.partial(pack_kernel, stage, 1, caps), sends, ins,
            [SMEM] * 3 + [ANY] * (len(ins) - 3), sends, "rest%d" % stage,
        )
        s2p, s2m = copies(
            functools.partial(pass_kernel, stage, caps), sends,
            [me, table, share, g1p, g1m, s2p, s2m, done[-1][0]],
            [SMEM] * 3 + [ANY] * 5, sends, "pass%d" % stage, {5: 0, 6: 1},
        )
        g2p = lax.ppermute(s2p, "seq", ring(stage, 1))
        g2m = lax.ppermute(s2m, "seq", ring(stage, -1))
        done.append(beside(2 * stage + 1, s2p))
        got += [g1p, g1m, g2p, g2m]
        after = [done[-1][0]]
    x_shapes = [jax.ShapeDtypeStruct((NB * HALF, 2, R, width), BF)]
    ins = [me, table, share, sel, kc, vc, sib] + got + after
    swap = [(i, i ^ 1) for i in range(NSEQ)]
    crossed = []
    for group in range(2):
        x = copies(
            functools.partial(cross_kernel, group, caps), x_shapes, ins,
            [SMEM] * 4 + [ANY] * (len(ins) - 4), x_shapes, "cross%d" % group,
        )[0]
        crossed.append(lax.ppermute(x, "seq", swap))
        ins = ins + [x]
    return got, crossed, done


def before_fetch(keys, values, key_count, selected):
    width = keys.shape[1]
    me = lax.axis_index("seq").astype(I32).reshape(1)
    kc = keys.reshape(NB * CH, R, width)
    vc = values.reshape(NB * CH, R, width)
    sent = pl.pallas_call(
        split_kernel,
        out_shape=jax.ShapeDtypeStruct((NB * HALF, 2, R, width), BF),
        in_specs=[SMEM, ANY, ANY],
        out_specs=VMEM,
        scratch_shapes=[pltpu.SemaphoreType.DMA],
        compiler_params=pltpu.CompilerParams(vmem_limit_bytes=VLIM),
        cost_estimate=pl.CostEstimate(flops=0, bytes_accessed=8 * 2**20, transcendentals=0),
        name="split",
    )(me, kc, vc)
    sib = lax.ppermute(sent, "seq", [(i, i ^ 1) for i in range(NSEQ)])
    return (me, kc, vc, sib) + plan(selected, key_count)


def on_device(queries, keys, values, key_count, selected, w_out):
    width = queries.shape[1]
    me, kc, vc, sib, table, share, level = before_fetch(keys, values, key_count, selected)
    sel = selected.reshape(-1)
    head = lax.axis_index("head").astype(I32).reshape(1)
    q, k, v = [a.reshape(NB, BSZ, width) for a in (queries, keys, values)]
    own_counts = lax.dynamic_slice_in_dim(key_count, me[0] * NB, NB)
    far_counts = key_count[lax.dynamic_slice_in_dim(selected, me[0] * NB, NB)]
    calls = (((0, 2), (0, 1)), ((0, 3), (1, 2)), ((1, 1), (1, 3)), ((0, 0), (1, 0)))
    pre = []
    for steps in calls:
        row = [me]
        for g, r in steps:
            block = ((head + r) & 3) * 2 + g
            row += [block, jnp.full((1,), g, I32), far_counts[block[0]]]
        pre.append(jnp.concatenate(row))
    up = [(i, (i + 1) % 4) for i in range(4)]
    down = [(i, (i - 1) % 4) for i in range(4)]

    def rest(caps, sib, table, share, pre, own_counts):
        def beside(r, after):
            return own_blocks(((head + r) & 3) * 2, 2, own_counts, q, k, v, after)

        got, crossed, own = fetch(caps, me, table, share, sel, kc, vc, sib, beside)
        parts = {}
        for row, steps in zip(pre, calls):
            made = attend(caps, steps, row, table, share, sel, q, own, kc, vc, sib, got, crossed)
            for (g, r), part in zip(steps, made):
                way = {0: None, 1: up, 2: up if g == 0 else down, 3: down}[r]
                for _ in range((0, 1, 2, 1)[r]):
                    part = lax.ppermute(part, "head", way)
                parts[g, r] = part
        return project(head, [parts[g, r] for g in range(2) for r in range(4)], w_out)

    return lax.switch(
        level, [functools.partial(rest, caps) for caps in LEVELS], sib, table, share, pre, own_counts
    )


def solution(mesh):
    placed = (P("seq", "head"), P("seq", "head"), P("seq", "head"), P(), P(), P())
    return jax.shard_map(
        on_device, mesh=mesh, in_specs=placed, out_specs=P(("seq", "head"), None), check_vma=False
    )
```

```python
import functools
import math

import jax
import jax.numpy as jnp
from jax import lax
from jax.experimental import pallas as pl
from jax.experimental.pallas import tpu as pltpu
from jax.sharding import PartitionSpec as P

HS = 128
BSZ = 512
R = 64
CH = BSZ // R
HALF = CH // 2
NB = 8
NSEQ = 32
LEVELS = ((21, 24), (22, 25), (23, 27), (26, 30), (64, 64))
VLIM = 60 * 2**20
ROW = 128
F32 = jnp.float32
I32 = jnp.int32
BF = jnp.bfloat16
ANY = pl.BlockSpec(memory_space=pl.ANY)
SMEM = pl.BlockSpec(memory_space=pltpu.SMEM)
VMEM = pl.BlockSpec(memory_space=pltpu.VMEM)


def mm(a, b):
    return jnp.dot(a.astype(BF), b.astype(BF), preferred_element_type=F32)


def uv_of(index, plane):
    x = lax.shift_right_logical(index, 3) & 3
    z = lax.shift_right_logical(index, 1) & 3
    return (z, x) if plane == 0 else (x, z)


def iota(shape, dim):
    return lax.broadcasted_iota(I32, shape, dim)


def plan_kernel(sel_ref, cnt_ref, table_ref):
    s = iota((NSEQ, ROW), 0)
    d = iota((NSEQ, ROW), 1)
    loc = jnp.full((NSEQ, ROW), -1, I32)
    grp = jnp.zeros((NSEQ, ROW), I32)
    for n in range(2 * NB):
        row = sel_ref[n : n + 1, :]
        hit = lax.shift_right_arithmetic(row, 3) == s
        loc = jnp.where(hit, row & 7, loc)
        grp = jnp.where(hit, (n >> 1) & 1, grp)
    count = jnp.zeros((NSEQ, ROW), I32)
    for j in range(NB):
        count = jnp.where(loc == j, cnt_ref[:, j : j + 1], count)
    total = lax.shift_right_logical(count + (R - 1), R.bit_length() - 1)

    i32, j32 = iota((NSEQ, NSEQ), 0), iota((NSEQ, NSEQ), 1)
    i128, j128 = iota((ROW, ROW), 0), iota((ROW, ROW), 1)
    chip_l = ((i32 >> 1) == (j32 >> 1)).astype(F32)
    chip_r = ((i128 >> 1) == (j128 >> 1)).astype(F32)
    odd_l = jnp.logical_and(j32 == i32 - 1, (i32 & 1) == 1).astype(F32)
    odd_r = jnp.logical_and(i128 == j128 - 1, (j128 & 1) == 1).astype(F32)
    lower = (j32 < i32).astype(F32)
    for plane in range(2):
        first = (plane - loc) & 1
        n_of = jnp.where(loc >= 0, lax.shift_right_logical(total - first + 1, 1), 0)
        n_f = n_of.astype(F32)
        u_i, v_i = uv_of(i128, plane)
        u_j, v_j = uv_of(j128, plane)
        same_u = u_i == u_j
        m1 = jnp.logical_and(same_u, (v_i * 2 + (i128 & 1)) < (v_j * 2 + (j128 & 1))).astype(F32)
        same_u = same_u.astype(F32)
        dup = jnp.zeros((NSEQ, ROW), jnp.bool_)
        for j in range(NB):
            is_j = loc == j
            dup = jnp.logical_or(dup, jnp.logical_and(is_j, mm(is_j.astype(F32), m1) > 0.5))
        n1 = jnp.where(dup, 0.0, n_f)
        a_n = mm(chip_l, n1)
        pos1 = mm(a_n, m1) + mm(odd_l, n1)
        of_first = jnp.zeros((NSEQ, ROW), F32)
        for j in range(NB):
            is_j = loc == j
            there = mm(jnp.where(jnp.logical_and(is_j, jnp.logical_not(dup)), pos1, 0.0), same_u)
            of_first = jnp.where(is_j, there, of_first)
        pos1 = jnp.where(dup, of_first, pos1)
        u_s, v_s = uv_of(i32, plane)
        u_t, v_t = uv_of(j32, plane)
        same_v = v_s == v_t
        m2 = jnp.logical_and(same_v, (u_t * 2 + (j32 & 1)) < (u_s * 2 + (i32 & 1))).astype(F32)
        pos2 = mm(m2, mm(n_f, chip_r)) + mm(n_f, odd_r)
        pos3 = jnp.where(
            grp == 0,
            mm(lower, jnp.where(grp == 0, n_f, 0.0)),
            mm(lower, jnp.where(grp == 1, n_f, 0.0)),
        )
        entry = n_of | (jnp.maximum(loc, 0) << 3)
        for index, place in enumerate((pos1, pos2, pos3)):
            entry = entry | (place.astype(I32) << (6 + 6 * index))
        entry = entry | (dup.astype(I32) << 24)

        to_u = jnp.logical_and(i128 < NSEQ, j128 - NSEQ == u_i).astype(F32)
        to_v = jnp.logical_and(i128 < NSEQ, j128 - NSEQ - 4 == v_i).astype(F32)
        u_a, _ = uv_of(s, plane)
        u_b, _ = uv_of(d, plane)
        line = jnp.where(u_a == u_b, mm(same_v.astype(F32), n_f), 0.0)
        lengths = mm(a_n, to_u) + mm(line, to_v)
        table_ref[plane * NSEQ : (plane + 1) * NSEQ, :] = jnp.where(d < NSEQ, entry, lengths.astype(I32))


def balance_kernel(table, share_ref, level_ref):
    def one(ring_number, need):
        plane, stage, g = ring_number >> 3, (ring_number >> 2) & 1, ring_number & 3
        by_x = plane == stage
        rows = [
            plane * NSEQ + jnp.where(by_x, g * 4 + a, a * 4 + g) * 2 for a in range(4)
        ]
        far = NSEQ + stage * 4
        l1, l2, l3 = [[table[rows[a], far + ((a + r) & 3)] for a in range(4)] for r in (1, 2, 3)]
        h = [(n + 1) >> 1 for n in l2]

        def loads():
            plus = [l1[a] + h[a] + h[(a - 1) & 3] for a in range(4)]
            minus = [l3[a] + l2[a] - h[a] + l2[(a + 1) & 3] - h[(a + 1) & 3] for a in range(4)]
            return plus, minus

        for a in range(4):
            plus, minus = loads()
            high = jnp.maximum(plus[a], plus[(a + 1) & 3]) - h[a]
            low = jnp.maximum(minus[a], minus[(a - 1) & 3]) - (l2[a] - h[a])
            h[a] = jnp.clip((low + l2[a] - high + 1) >> 1, 0, l2[a])
        plus, minus = loads()
        most = functools.reduce(jnp.maximum, plus + minus)
        least = functools.reduce(jnp.maximum, h + [l2[a] - h[a] for a in range(4)])
        for a in range(4):
            share_ref[ring_number * 4 + a] = h[a]
        here = jnp.maximum((most + 1) >> 1, least)
        return (
            jnp.where(stage == 0, jnp.maximum(need[0], here), need[0]),
            jnp.where(stage == 1, jnp.maximum(need[1], here), need[1]),
        )

    need = lax.fori_loop(0, 16, one, (jnp.int32(0), jnp.int32(0)))
    level = jnp.int32(0)
    for cap in LEVELS[:-1]:
        level += jnp.logical_or(need[0] > cap[0], need[1] > cap[1]).astype(I32)
    level_ref[0] = level


def plan(selected, key_count):
    by_dest = jnp.pad(
        selected.reshape(NSEQ, 2 * NB).T, ((0, 0), (0, ROW - NSEQ)), constant_values=-1
    )
    table = pl.pallas_call(
        plan_kernel,
        out_shape=jax.ShapeDtypeStruct((2 * NSEQ, ROW), I32),
        in_specs=[VMEM, VMEM],
        out_specs=VMEM,
        compiler_params=pltpu.CompilerParams(vmem_limit_bytes=VLIM),
        name="plan",
    )(by_dest, key_count.reshape(NSEQ, NB))
    share, level = pl.pallas_call(
        balance_kernel,
        out_shape=(jax.ShapeDtypeStruct((64,), I32), jax.ShapeDtypeStruct((1,), I32)),
        in_specs=[SMEM],
        out_specs=(SMEM, SMEM),
        compiler_params=pltpu.CompilerParams(vmem_limit_bytes=VLIM),
        name="balance",
    )(table)
    return table, share, level[0]


def both_start(src_k, src_v, dst, sem):
    pltpu.make_async_copy(src_k, dst.at[0], sem).start()
    pltpu.make_async_copy(src_v, dst.at[1], sem).start()


def drain(count, like, sem):
    def one(_, carry):
        pltpu.make_async_copy(like, like, sem).wait()
        return carry

    lax.fori_loop(0, count, one, 0)


def spill(low, high, src, dst, sem):
    def one(row, carry):
        pltpu.make_async_copy(src.at[row], dst.at[row], sem).start()
        return carry

    lax.fori_loop(low, high, one, 0)
    return jnp.maximum(high - low, 0)


def split_kernel(me_ref, k_ref, v_ref, out_ref, sem):
    other = 1 - (me_ref[0] & 1)

    def one(index, carry):
        block = index // HALF
        chunk = block * CH + 2 * (index % HALF) + ((other - block) & 1)
        both_start(k_ref.at[chunk], v_ref.at[chunk], out_ref.at[index], sem)
        return carry

    lax.fori_loop(0, NB * HALF, one, 0)
    pltpu.make_async_copy(out_ref, out_ref, sem).wait()


class Place:
    def __init__(self, me, table, share, caps):
        self.me, self.table, self.share, self.caps = me, table, share, caps
        self.p = me & 1
        x, z = (me >> 3) & 3, (me >> 1) & 3
        self.u0 = jnp.where(self.p == 0, z, x)
        self.v0 = jnp.where(self.p == 0, x, z)

    def index(self, u, v, c):
        x = jnp.where(self.p == 0, v, u)
        z = jnp.where(self.p == 0, u, v)
        return (x * 4 + z) * 2 + c

    def entry(self, s, d):
        return self.table[self.p * NSEQ + s, d]

    def length(self, stage, a, b):
        a, b = a & 3, b & 3
        node = self.index(a, self.v0, 0) if stage == 0 else self.index(self.u0, a, 0)
        return self.table[self.p * NSEQ + node, NSEQ + 4 * stage + b]

    def halves(self, stage, a):
        a = a & 3
        ring_of = self.v0 if stage == 0 else self.u0
        h = self.share[((self.p * 2 + stage) * 4 + ring_of) * 4 + a]
        return h, self.length(stage, a, a + 2) - h

    def here(self, stage):
        return self.u0 if stage == 0 else self.v0


def chunk_of(loc, t, plane):
    return loc * CH + 2 * t + ((plane - loc) & 1)


class Source:
    def __init__(self, place, k_ref, v_ref, sib_ref, got):
        self.place, self.k, self.v, self.sib, self.got = place, k_ref, v_ref, sib_ref, got
        self.info = []
        for stage in range(len(got)):
            b = place.here(stage)
            far_p, far_m = place.halves(stage, b + 2)
            near_p, _ = place.halves(stage, b - 1)
            _, near_m = place.halves(stage, b + 1)
            self.info.append((far_p, far_m, near_p, near_m))

    def chunk(self, stage, a, q, t, loc, own, put):
        place = self.place
        if stage < 0:

            @pl.when(own)
            def _():
                c = chunk_of(loc, t, place.p)
                put(self.k.at[c], self.v.at[c])

            @pl.when(jnp.logical_not(own))
            def _():
                put(self.sib.at[loc * HALF + t])

            return
        g1p, g1m, g2p, g2m = self.got[stage]
        far_p, far_m, near_p, near_m = self.info[stage]
        cap = place.caps[stage]
        r = (place.here(stage) - a) & 3
        plus = jnp.logical_or(r == 1, jnp.logical_and(r == 2, q < far_p))
        near = jnp.where(r == 1, near_p, near_m)
        far = jnp.where(r == 1, far_p, far_m)
        first = jnp.logical_and(r != 2, q < cap - near)
        row = jnp.where(
            r == 2,
            jnp.where(plus, q, q - far_p),
            jnp.where(first, near + q, far + q - (cap - near)),
        )
        for is_plus, is_first, ref in (
            (True, True, g1p), (False, True, g1m), (True, False, g2p), (False, False, g2m),
        ):
            cond = jnp.logical_and(plus == is_plus, first == is_first)

            @pl.when(cond)
            def _(ref=ref):
                put(ref.at[row])

    def pair(self, s, e, put):
        place = self.place
        n, loc = e & 7, (e >> 3) & 7
        c = s & 1
        x, z = (s >> 3) & 3, (s >> 1) & 3
        u = jnp.where(place.p == 0, z, x)
        v = jnp.where(place.p == 0, x, z)
        own = c == place.p
        mine = u == place.u0
        last = len(self.got) - 1

        def loop(stage, a, base):
            def one(t, carry):
                self.chunk(stage, a, base + t, t, loc, own, functools.partial(put, t))
                return carry

            lax.fori_loop(0, n, one, 0)

        def early():
            if last < 0:
                loop(-1, 0, 0)
                return

            @pl.when(mine)
            def _():
                loop(-1, 0, 0)

            @pl.when(jnp.logical_not(mine))
            def _():
                loop(0, u, (e >> 6) & 63)

        if last < 1:
            early()
        else:
            same_v = v == place.v0

            @pl.when(same_v)
            def _():
                early()

            @pl.when(jnp.logical_not(same_v))
            def _():
                loop(1, v, (e >> 12) & 63)
        return n


def copier(dst, sem):
    def put(*src):
        if len(src) == 2:
            both_start(src[0], src[1], dst, sem)
        else:
            pltpu.make_async_copy(src[0], dst, sem).start()

    return put


def pack_kernel(stage, part, caps, me_ref, table, share, k_ref, v_ref, sib_ref, *refs):
    got = (refs[:4],) if stage else ()
    out_p, out_m, hold_p, hold_m, sem, sem_out = refs[len(refs) - 6 :]
    place = Place(me_ref[0], table, share, caps)
    source = Source(place, k_ref, v_ref, sib_ref, got)
    b = place.here(stage)
    cap = caps[stage]
    half_p, half_m = place.halves(stage, b)
    pass_p, _ = place.halves(stage, b - 1)
    _, pass_m = place.halves(stage, b + 1)
    shift = 6 if stage == 0 else 12
    started = 0
    for r in (2, 1, 3) if part == 0 else (1, 3):
        to = (b + r) & 3

        def one(i, count, r=r, to=to):
            if stage == 0:
                s = place.index(place.u0, place.v0, i & 1)
                d = place.index(to, i >> 2, (i >> 1) & 1)
            else:
                s = place.index(i >> 2, place.v0, (i >> 1) & 1)
                d = place.index(place.u0, to, i & 1)
            e = place.entry(s, d)
            base = (e >> shift) & 63
            if stage == 0:
                e = jnp.where((e >> 24) & 1 == 1, 0, e)

            if r == 2:
                rows = ((hold_p, 0, half_p, 0), (hold_m, half_p, 1 << 20, -half_p))
            else:
                hold, half, passed = (hold_p, half_p, pass_p) if r == 1 else (hold_m, half_m, pass_m)
                fits = cap - half
                rows = ((hold, 0, fits, half),) if part == 0 else ((hold, fits, 1 << 20, passed - fits),)

            def put(t, *src):
                q = base + t
                for hold, low, high, move in rows:

                    @pl.when(jnp.logical_and(q >= low, q < high))
                    def _(hold=hold, move=move):
                        copier(hold.at[q + move], sem)(*src)

            source.pair(s, e, put)
            n = e & 7
            return count + sum(
                jnp.maximum(jnp.minimum(base + n, high) - jnp.maximum(base, low), 0) for _, low, high, _ in rows
            )

        started = lax.fori_loop(0, 16, one, started)
    drain(started, hold_p.at[0], sem)
    started = 0
    for half, passed, n, hold, out in (
        (half_p, pass_p, place.length(stage, b, b + 1), hold_p, out_p),
        (half_m, pass_m, place.length(stage, b, b - 1), hold_m, out_m),
    ):
        fits = jnp.minimum(n, cap - half)
        if part == 0:
            started += spill(0, half + fits, hold, out, sem_out)
        else:
            started += spill(passed, passed + n - fits, hold, out, sem_out)
    drain(started, hold_p.at[0], sem_out)


def pass_kernel(stage, caps, me_ref, table, share, g1p, g1m, in_p, in_m, after, s2p, s2m, hold_p, hold_m, sem, sem_out):
    place = Place(me_ref[0], table, share, caps)
    b = place.here(stage)
    pass_p, _ = place.halves(stage, b - 1)
    _, pass_m = place.halves(stage, b + 1)
    started = spill(0, pass_p, g1p, hold_p, sem) + spill(0, pass_m, g1m, hold_m, sem)
    drain(started, hold_p.at[0], sem)
    started = spill(0, pass_p, hold_p, s2p, sem_out) + spill(0, pass_m, hold_m, s2m, sem_out)
    drain(started, hold_p.at[0], sem_out)


def cross_kernel(caps, me_ref, table, share, sel, k_ref, v_ref, sib_ref, *refs):
    got = (refs[:4], refs[4:8])
    out0, out1, x0, x1, sem, sem_out = refs[-6:]
    place = Place(me_ref[0], table, share, caps)
    source = Source(place, k_ref, v_ref, sib_ref, got)
    dest = place.me ^ 1

    def one(n, counts):
        s = sel[dest * 2 * NB + n] >> 3
        e = place.entry(s, dest)
        base = (e >> 18) & 63
        group = (n >> 1) & 1

        def put(t, *src):
            @pl.when(group == 0)
            def _():
                copier(x0.at[base + t], sem)(*src)

            @pl.when(group == 1)
            def _():
                copier(x1.at[base + t], sem)(*src)

        here = source.pair(s, e, put)
        return counts[0] + jnp.where(group == 0, here, 0), counts[1] + jnp.where(group == 1, here, 0)

    count0, count1 = lax.fori_loop(0, 2 * NB, one, (0, 0))
    drain(count0 + count1, x0.at[0], sem)
    started = spill(0, count0, x0, out0, sem_out) + spill(0, count1, x1, out1, sem_out)
    drain(started, x0.at[0], sem_out)


SIZES = (2, 4, 6, 8)
SCALE = 1.0 / math.sqrt(HS)


def heads_pipeline(keys, heads, q_of, k_of, v_of, bias, top_of, finish, scores, weights):
    tops = {}
    for i in range(heads + 2):
        if i < heads:
            q = q_of(i)
            hot = (iota(q.shape, 1) == 0).astype(F32).astype(BF)
            s = lax.dot_general(
                jnp.concatenate([q, hot], axis=1), jnp.concatenate([k_of(i), bias[:keys]], axis=1),
                (((1,), (1,)), ((), ())), preferred_element_type=F32,
            )
            scores[i % 2][:, :keys] = s
            tops[i] = jnp.max(s, axis=1, keepdims=True)
            top = top_of(i)
            if top is not None:
                tops[i] = jnp.maximum(tops[i], top)
        if 0 <= i - 1 < heads:
            h = i - 1
            w = jnp.exp(scores[h % 2][:, :keys] * SCALE - tops[h] * SCALE)
            weights[h % 2][:, :keys] = w.astype(BF)
        if i - 2 >= 0:
            h = i - 2
            v = v_of(h)
            a = jnp.dot(
                weights[h % 2][:, :keys], jnp.concatenate([v, jnp.ones(v.shape, BF)], axis=1),
                preferred_element_type=F32,
            )
            finish(h, tops.pop(h), a)


def bias_of(dead):
    return jnp.where(jnp.logical_and(dead, iota(dead.shape, 1) == 0), -1e30, 0.0).astype(BF)


def own_kernel(pre, q_ref, k_ref, v_ref, after, acc_ref, stat_ref, bias, s0, s1, w0, w1):
    count = pre[pl.program_id(0) + pre[NB]]
    bias[...] = bias_of(iota((BSZ, HS), 0) >= count)
    lane = iota((BSZ, HS), 1)

    def work(keys):
        def finish(h, m, a):
            acc_ref[0, :, h * HS : (h + 1) * HS] = a[:, :HS]
            before = stat_ref[0] if h else jnp.zeros((BSZ, HS), F32)
            stat_ref[0] = jnp.where(lane == h, m, jnp.where(lane == h + 4, a[:, HS:], before))

        cols = lambda ref, rows: lambda h: ref[0, :rows, h * HS : (h + 1) * HS]
        heads_pipeline(
            keys, q_ref.shape[2] // HS, cols(q_ref, BSZ), cols(k_ref, keys), cols(v_ref, keys), bias,
            lambda h: None, finish, (s0, s1), (w0, w1),
        )

    pl.when(count <= BSZ // 2)(functools.partial(work, BSZ // 2))
    pl.when(count > BSZ // 2)(functools.partial(work, BSZ))


def own_blocks(first, number, counts, q, k, v, after):
    width = q.shape[-1]
    block = pl.BlockSpec((1, BSZ, width), lambda i, pre: (pre[NB] + i, 0, 0))
    return pl.pallas_call(
        own_kernel,
        out_shape=(
            jax.ShapeDtypeStruct((number, BSZ, width), F32),
            jax.ShapeDtypeStruct((number, BSZ, HS), F32),
        ),
        grid_spec=pltpu.PrefetchScalarGridSpec(
            num_scalar_prefetch=1,
            grid=(number,),
            in_specs=[block] * 3 + [ANY],
            out_specs=(
                pl.BlockSpec((1, BSZ, width), lambda i, pre: (i, 0, 0)),
                pl.BlockSpec((1, BSZ, HS), lambda i, pre: (i, 0, 0)),
            ),
            scratch_shapes=[pltpu.VMEM((BSZ, HS), BF)]
            + [pltpu.VMEM((BSZ, BSZ), F32)] * 2 + [pltpu.VMEM((BSZ, BSZ), BF)] * 2,
        ),
        compiler_params=pltpu.CompilerParams(vmem_limit_bytes=VLIM),
        cost_estimate=pl.CostEstimate(
            flops=number * 8 * BSZ * BSZ * width, bytes_accessed=number * BSZ * width * 10, transcendentals=0
        ),
        name="own",
    )(jnp.concatenate([counts, first]), q, k, v, after)


def attend_kernel(steps, caps, pre, table, share, sel, q_ref, k_ref, v_ref, sib_ref, *refs):
    got, refs = (refs[:4], refs[4:8]), refs[8:]
    groups = sorted({g for g, _ in steps})
    crossed, refs = dict(zip(groups, refs)), refs[len(groups) :]
    owns, refs = [refs[2 * i : 2 * i + 2] for i in range(len(steps))], refs[2 * len(steps) :]
    outs, refs = refs[: len(steps)], refs[len(steps) :]
    kb, vb, bias, qb, accb, statb, ob, s0, s1, w0, w1, sem, fixed = refs
    width = q_ref.shape[2]
    me = pre[0]
    place = Place(me, table, share, caps)
    source = Source(place, k_ref, v_ref, sib_ref, got)
    plane = 1 - place.p

    def live(t):
        return [lax.shift_right_logical(pre[4 * t + 3 + i] + (R - 1), R.bit_length() - 1) for i in range(2)]

    def operands(t):
        acc, stat = owns[t]
        return [
            pltpu.make_async_copy(q_ref.at[pre[4 * t + 1]], qb.at[t], fixed.at[t]),
            pltpu.make_async_copy(acc.at[steps[t][0]], accb.at[t], fixed.at[t]),
            pltpu.make_async_copy(stat.at[steps[t][0]], statb.at[t], fixed.at[t]),
        ]

    for t in range(len(steps)):
        for copy in operands(t):
            copy.start()

    def gather(t, carry):
        block, group = pre[4 * t + 1], pre[4 * t + 2]
        n0, n1 = live(t)
        chunks = n0 + n1

        def pair(i, start):
            s = sel[(me * NB + block) * 2 + i] >> 3
            e = place.entry(s, me)
            loc = (e >> 3) & 7

            def put(c, *src):
                row = start + 2 * c + ((place.p - loc) & 1)
                src_k, src_v = src if len(src) == 2 else (src[0].at[0], src[0].at[1])
                pltpu.make_async_copy(src_k, kb.at[t, row], sem.at[t]).start()
                pltpu.make_async_copy(src_v, vb.at[t, row], sem.at[t]).start()

            source.pair(s, e, put)
            other = table[plane * NSEQ + s, me]
            base = (other >> 18) & 63
            for g, x_ref in crossed.items():

                def cross(c, carry):
                    row = start + 2 * c + ((plane - loc) & 1)
                    pltpu.make_async_copy(x_ref.at[base + c, 0], kb.at[t, row], sem.at[t]).start()
                    pltpu.make_async_copy(x_ref.at[base + c, 1], vb.at[t, row], sem.at[t]).start()
                    return carry

                lax.fori_loop(0, jnp.where(group == g, other & 7, 0), cross, 0)
            return n0

        lax.fori_loop(0, 2, pair, 0)

        key = iota((2 * BSZ, HS), 0)
        begin = n0 * R
        dead = jnp.logical_and(
            key >= pre[4 * t + 3], jnp.logical_or(key < begin, key >= begin + pre[4 * t + 4])
        )
        bias[t] = bias_of(dead)

        for extra in range(3):

            @pl.when(chunks + extra < 2 * CH)
            def _():
                kb[t, chunks + extra] = jnp.zeros((R, width), BF)
                vb[t, chunks + extra] = jnp.zeros((R, width), BF)

        return carry

    lax.fori_loop(0, len(steps), gather, 0)

    def work(tiles, t):
        keys = tiles * HS
        column = lambda i: jnp.sum(jnp.where(iota((BSZ, HS), 1) == i, statb[t], 0.0), axis=1, keepdims=True)
        part = lambda h: slice(h * HS, (h + 1) * HS)
        own_m = {}

        def top_of(h):
            own_m[h] = column(h)
            return own_m[h]

        def finish(h, m, a):
            factor = jnp.exp((own_m[h] - m) * SCALE)
            numer = a[:, :HS] + factor * accb[t, :, part(h)]
            ob[t, :, part(h)] = (numer / (a[:, HS:] + factor * column(h + 4))).astype(BF)

        heads_pipeline(
            keys, width // HS,
            lambda h: qb[t, :, part(h)],
            lambda h: kb[t, : tiles * 2, :, part(h)].reshape(keys, HS),
            lambda h: vb[t, : tiles * 2, :, part(h)].reshape(keys, HS),
            bias.at[t], top_of, finish, (s0, s1), (w0, w1),
        )

    def compute(t, carry):
        n0, n1 = live(t)
        chunks = n0 + n1
        drain(2 * chunks, kb.at[0, 0], sem.at[t])
        for like in (qb, accb, statb):
            pltpu.make_async_copy(like.at[0], like.at[0], fixed.at[t]).wait()
        least = 0
        for tiles in SIZES:
            pl.when(jnp.logical_and(chunks > least, chunks <= 2 * tiles))(functools.partial(work, tiles, t))
            least = 2 * tiles
        return carry

    lax.fori_loop(0, len(steps), compute, 0)
    for t in range(len(steps)):
        outs[t][...] = ob[t]


def attend(caps, steps, pre, table, share, sel, q, own, kc, vc, sib, got, crossed):
    width = q.shape[-1]
    n = len(steps)
    ins = [q, kc, vc, sib] + got + [crossed[g] for g in sorted({g for g, _ in steps})]
    for _, r in steps:
        ins += own[r]
    out = pl.BlockSpec((BSZ, width), lambda i, pre: (0, 0))
    return pl.pallas_call(
        functools.partial(attend_kernel, steps, caps),
        out_shape=[jax.ShapeDtypeStruct((BSZ, width), BF)] * n,
        grid_spec=pltpu.PrefetchScalarGridSpec(
            num_scalar_prefetch=1,
            grid=(1,),
            in_specs=[SMEM] * 3 + [ANY] * len(ins),
            out_specs=[out] * n,
            scratch_shapes=[
                pltpu.VMEM((n, 2 * CH, R, width), BF),
                pltpu.VMEM((n, 2 * CH, R, width), BF),
                pltpu.VMEM((n, 2 * BSZ, HS), BF),
                pltpu.VMEM((n, BSZ, width), BF),
                pltpu.VMEM((n, BSZ, width), F32),
                pltpu.VMEM((n, BSZ, HS), F32),
                pltpu.VMEM((n, BSZ, width), BF),
                pltpu.VMEM((BSZ, 2 * BSZ), F32),
                pltpu.VMEM((BSZ, 2 * BSZ), F32),
                pltpu.VMEM((BSZ, 2 * BSZ), BF),
                pltpu.VMEM((BSZ, 2 * BSZ), BF),
                pltpu.SemaphoreType.DMA((n,)),
                pltpu.SemaphoreType.DMA((n,)),
            ],
        ),
        compiler_params=pltpu.CompilerParams(vmem_limit_bytes=VLIM),
        cost_estimate=pl.CostEstimate(
            flops=n * 8 * BSZ * BSZ * width, bytes_accessed=n * 8 * BSZ * width * 2, transcendentals=0
        ),
        name="attend",
    )(pre, table, share, sel, *ins)


def project_kernel(pre, *refs):
    parts, (w_ref, o_ref, rows) = refs[:-3], refs[-3:]
    width = parts[0].shape[1]

    @pl.when(pl.program_id(0) == 0)
    def _():
        for index, part in enumerate(parts):
            g, r = index >> 2, index & 3
            head = (pre[0] - r) & 3
            rows[g * BSZ : (g + 1) * BSZ, pl.ds(pl.multiple_of(head * width, width), width)] = part[...]

    o_ref[...] = jnp.dot(rows[...], w_ref[...], preferred_element_type=F32).astype(BF)


def project(head, parts, w_out):
    cols = w_out.shape[1]
    tile = 512
    whole = lambda a: pl.BlockSpec(a.shape, lambda n, pre: (0, 0))
    return pl.pallas_call(
        project_kernel,
        out_shape=jax.ShapeDtypeStruct((2 * BSZ, cols), BF),
        grid_spec=pltpu.PrefetchScalarGridSpec(
            num_scalar_prefetch=1,
            grid=(cols // tile,),
            in_specs=[whole(a) for a in parts] + [pl.BlockSpec((w_out.shape[0], tile), lambda n, pre: (0, n))],
            out_specs=pl.BlockSpec((2 * BSZ, tile), lambda n, pre: (0, n)),
            scratch_shapes=[pltpu.VMEM((2 * BSZ, w_out.shape[0]), BF)],
        ),
        compiler_params=pltpu.CompilerParams(vmem_limit_bytes=VLIM),
        cost_estimate=pl.CostEstimate(
            flops=4 * BSZ * cols * cols, bytes_accessed=2 * cols * cols + 8 * BSZ * cols, transcendentals=0
        ),
        name="project",
    )(head, *parts, w_out)


def ring(stage, step):
    pairs = []
    for x in range(4):
        for z in range(4):
            for c in range(2):
                along_z = (c == 0) == (stage == 0)
                to = (x, (z + step) % 4) if along_z else ((x + step) % 4, z)
                pairs.append(((x * 4 + z) * 2 + c, (to[0] * 4 + to[1]) * 2 + c))
    return pairs


def copies(kernel, outs, ins, specs, hold, name, aliases=None, moved=8 * 2**20):
    return pl.pallas_call(
        kernel,
        out_shape=outs,
        in_specs=specs,
        out_specs=[ANY] * len(outs),
        scratch_shapes=[pltpu.VMEM(a.shape, a.dtype) for a in hold] + [pltpu.SemaphoreType.DMA] * 2,
        input_output_aliases=aliases or {},
        compiler_params=pltpu.CompilerParams(vmem_limit_bytes=VLIM),
        cost_estimate=pl.CostEstimate(flops=0, bytes_accessed=moved, transcendentals=0),
        name=name,
    )(*ins)


def fetch(caps, me, table, share, sel, kc, vc, sib, beside):
    width = kc.shape[-1]
    got, done, after = [], [], []
    for stage in range(2):
        sends = [jax.ShapeDtypeStruct((caps[stage], 2, R, width), BF)] * 2
        ins = [me, table, share, kc, vc, sib] + got + after
        s1p, s1m = copies(
            functools.partial(pack_kernel, stage, 0, caps), sends, ins,
            [SMEM] * 3 + [ANY] * (len(ins) - 3), sends, "pack%d" % stage,
        )
        g1p = lax.ppermute(s1p, "seq", ring(stage, 1))
        g1m = lax.ppermute(s1m, "seq", ring(stage, -1))
        done.append(beside(2 * stage, s1p))
        ins = [me, table, share, kc, vc, sib] + got + [done[-1][0]]
        s2p, s2m = copies(
            functools.partial(pack_kernel, stage, 1, caps), sends, ins,
            [SMEM] * 3 + [ANY] * (len(ins) - 3), sends, "rest%d" % stage,
        )
        s2p, s2m = copies(
            functools.partial(pass_kernel, stage, caps), sends,
            [me, table, share, g1p, g1m, s2p, s2m, done[-1][0]],
            [SMEM] * 3 + [ANY] * 5, sends, "pass%d" % stage, {5: 0, 6: 1},
        )
        g2p = lax.ppermute(s2p, "seq", ring(stage, 1))
        g2m = lax.ppermute(s2m, "seq", ring(stage, -1))
        done.append(beside(2 * stage + 1, s2p))
        got += [g1p, g1m, g2p, g2m]
        after = [done[-1][0]]
    x_shapes = [jax.ShapeDtypeStruct((NB * HALF, 2, R, width), BF)] * 2
    ins = [me, table, share, sel, kc, vc, sib] + got + after
    crossed = copies(
        functools.partial(cross_kernel, caps), x_shapes, ins, [SMEM] * 4 + [ANY] * (len(ins) - 4), x_shapes, "cross",
    )
    swap = [(i, i ^ 1) for i in range(NSEQ)]
    return got, [lax.ppermute(x, "seq", swap) for x in crossed], done


def before_fetch(keys, values, key_count, selected):
    width = keys.shape[1]
    me = lax.axis_index("seq").astype(I32).reshape(1)
    kc = keys.reshape(NB * CH, R, width)
    vc = values.reshape(NB * CH, R, width)
    sent = pl.pallas_call(
        split_kernel,
        out_shape=jax.ShapeDtypeStruct((NB * HALF, 2, R, width), BF),
        in_specs=[SMEM, ANY, ANY],
        out_specs=VMEM,
        scratch_shapes=[pltpu.SemaphoreType.DMA],
        compiler_params=pltpu.CompilerParams(vmem_limit_bytes=VLIM),
        cost_estimate=pl.CostEstimate(flops=0, bytes_accessed=8 * 2**20, transcendentals=0),
        name="split",
    )(me, kc, vc)
    sib = lax.ppermute(sent, "seq", [(i, i ^ 1) for i in range(NSEQ)])
    return (me, kc, vc, sib) + plan(selected, key_count)


def on_device(queries, keys, values, key_count, selected, w_out):
    width = queries.shape[1]
    me, kc, vc, sib, table, share, level = before_fetch(keys, values, key_count, selected)
    sel = selected.reshape(-1)
    head = lax.axis_index("head").astype(I32).reshape(1)
    q, k, v = [a.reshape(NB, BSZ, width) for a in (queries, keys, values)]
    own_counts = lax.dynamic_slice_in_dim(key_count, me[0] * NB, NB)
    far_counts = key_count[lax.dynamic_slice_in_dim(selected, me[0] * NB, NB)]
    calls = (((0, 2), (0, 3)), ((0, 1), (1, 2)), ((1, 1), (1, 3)), ((0, 0), (1, 0)))
    pre = []
    for steps in calls:
        row = [me]
        for g, r in steps:
            block = ((head + r) & 3) * 2 + g
            row += [block, jnp.full((1,), g, I32), far_counts[block[0]]]
        pre.append(jnp.concatenate(row))
    up = [(i, (i + 1) % 4) for i in range(4)]
    down = [(i, (i - 1) % 4) for i in range(4)]

    def rest(caps, sib, table, share, pre, own_counts):
        def beside(r, after):
            return own_blocks(((head + r) & 3) * 2, 2, own_counts, q, k, v, after)

        got, crossed, own = fetch(caps, me, table, share, sel, kc, vc, sib, beside)
        parts = {}
        for row, steps in zip(pre, calls):
            made = attend(caps, steps, row, table, share, sel, q, own, kc, vc, sib, got, crossed)
            for (g, r), part in zip(steps, made):
                way = {0: None, 1: up, 2: up if g == 0 else down, 3: down}[r]
                for _ in range((0, 1, 2, 1)[r]):
                    part = lax.ppermute(part, "head", way)
                parts[g, r] = part
        return project(head, [parts[g, r] for g in range(2) for r in range(4)], w_out)

    return lax.switch(
        level, [functools.partial(rest, caps) for caps in LEVELS], sib, table, share, pre, own_counts
    )


def solution(mesh):
    placed = (P("seq", "head"), P("seq", "head"), P("seq", "head"), P(), P(), P())
    return jax.shard_map(
        on_device, mesh=mesh, in_specs=placed, out_specs=P(("seq", "head"), None), check_vma=False
    )
```

```python
import functools
import math

import jax
import jax.numpy as jnp
from jax import lax
from jax.experimental import pallas as pl
from jax.experimental.pallas import tpu as pltpu
from jax.sharding import PartitionSpec as P

HS = 128
BSZ = 512
R = 64
CH = BSZ // R
HALF = CH // 2
NB = 8
NSEQ = 32
LEVELS = ((21, 24), (22, 25), (23, 27), (26, 30), (64, 64))
VLIM = 60 * 2**20
ROW = 128
F32 = jnp.float32
I32 = jnp.int32
BF = jnp.bfloat16
ANY = pl.BlockSpec(memory_space=pl.ANY)
SMEM = pl.BlockSpec(memory_space=pltpu.SMEM)
VMEM = pl.BlockSpec(memory_space=pltpu.VMEM)


def mm(a, b):
    return jnp.dot(a.astype(BF), b.astype(BF), preferred_element_type=F32)


def uv_of(index, plane):
    x = lax.shift_right_logical(index, 3) & 3
    z = lax.shift_right_logical(index, 1) & 3
    return (z, x) if plane == 0 else (x, z)


def iota(shape, dim):
    return lax.broadcasted_iota(I32, shape, dim)


def plan_kernel(sel_ref, cnt_ref, table_ref):
    s = iota((NSEQ, ROW), 0)
    d = iota((NSEQ, ROW), 1)
    loc = jnp.full((NSEQ, ROW), -1, I32)
    grp = jnp.zeros((NSEQ, ROW), I32)
    for n in range(2 * NB):
        row = sel_ref[n : n + 1, :]
        hit = lax.shift_right_arithmetic(row, 3) == s
        loc = jnp.where(hit, row & 7, loc)
        grp = jnp.where(hit, (n >> 1) & 1, grp)
    count = jnp.zeros((NSEQ, ROW), I32)
    for j in range(NB):
        count = jnp.where(loc == j, cnt_ref[:, j : j + 1], count)
    total = lax.shift_right_logical(count + (R - 1), R.bit_length() - 1)

    i32, j32 = iota((NSEQ, NSEQ), 0), iota((NSEQ, NSEQ), 1)
    i128, j128 = iota((ROW, ROW), 0), iota((ROW, ROW), 1)
    chip_l = ((i32 >> 1) == (j32 >> 1)).astype(F32)
    chip_r = ((i128 >> 1) == (j128 >> 1)).astype(F32)
    odd_l = jnp.logical_and(j32 == i32 - 1, (i32 & 1) == 1).astype(F32)
    odd_r = jnp.logical_and(i128 == j128 - 1, (j128 & 1) == 1).astype(F32)
    lower = (j32 < i32).astype(F32)
    for plane in range(2):
        first = (plane - loc) & 1
        n_of = jnp.where(loc >= 0, lax.shift_right_logical(total - first + 1, 1), 0)
        n_f = n_of.astype(F32)
        u_i, v_i = uv_of(i128, plane)
        u_j, v_j = uv_of(j128, plane)
        same_u = u_i == u_j
        m1 = jnp.logical_and(same_u, (v_i * 2 + (i128 & 1)) < (v_j * 2 + (j128 & 1))).astype(F32)
        same_u = same_u.astype(F32)
        dup = jnp.zeros((NSEQ, ROW), jnp.bool_)
        for j in range(NB):
            is_j = loc == j
            dup = jnp.logical_or(dup, jnp.logical_and(is_j, mm(is_j.astype(F32), m1) > 0.5))
        n1 = jnp.where(dup, 0.0, n_f)
        a_n = mm(chip_l, n1)
        pos1 = mm(a_n, m1) + mm(odd_l, n1)
        of_first = jnp.zeros((NSEQ, ROW), F32)
        for j in range(NB):
            is_j = loc == j
            there = mm(jnp.where(jnp.logical_and(is_j, jnp.logical_not(dup)), pos1, 0.0), same_u)
            of_first = jnp.where(is_j, there, of_first)
        pos1 = jnp.where(dup, of_first, pos1)
        u_s, v_s = uv_of(i32, plane)
        u_t, v_t = uv_of(j32, plane)
        same_v = v_s == v_t
        m2 = jnp.logical_and(same_v, (u_t * 2 + (j32 & 1)) < (u_s * 2 + (i32 & 1))).astype(F32)
        pos2 = mm(m2, mm(n_f, chip_r)) + mm(n_f, odd_r)
        pos3 = jnp.where(
            grp == 0,
            mm(lower, jnp.where(grp == 0, n_f, 0.0)),
            mm(lower, jnp.where(grp == 1, n_f, 0.0)),
        )
        entry = n_of | (jnp.maximum(loc, 0) << 3)
        for index, place in enumerate((pos1, pos2, pos3)):
            entry = entry | (place.astype(I32) << (6 + 6 * index))
        entry = entry | (dup.astype(I32) << 24)

        to_u = jnp.logical_and(i128 < NSEQ, j128 - NSEQ == u_i).astype(F32)
        to_v = jnp.logical_and(i128 < NSEQ, j128 - NSEQ - 4 == v_i).astype(F32)
        u_a, _ = uv_of(s, plane)
        u_b, _ = uv_of(d, plane)
        line = jnp.where(u_a == u_b, mm(same_v.astype(F32), n_f), 0.0)
        lengths = mm(a_n, to_u) + mm(line, to_v)
        table_ref[plane * NSEQ : (plane + 1) * NSEQ, :] = jnp.where(d < NSEQ, entry, lengths.astype(I32))


def balance_kernel(table, share_ref, level_ref):
    def one(ring_number, need):
        plane, stage, g = ring_number >> 3, (ring_number >> 2) & 1, ring_number & 3
        by_x = plane == stage
        rows = [
            plane * NSEQ + jnp.where(by_x, g * 4 + a, a * 4 + g) * 2 for a in range(4)
        ]
        far = NSEQ + stage * 4
        l1, l2, l3 = [[table[rows[a], far + ((a + r) & 3)] for a in range(4)] for r in (1, 2, 3)]
        h = [(n + 1) >> 1 for n in l2]

        def loads():
            plus = [l1[a] + h[a] + h[(a - 1) & 3] for a in range(4)]
            minus = [l3[a] + l2[a] - h[a] + l2[(a + 1) & 3] - h[(a + 1) & 3] for a in range(4)]
            return plus, minus

        for a in range(4):
            plus, minus = loads()
            high = jnp.maximum(plus[a], plus[(a + 1) & 3]) - h[a]
            low = jnp.maximum(minus[a], minus[(a - 1) & 3]) - (l2[a] - h[a])
            h[a] = jnp.clip((low + l2[a] - high + 1) >> 1, 0, l2[a])
        plus, minus = loads()
        most = functools.reduce(jnp.maximum, plus + minus)
        least = functools.reduce(jnp.maximum, h + [l2[a] - h[a] for a in range(4)])
        for a in range(4):
            share_ref[ring_number * 4 + a] = h[a]
        here = jnp.maximum((most + 1) >> 1, least)
        return (
            jnp.where(stage == 0, jnp.maximum(need[0], here), need[0]),
            jnp.where(stage == 1, jnp.maximum(need[1], here), need[1]),
        )

    need = lax.fori_loop(0, 16, one, (jnp.int32(0), jnp.int32(0)))
    level = jnp.int32(0)
    for cap in LEVELS[:-1]:
        level += jnp.logical_or(need[0] > cap[0], need[1] > cap[1]).astype(I32)
    level_ref[0] = level


def plan(selected, key_count):
    by_dest = jnp.pad(
        selected.reshape(NSEQ, 2 * NB).T, ((0, 0), (0, ROW - NSEQ)), constant_values=-1
    )
    table = pl.pallas_call(
        plan_kernel,
        out_shape=jax.ShapeDtypeStruct((2 * NSEQ, ROW), I32),
        in_specs=[VMEM, VMEM],
        out_specs=VMEM,
        compiler_params=pltpu.CompilerParams(vmem_limit_bytes=VLIM),
        name="plan",
    )(by_dest, key_count.reshape(NSEQ, NB))
    share, level = pl.pallas_call(
        balance_kernel,
        out_shape=(jax.ShapeDtypeStruct((64,), I32), jax.ShapeDtypeStruct((1,), I32)),
        in_specs=[SMEM],
        out_specs=(SMEM, SMEM),
        compiler_params=pltpu.CompilerParams(vmem_limit_bytes=VLIM),
        name="balance",
    )(table)
    return table, share, level[0]


def both_start(src_k, src_v, dst, sem):
    pltpu.make_async_copy(src_k, dst.at[0], sem).start()
    pltpu.make_async_copy(src_v, dst.at[1], sem).start()


def drain(count, like, sem):
    def one(_, carry):
        pltpu.make_async_copy(like, like, sem).wait()
        return carry

    lax.fori_loop(0, count, one, 0)


def spill(low, high, src, dst, sem):
    def one(row, carry):
        pltpu.make_async_copy(src.at[row], dst.at[row], sem).start()
        return carry

    lax.fori_loop(low, high, one, 0)
    return jnp.maximum(high - low, 0)


def split_kernel(me_ref, k_ref, v_ref, out_ref, sem):
    other = 1 - (me_ref[0] & 1)

    def one(index, carry):
        block = index // HALF
        chunk = block * CH + 2 * (index % HALF) + ((other - block) & 1)
        both_start(k_ref.at[chunk], v_ref.at[chunk], out_ref.at[index], sem)
        return carry

    lax.fori_loop(0, NB * HALF, one, 0)
    pltpu.make_async_copy(out_ref, out_ref, sem).wait()


class Place:
    def __init__(self, me, table, share, caps):
        self.me, self.table, self.share, self.caps = me, table, share, caps
        self.p = me & 1
        x, z = (me >> 3) & 3, (me >> 1) & 3
        self.u0 = jnp.where(self.p == 0, z, x)
        self.v0 = jnp.where(self.p == 0, x, z)

    def index(self, u, v, c):
        x = jnp.where(self.p == 0, v, u)
        z = jnp.where(self.p == 0, u, v)
        return (x * 4 + z) * 2 + c

    def entry(self, s, d):
        return self.table[self.p * NSEQ + s, d]

    def length(self, stage, a, b):
        a, b = a & 3, b & 3
        node = self.index(a, self.v0, 0) if stage == 0 else self.index(self.u0, a, 0)
        return self.table[self.p * NSEQ + node, NSEQ + 4 * stage + b]

    def halves(self, stage, a):
        a = a & 3
        ring_of = self.v0 if stage == 0 else self.u0
        h = self.share[((self.p * 2 + stage) * 4 + ring_of) * 4 + a]
        return h, self.length(stage, a, a + 2) - h

    def here(self, stage):
        return self.u0 if stage == 0 else self.v0


def chunk_of(loc, t, plane):
    return loc * CH + 2 * t + ((plane - loc) & 1)


class Source:
    def __init__(self, place, k_ref, v_ref, sib_ref, got):
        self.place, self.k, self.v, self.sib, self.got = place, k_ref, v_ref, sib_ref, got
        self.info = []
        for stage in range(len(got)):
            b = place.here(stage)
            far_p, far_m = place.halves(stage, b + 2)
            near_p, _ = place.halves(stage, b - 1)
            _, near_m = place.halves(stage, b + 1)
            self.info.append((far_p, far_m, near_p, near_m))

    def chunk(self, stage, a, q, t, loc, own, put):
        place = self.place
        if stage < 0:

            @pl.when(own)
            def _():
                c = chunk_of(loc, t, place.p)
                put(self.k.at[c], self.v.at[c])

            @pl.when(jnp.logical_not(own))
            def _():
                put(self.sib.at[loc * HALF + t])

            return
        g1p, g1m, g2p, g2m = self.got[stage]
        far_p, far_m, near_p, near_m = self.info[stage]
        cap = place.caps[stage]
        r = (place.here(stage) - a) & 3
        plus = jnp.logical_or(r == 1, jnp.logical_and(r == 2, q < far_p))
        near = jnp.where(r == 1, near_p, near_m)
        far = jnp.where(r == 1, far_p, far_m)
        first = jnp.logical_and(r != 2, q < cap - near)
        row = jnp.where(
            r == 2,
            jnp.where(plus, q, q - far_p),
            jnp.where(first, near + q, far + q - (cap - near)),
        )
        for is_plus, is_first, ref in (
            (True, True, g1p), (False, True, g1m), (True, False, g2p), (False, False, g2m),
        ):
            cond = jnp.logical_and(plus == is_plus, first == is_first)

            @pl.when(cond)
            def _(ref=ref):
                put(ref.at[row])

    def pair(self, s, e, put):
        place = self.place
        n, loc = e & 7, (e >> 3) & 7
        c = s & 1
        x, z = (s >> 3) & 3, (s >> 1) & 3
        u = jnp.where(place.p == 0, z, x)
        v = jnp.where(place.p == 0, x, z)
        own = c == place.p
        mine = u == place.u0
        last = len(self.got) - 1

        def loop(stage, a, base):
            def one(t, carry):
                self.chunk(stage, a, base + t, t, loc, own, functools.partial(put, t))
                return carry

            lax.fori_loop(0, n, one, 0)

        def early():
            if last < 0:
                loop(-1, 0, 0)
                return

            @pl.when(mine)
            def _():
                loop(-1, 0, 0)

            @pl.when(jnp.logical_not(mine))
            def _():
                loop(0, u, (e >> 6) & 63)

        if last < 1:
            early()
        else:
            same_v = v == place.v0

            @pl.when(same_v)
            def _():
                early()

            @pl.when(jnp.logical_not(same_v))
            def _():
                loop(1, v, (e >> 12) & 63)
        return n


def copier(dst, sem):
    def put(*src):
        if len(src) == 2:
            both_start(src[0], src[1], dst, sem)
        else:
            pltpu.make_async_copy(src[0], dst, sem).start()

    return put


def pack_kernel(stage, part, caps, me_ref, table, share, k_ref, v_ref, sib_ref, *refs):
    got = (refs[:4],) if stage else ()
    out_p, out_m, hold_p, hold_m, sem, sem_out = refs[len(refs) - 6 :]
    place = Place(me_ref[0], table, share, caps)
    source = Source(place, k_ref, v_ref, sib_ref, got)
    b = place.here(stage)
    cap = caps[stage]
    half_p, half_m = place.halves(stage, b)
    pass_p, _ = place.halves(stage, b - 1)
    _, pass_m = place.halves(stage, b + 1)
    shift = 6 if stage == 0 else 12
    started = 0
    for r in (2, 1, 3) if part == 0 else (1, 3):
        to = (b + r) & 3

        def one(i, count, r=r, to=to):
            if stage == 0:
                s = place.index(place.u0, place.v0, i & 1)
                d = place.index(to, i >> 2, (i >> 1) & 1)
            else:
                s = place.index(i >> 2, place.v0, (i >> 1) & 1)
                d = place.index(place.u0, to, i & 1)
            e = place.entry(s, d)
            base = (e >> shift) & 63
            if stage == 0:
                e = jnp.where((e >> 24) & 1 == 1, 0, e)

            if r == 2:
                rows = ((hold_p, 0, half_p, 0), (hold_m, half_p, 1 << 20, -half_p))
            else:
                hold, half, passed = (hold_p, half_p, pass_p) if r == 1 else (hold_m, half_m, pass_m)
                fits = cap - half
                rows = ((hold, 0, fits, half),) if part == 0 else ((hold, fits, 1 << 20, passed - fits),)

            def put(t, *src):
                q = base + t
                for hold, low, high, move in rows:

                    @pl.when(jnp.logical_and(q >= low, q < high))
                    def _(hold=hold, move=move):
                        copier(hold.at[q + move], sem)(*src)

            source.pair(s, e, put)
            n = e & 7
            return count + sum(
                jnp.maximum(jnp.minimum(base + n, high) - jnp.maximum(base, low), 0) for _, low, high, _ in rows
            )

        started = lax.fori_loop(0, 16, one, started)
    drain(started, hold_p.at[0], sem)
    started = 0
    for half, passed, n, hold, out in (
        (half_p, pass_p, place.length(stage, b, b + 1), hold_p, out_p),
        (half_m, pass_m, place.length(stage, b, b - 1), hold_m, out_m),
    ):
        fits = jnp.minimum(n, cap - half)
        if part == 0:
            started += spill(0, half + fits, hold, out, sem_out)
        else:
            started += spill(passed, passed + n - fits, hold, out, sem_out)
    drain(started, hold_p.at[0], sem_out)


def pass_kernel(stage, caps, me_ref, table, share, g1p, g1m, in_p, in_m, after, s2p, s2m, hold_p, hold_m, sem, sem_out):
    place = Place(me_ref[0], table, share, caps)
    b = place.here(stage)
    pass_p, _ = place.halves(stage, b - 1)
    _, pass_m = place.halves(stage, b + 1)
    started = spill(0, pass_p, g1p, hold_p, sem) + spill(0, pass_m, g1m, hold_m, sem)
    drain(started, hold_p.at[0], sem)
    started = spill(0, pass_p, hold_p, s2p, sem_out) + spill(0, pass_m, hold_m, s2m, sem_out)
    drain(started, hold_p.at[0], sem_out)


def cross_kernel(caps, me_ref, table, share, sel, k_ref, v_ref, sib_ref, *refs):
    got = (refs[:4], refs[4:8])
    out0, out1, x0, x1, sem, sem_out = refs[-6:]
    place = Place(me_ref[0], table, share, caps)
    source = Source(place, k_ref, v_ref, sib_ref, got)
    dest = place.me ^ 1

    def one(n, counts):
        s = sel[dest * 2 * NB + n] >> 3
        e = place.entry(s, dest)
        base = (e >> 18) & 63
        group = (n >> 1) & 1

        def put(t, *src):
            @pl.when(group == 0)
            def _():
                copier(x0.at[base + t], sem)(*src)

            @pl.when(group == 1)
            def _():
                copier(x1.at[base + t], sem)(*src)

        here = source.pair(s, e, put)
        return counts[0] + jnp.where(group == 0, here, 0), counts[1] + jnp.where(group == 1, here, 0)

    count0, count1 = lax.fori_loop(0, 2 * NB, one, (0, 0))
    drain(count0 + count1, x0.at[0], sem)
    started = spill(0, count0, x0, out0, sem_out) + spill(0, count1, x1, out1, sem_out)
    drain(started, x0.at[0], sem_out)


SIZES = (2, 4, 6, 8)
SCALE = 1.0 / math.sqrt(HS)


def heads_pipeline(keys, heads, q_of, k_of, v_of, bias, top_of, finish, scores, weights):
    tops = {}
    for i in range(heads + 2):
        if i < heads:
            q = q_of(i)
            hot = (iota(q.shape, 1) == 0).astype(F32).astype(BF)
            s = lax.dot_general(
                jnp.concatenate([q, hot], axis=1), jnp.concatenate([k_of(i), bias[:keys]], axis=1),
                (((1,), (1,)), ((), ())), preferred_element_type=F32,
            )
            scores[i % 2][:, :keys] = s
            tops[i] = jnp.max(s, axis=1, keepdims=True)
            top = top_of(i)
            if top is not None:
                tops[i] = jnp.maximum(tops[i], top)
        if 0 <= i - 1 < heads:
            h = i - 1
            w = jnp.exp(scores[h % 2][:, :keys] * SCALE - tops[h] * SCALE)
            weights[h % 2][:, :keys] = w.astype(BF)
        if i - 2 >= 0:
            h = i - 2
            v = v_of(h)
            a = jnp.dot(
                weights[h % 2][:, :keys], jnp.concatenate([v, jnp.ones(v.shape, BF)], axis=1),
                preferred_element_type=F32,
            )
            finish(h, tops.pop(h), a)


def bias_of(dead):
    return jnp.where(jnp.logical_and(dead, iota(dead.shape, 1) == 0), -1e30, 0.0).astype(BF)


def own_kernel(pre, q_ref, k_ref, v_ref, after, acc_ref, stat_ref, bias, s0, s1, w0, w1):
    count = pre[pl.program_id(0) + pre[NB]]
    bias[...] = bias_of(iota((BSZ, HS), 0) >= count)
    lane = iota((BSZ, HS), 1)

    def work(keys):
        def finish(h, m, a):
            acc_ref[0, :, h * HS : (h + 1) * HS] = a[:, :HS]
            before = stat_ref[0] if h else jnp.zeros((BSZ, HS), F32)
            stat_ref[0] = jnp.where(lane == h, m, jnp.where(lane == h + 4, a[:, HS:], before))

        cols = lambda ref, rows: lambda h: ref[0, :rows, h * HS : (h + 1) * HS]
        heads_pipeline(
            keys, q_ref.shape[2] // HS, cols(q_ref, BSZ), cols(k_ref, keys), cols(v_ref, keys), bias,
            lambda h: None, finish, (s0, s1), (w0, w1),
        )

    pl.when(count <= BSZ // 2)(functools.partial(work, BSZ // 2))
    pl.when(count > BSZ // 2)(functools.partial(work, BSZ))


def own_blocks(first, number, counts, q, k, v, after):
    width = q.shape[-1]
    block = pl.BlockSpec((1, BSZ, width), lambda i, pre: (pre[NB] + i, 0, 0))
    return pl.pallas_call(
        own_kernel,
        out_shape=(
            jax.ShapeDtypeStruct((number, BSZ, width), F32),
            jax.ShapeDtypeStruct((number, BSZ, HS), F32),
        ),
        grid_spec=pltpu.PrefetchScalarGridSpec(
            num_scalar_prefetch=1,
            grid=(number,),
            in_specs=[block] * 3 + [ANY],
            out_specs=(
                pl.BlockSpec((1, BSZ, width), lambda i, pre: (i, 0, 0)),
                pl.BlockSpec((1, BSZ, HS), lambda i, pre: (i, 0, 0)),
            ),
            scratch_shapes=[pltpu.VMEM((BSZ, HS), BF)]
            + [pltpu.VMEM((BSZ, BSZ), F32)] * 2 + [pltpu.VMEM((BSZ, BSZ), BF)] * 2,
        ),
        compiler_params=pltpu.CompilerParams(vmem_limit_bytes=VLIM),
        cost_estimate=pl.CostEstimate(
            flops=number * 8 * BSZ * BSZ * width, bytes_accessed=number * BSZ * width * 10, transcendentals=0
        ),
        name="own",
    )(jnp.concatenate([counts, first]), q, k, v, after)


def attend_kernel(steps, caps, pre, table, share, sel, q_ref, k_ref, v_ref, sib_ref, *refs):
    got, refs = (refs[:4], refs[4:8]), refs[8:]
    groups = sorted({g for g, _ in steps})
    crossed, refs = dict(zip(groups, refs)), refs[len(groups) :]
    owns = [refs[2 * i : 2 * i + 2] for i in range(len(steps))]
    outs, refs = refs[-13 - len(steps) : -13], refs[-13:]
    kb, vb, bias, qb, accb, statb, ob, s0, s1, w0, w1, sem, fixed = refs
    width = q_ref.shape[2]
    me = pre[0]
    place = Place(me, table, share, caps)
    source = Source(place, k_ref, v_ref, sib_ref, got)
    plane = 1 - place.p

    def live(t):
        return [lax.shift_right_logical(pre[4 * t + 3 + i] + (R - 1), R.bit_length() - 1) for i in range(2)]

    def operands(t):
        acc, stat = owns[t]
        return [
            pltpu.make_async_copy(q_ref.at[pre[4 * t + 1]], qb.at[t], fixed.at[t]),
            pltpu.make_async_copy(acc.at[steps[t][0]], accb.at[t], fixed.at[t]),
            pltpu.make_async_copy(stat.at[steps[t][0]], statb.at[t], fixed.at[t]),
        ]

    for t in range(len(steps)):
        for copy in operands(t):
            copy.start()

    def gather(t, carry):
        block, group = pre[4 * t + 1], pre[4 * t + 2]
        n0, n1 = live(t)
        chunks = n0 + n1

        def pair(i, start):
            s = sel[(me * NB + block) * 2 + i] >> 3
            e = place.entry(s, me)
            loc = (e >> 3) & 7

            def put(c, *src):
                row = start + 2 * c + ((place.p - loc) & 1)
                src_k, src_v = src if len(src) == 2 else (src[0].at[0], src[0].at[1])
                pltpu.make_async_copy(src_k, kb.at[t, row], sem.at[t]).start()
                pltpu.make_async_copy(src_v, vb.at[t, row], sem.at[t]).start()

            source.pair(s, e, put)
            other = table[plane * NSEQ + s, me]
            base = (other >> 18) & 63
            for g, x_ref in crossed.items():

                def cross(c, carry):
                    row = start + 2 * c + ((plane - loc) & 1)
                    pltpu.make_async_copy(x_ref.at[base + c, 0], kb.at[t, row], sem.at[t]).start()
                    pltpu.make_async_copy(x_ref.at[base + c, 1], vb.at[t, row], sem.at[t]).start()
                    return carry

                lax.fori_loop(0, jnp.where(group == g, other & 7, 0), cross, 0)
            return n0

        lax.fori_loop(0, 2, pair, 0)

        key = iota((2 * BSZ, HS), 0)
        begin = n0 * R
        dead = jnp.logical_and(
            key >= pre[4 * t + 3], jnp.logical_or(key < begin, key >= begin + pre[4 * t + 4])
        )
        bias[t] = bias_of(dead)

        for extra in range(3):

            @pl.when(chunks + extra < 2 * CH)
            def _():
                kb[t, chunks + extra] = jnp.zeros((R, width), BF)
                vb[t, chunks + extra] = jnp.zeros((R, width), BF)

        return carry

    lax.fori_loop(0, len(steps), gather, 0)

    def work(tiles, t):
        keys = tiles * HS
        column = lambda i: jnp.sum(jnp.where(iota((BSZ, HS), 1) == i, statb[t], 0.0), axis=1, keepdims=True)
        part = lambda h: slice(h * HS, (h + 1) * HS)
        own_m = {}

        def top_of(h):
            own_m[h] = column(h)
            return own_m[h]

        def finish(h, m, a):
            factor = jnp.exp((own_m[h] - m) * SCALE)
            numer = a[:, :HS] + factor * accb[t, :, part(h)]
            ob[t, :, part(h)] = (numer / (a[:, HS:] + factor * column(h + 4))).astype(BF)

        heads_pipeline(
            keys, width // HS,
            lambda h: qb[t, :, part(h)],
            lambda h: kb[t, : tiles * 2, :, part(h)].reshape(keys, HS),
            lambda h: vb[t, : tiles * 2, :, part(h)].reshape(keys, HS),
            bias.at[t], top_of, finish, (s0, s1), (w0, w1),
        )

    def compute(t, carry):
        n0, n1 = live(t)
        chunks = n0 + n1
        drain(2 * chunks, kb.at[0, 0], sem.at[t])
        for like in (qb, accb, statb):
            pltpu.make_async_copy(like.at[0], like.at[0], fixed.at[t]).wait()
        least = 0
        for tiles in SIZES:
            pl.when(jnp.logical_and(chunks > least, chunks <= 2 * tiles))(functools.partial(work, tiles, t))
            least = 2 * tiles
        return carry

    lax.fori_loop(0, len(steps), compute, 0)
    for t in range(len(steps)):
        outs[t][...] = ob[t]


def attend(caps, steps, pre, table, share, sel, q, own, kc, vc, sib, got, crossed, after):
    width = q.shape[-1]
    n = len(steps)
    ins = [q, kc, vc, sib] + got + [crossed[g] for g in sorted({g for g, _ in steps})]
    for _, r in steps:
        ins += own[r]
    ins += after
    out = pl.BlockSpec((BSZ, width), lambda i, pre: (0, 0))
    return pl.pallas_call(
        functools.partial(attend_kernel, steps, caps),
        out_shape=[jax.ShapeDtypeStruct((BSZ, width), BF)] * n,
        grid_spec=pltpu.PrefetchScalarGridSpec(
            num_scalar_prefetch=1,
            grid=(1,),
            in_specs=[SMEM] * 3 + [ANY] * len(ins),
            out_specs=[out] * n,
            scratch_shapes=[
                pltpu.VMEM((n, 2 * CH, R, width), BF),
                pltpu.VMEM((n, 2 * CH, R, width), BF),
                pltpu.VMEM((n, 2 * BSZ, HS), BF),
                pltpu.VMEM((n, BSZ, width), BF),
                pltpu.VMEM((n, BSZ, width), F32),
                pltpu.VMEM((n, BSZ, HS), F32),
                pltpu.VMEM((n, BSZ, width), BF),
                pltpu.VMEM((BSZ, 2 * BSZ), F32),
                pltpu.VMEM((BSZ, 2 * BSZ), F32),
                pltpu.VMEM((BSZ, 2 * BSZ), BF),
                pltpu.VMEM((BSZ, 2 * BSZ), BF),
                pltpu.SemaphoreType.DMA((n,)),
                pltpu.SemaphoreType.DMA((n,)),
            ],
        ),
        compiler_params=pltpu.CompilerParams(vmem_limit_bytes=VLIM),
        cost_estimate=pl.CostEstimate(
            flops=n * 8 * BSZ * BSZ * width, bytes_accessed=n * 8 * BSZ * width * 2, transcendentals=0
        ),
        name="attend",
    )(pre, table, share, sel, *ins)


def project_kernel(pre, *refs):
    parts, (w_ref, o_ref, rows) = refs[:-3], refs[-3:]
    width = parts[0].shape[1]

    @pl.when(pl.program_id(0) == 0)
    def _():
        for index, part in enumerate(parts):
            g, r = index >> 2, index & 3
            head = (pre[0] - r) & 3
            rows[g * BSZ : (g + 1) * BSZ, pl.ds(pl.multiple_of(head * width, width), width)] = part[...]

    o_ref[...] = jnp.dot(rows[...], w_ref[...], preferred_element_type=F32).astype(BF)


def project(head, parts, w_out):
    cols = w_out.shape[1]
    tile = 512
    whole = lambda a: pl.BlockSpec(a.shape, lambda n, pre: (0, 0))
    return pl.pallas_call(
        project_kernel,
        out_shape=jax.ShapeDtypeStruct((2 * BSZ, cols), BF),
        grid_spec=pltpu.PrefetchScalarGridSpec(
            num_scalar_prefetch=1,
            grid=(cols // tile,),
            in_specs=[whole(a) for a in parts] + [pl.BlockSpec((w_out.shape[0], tile), lambda n, pre: (0, n))],
            out_specs=pl.BlockSpec((2 * BSZ, tile), lambda n, pre: (0, n)),
            scratch_shapes=[pltpu.VMEM((2 * BSZ, w_out.shape[0]), BF)],
        ),
        compiler_params=pltpu.CompilerParams(vmem_limit_bytes=VLIM),
        cost_estimate=pl.CostEstimate(
            flops=4 * BSZ * cols * cols, bytes_accessed=2 * cols * cols + 8 * BSZ * cols, transcendentals=0
        ),
        name="project",
    )(head, *parts, w_out)


def ring(stage, step):
    pairs = []
    for x in range(4):
        for z in range(4):
            for c in range(2):
                along_z = (c == 0) == (stage == 0)
                to = (x, (z + step) % 4) if along_z else ((x + step) % 4, z)
                pairs.append(((x * 4 + z) * 2 + c, (to[0] * 4 + to[1]) * 2 + c))
    return pairs


def copies(kernel, outs, ins, specs, hold, name, aliases=None, moved=8 * 2**20):
    return pl.pallas_call(
        kernel,
        out_shape=outs,
        in_specs=specs,
        out_specs=[ANY] * len(outs),
        scratch_shapes=[pltpu.VMEM(a.shape, a.dtype) for a in hold] + [pltpu.SemaphoreType.DMA] * 2,
        input_output_aliases=aliases or {},
        compiler_params=pltpu.CompilerParams(vmem_limit_bytes=VLIM),
        cost_estimate=pl.CostEstimate(flops=0, bytes_accessed=moved, transcendentals=0),
        name=name,
    )(*ins)


def fetch(caps, me, table, share, sel, kc, vc, sib, beside):
    width = kc.shape[-1]
    got, done, after = [], [], []
    for stage in range(2):
        sends = [jax.ShapeDtypeStruct((caps[stage], 2, R, width), BF)] * 2
        ins = [me, table, share, kc, vc, sib] + got + after
        s1p, s1m = copies(
            functools.partial(pack_kernel, stage, 0, caps), sends, ins,
            [SMEM] * 3 + [ANY] * (len(ins) - 3), sends, "pack%d" % stage,
        )
        g1p = lax.ppermute(s1p, "seq", ring(stage, 1))
        g1m = lax.ppermute(s1m, "seq", ring(stage, -1))
        done.append(beside(2 * stage, s1p))
        ins = [me, table, share, kc, vc, sib] + got + [done[-1][0]]
        s2p, s2m = copies(
            functools.partial(pack_kernel, stage, 1, caps), sends, ins,
            [SMEM] * 3 + [ANY] * (len(ins) - 3), sends, "rest%d" % stage,
        )
        s2p, s2m = copies(
            functools.partial(pass_kernel, stage, caps), sends,
            [me, table, share, g1p, g1m, s2p, s2m, done[-1][0]],
            [SMEM] * 3 + [ANY] * 5, sends, "pass%d" % stage, {5: 0, 6: 1},
        )
        g2p = lax.ppermute(s2p, "seq", ring(stage, 1))
        g2m = lax.ppermute(s2m, "seq", ring(stage, -1))
        done.append(beside(2 * stage + 1, s2p))
        got += [g1p, g1m, g2p, g2m]
        after = [done[-1][0]]
    x_shapes = [jax.ShapeDtypeStruct((NB * HALF, 2, R, width), BF)] * 2
    ins = [me, table, share, sel, kc, vc, sib] + got + after
    crossed = copies(
        functools.partial(cross_kernel, caps), x_shapes, ins, [SMEM] * 4 + [ANY] * (len(ins) - 4), x_shapes, "cross",
    )
    swap = [(i, i ^ 1) for i in range(NSEQ)]
    return got, [lax.ppermute(x, "seq", swap) for x in crossed], done


def before_fetch(keys, values, key_count, selected):
    width = keys.shape[1]
    me = lax.axis_index("seq").astype(I32).reshape(1)
    kc = keys.reshape(NB * CH, R, width)
    vc = values.reshape(NB * CH, R, width)
    sent = pl.pallas_call(
        split_kernel,
        out_shape=jax.ShapeDtypeStruct((NB * HALF, 2, R, width), BF),
        in_specs=[SMEM, ANY, ANY],
        out_specs=VMEM,
        scratch_shapes=[pltpu.SemaphoreType.DMA],
        compiler_params=pltpu.CompilerParams(vmem_limit_bytes=VLIM),
        cost_estimate=pl.CostEstimate(flops=0, bytes_accessed=8 * 2**20, transcendentals=0),
        name="split",
    )(me, kc, vc)
    sib = lax.ppermute(sent, "seq", [(i, i ^ 1) for i in range(NSEQ)])
    return (me, kc, vc, sib) + plan(selected, key_count)


def on_device(queries, keys, values, key_count, selected, w_out):
    width = queries.shape[1]
    me, kc, vc, sib, table, share, level = before_fetch(keys, values, key_count, selected)
    sel = selected.reshape(-1)
    head = lax.axis_index("head").astype(I32).reshape(1)
    q, k, v = [a.reshape(NB, BSZ, width) for a in (queries, keys, values)]
    own_counts = lax.dynamic_slice_in_dim(key_count, me[0] * NB, NB)
    far_counts = key_count[lax.dynamic_slice_in_dim(selected, me[0] * NB, NB)]
    calls = (((0, 2), (1, 2)), ((0, 1), (0, 3)), ((1, 1), (1, 3)), ((0, 0), (1, 0)))
    pre = []
    for steps in calls:
        row = [me]
        for g, r in steps:
            block = ((head + r) & 3) * 2 + g
            row += [block, jnp.full((1,), g, I32), far_counts[block[0]]]
        pre.append(jnp.concatenate(row))
    up = [(i, (i + 1) % 4) for i in range(4)]
    down = [(i, (i - 1) % 4) for i in range(4)]

    def rest(caps, sib, table, share, pre, own_counts):
        def beside(r, after):
            return own_blocks(((head + r) & 3) * 2, 2, own_counts, q, k, v, after)

        got, crossed, own = fetch(caps, me, table, share, sel, kc, vc, sib, beside)
        parts, hops = {}, []
        for index, (row, steps) in enumerate(zip(pre, calls)):
            after = hops[0] if index == 2 else hops[1] if index == 3 else []
            made = attend(caps, steps, row, table, share, sel, q, own, kc, vc, sib, got, crossed, after)
            for (g, r), part in zip(steps, made):
                way = {0: None, 1: up, 2: up if g == 0 else down, 3: down}[r]
                if r:
                    part = lax.ppermute(part, "head", way)
                parts[g, r] = part
            if index == 0:
                hops = [[parts[0, 2], parts[1, 2]]]
                parts[0, 2] = lax.ppermute(parts[0, 2], "head", up)
                parts[1, 2] = lax.ppermute(parts[1, 2], "head", down)
                hops.append([parts[0, 2], parts[1, 2]])
        return project(head, [parts[g, r] for g in range(2) for r in range(4)], w_out)

    return lax.switch(
        level, [functools.partial(rest, caps) for caps in LEVELS], sib, table, share, pre, own_counts
    )


def solution(mesh):
    placed = (P("seq", "head"), P("seq", "head"), P("seq", "head"), P(), P(), P())
    return jax.shard_map(
        on_device, mesh=mesh, in_specs=placed, out_specs=P(("seq", "head"), None), check_vma=False
    )
```
